32 devices in a mesh: expert: 8 (over z, x), dp: 4 (over y, core).
Axes of the slice: x: 2, y: 2, z: 4, core: 2. Of those that a mesh axis runs over, the one named last changes fastest.
Arguments:
- tokens: bfloat16 [256, 64, 384], P(('expert', 'dp')), may hold values from -6 to 6
- router: bfloat16 [384, 8], replicated, may hold values from -8.675276 to 8.675276
- w_in: bfloat16 [8, 384, 1536], P('expert'), may hold values from -0.3125 to 0.3125
- w_out: bfloat16 [8, 384, 1536], P('expert'), may hold values from -0.15625 to 0.15625
- out_grad: bfloat16 [256, 64, 384], P(('expert', 'dp')), may hold values from -6 to 6
Outputs:
- tokens_grad: bfloat16 [256, 64, 384], P(('expert', 'dp'))
- w_in_grad: float32 [8, 384, 1536], P('expert', 'dp')
- w_out_grad: float32 [8, 384, 1536], P('expert', 'dp')
- router_grad: float32 [384, 8], P('dp')
The draws below stay inside these ranges and needn't reach their ends.
All inputs are finite; a program needn't handle non-finite values.
Results may differ from the reference program's by a relative error of at most 0.029.
Values may be sent and summed in bfloat16 or wider, within the bound.
No kernel may reach another device: no remote copies, remote signals or barrier semaphores. Data moves between devices by JAX's collectives and lax.ppermute only.
A program may use at most 64 MiB of HBM per device.

```python
import math
import jax
import jax.numpy as jnp
from jax import lax

D = 384
FF = 1536
M = 64
IMG_DEV = 8
EXPERTS = 8
IMAGES = 256
N_EXPERT = 8
N_DP = 4


def draw_router(key, part):
    keys = jax.random.split(jax.random.fold_in(key, 11), 1)
    return (jnp.clip(jax.random.normal(keys[0], (D, EXPERTS), jnp.float32), -4.0, 4.0) * (3.0 / math.sqrt(D))).astype(jnp.bfloat16)


def levels(key, dims, cuts, low, high):
    level = 1.0
    for axis_at, parts in cuts:
        steps = jax.random.uniform(jax.random.fold_in(jax.random.fold_in(key, 6), axis_at), (parts,), jnp.float32, low / len(cuts), high / len(cuts))
        level = level * jnp.repeat(jnp.exp(steps), dims[axis_at] // parts).reshape((-1,) + (1,) * (len(dims) - 1 - axis_at))
    return level


def bell_draw(stream_key, dims, deviation, most, pieces=(), held_as=jnp.bfloat16):
    factor_of = levels(stream_key, dims, pieces, -0.22, 0.18) if pieces else 1.0
    values = jax.random.normal(stream_key, dims, jnp.float32) * deviation * factor_of
    return jnp.minimum(jnp.maximum(values, -most), most).astype(held_as)


def setup_inputs(seed: int = 0) -> dict:
    key_of = jax.random.split(jax.random.key(seed), 6)
    return {
        "tokens": bell_draw(key_of[0], (IMAGES, M, D), 1.0, 6.0, ((0, 32),)),
        "router": draw_router(jax.random.fold_in(key_of[5], 71), 0),
        "w_in": bell_draw(key_of[2], (EXPERTS, D, FF), D ** -0.5, 0.3125, ((0, 8),)),
        "w_out": bell_draw(key_of[3], (EXPERTS, D, FF), FF ** -0.5, 0.15625, ((0, 8),)),
        "out_grad": bell_draw(key_of[4], (IMAGES, M, D), 1.0, 6.0, ((0, 32),)),
    }


def gelu_pair(value):
    coef = math.sqrt(2.0 / math.pi)
    inner = coef * (value + 0.044715 * value * value * value)
    tangent = jnp.tanh(inner)
    result = 0.5 * value * (1.0 + tangent)
    slope = 0.5 * (1.0 + tangent) + 0.5 * value * (1.0 - tangent * tangent) * coef * (1.0 + 3.0 * 0.044715 * value * value)
    return (result, slope)

def round_keep(value):
    return lax.optimization_barrier(value.astype(jnp.bfloat16)).astype(jnp.float32)

def reference(tokens, router, w_in, w_out, out_grad):
    f32 = jnp.float32
    bf16 = jnp.bfloat16
    grouped = tokens.reshape(N_EXPERT, N_DP, IMG_DEV, M, D).transpose(1, 0, 2, 3, 4).reshape(N_DP, N_EXPERT * IMG_DEV, M, D)
    grads_in = out_grad.reshape(N_EXPERT, N_DP, IMG_DEV, M, D).transpose(1, 0, 2, 3, 4).reshape(N_DP, N_EXPERT * IMG_DEV, M, D)
    router_f = router.astype(f32)
    w_in_f = w_in.astype(f32)
    w_out_f = w_out.astype(f32)

    def group(carry, item):
        win_acc, wout_acc, router_acc = carry
        toks, cotan = item
        toks_f = toks.astype(f32)
        logits = jnp.einsum('bmd,de->bme', toks_f, router_f)
        dispatch = jax.nn.softmax(logits, axis=1)
        combine = jax.nn.softmax(logits, axis=2)
        dispatch_b = dispatch.astype(bf16).astype(f32)
        combine_b = combine.astype(bf16).astype(f32)
        slot_in = jnp.einsum('bme,bmd->bed', dispatch_b, toks_f).astype(bf16).astype(f32)
        slot_grad = jnp.einsum('bme,bmd->bed', combine_b, cotan.astype(f32)).astype(bf16).astype(f32)
        pre_act = jnp.einsum('bed,edf->bef', slot_in, w_in_f)
        value, slope = gelu_pair(pre_act)
        hidden = value.astype(bf16).astype(f32)
        slot_out = jnp.einsum('bef,edf->bed', hidden, w_out_f).astype(bf16).astype(f32)
        hid_grad = jnp.einsum('bed,edf->bef', slot_grad, w_out_f)
        pre_grad = (hid_grad * slope).astype(bf16).astype(f32)
        slot_in_grad = jnp.einsum('bef,edf->bed', pre_grad, w_in_f).astype(bf16).astype(f32)
        win_part = round_keep(jnp.einsum('bed,bef->edf', slot_in, pre_grad))
        wout_part = round_keep(jnp.einsum('bed,bef->edf', slot_grad, hidden))
        comb_grad = jnp.einsum('bmd,bed->bme', cotan.astype(f32), slot_out)
        disp_grad = jnp.einsum('bmd,bed->bme', toks_f, slot_in_grad)
        logit_grad = combine * (comb_grad - lax.optimization_barrier(jnp.sum(combine * comb_grad, axis=2, keepdims=True)))
        logit_grad = logit_grad + dispatch * (disp_grad - lax.optimization_barrier(jnp.sum(dispatch * disp_grad, axis=1, keepdims=True)))
        logit_grad = logit_grad.astype(bf16).astype(f32)
        tok_grad = jnp.einsum('bme,bed->bmd', dispatch_b, slot_in_grad) + jnp.einsum('bme,de->bmd', logit_grad, router_f)
        router_part = jnp.einsum('bmd,bme->de', toks_f, logit_grad)
        return ((win_acc + win_part, wout_acc + wout_part, router_acc + router_part), tok_grad.astype(bf16))
    init = (jnp.zeros((EXPERTS, D, FF), f32), jnp.zeros((EXPERTS, D, FF), f32), jnp.zeros((D, EXPERTS), f32))
    (win_grad, wout_grad, router_grad), stacked = lax.scan(group, init, (grouped, grads_in))
    tokens_grad = stacked.reshape(N_DP, N_EXPERT, IMG_DEV, M, D).transpose(1, 0, 2, 3, 4).reshape(IMAGES, M, D)
    return (tokens_grad, win_grad, wout_grad, router_grad)
```

```python
import math

import jax
import jax.numpy as jnp
from jax import lax
from jax.sharding import PartitionSpec as P

D = 384


def gelu_pair(value):
    coef = math.sqrt(2.0 / math.pi)
    inner = coef * (value + 0.044715 * value * value * value)
    tangent = jnp.tanh(inner)
    result = 0.5 * value * (1.0 + tangent)
    slope = 0.5 * (1.0 + tangent) + 0.5 * value * (1.0 - tangent * tangent) * coef * (
        1.0 + 3.0 * 0.044715 * value * value
    )
    return (result, slope)


def on_device(tokens, router, w_in, w_out, out_grad):
    f32 = jnp.float32
    bf16 = jnp.bfloat16
    owners = lax.axis_size("expert")
    images = tokens.shape[0]
    experts_all = router.shape[1]
    per_owner = w_in.shape[0]
    row_count = D // lax.axis_size("dp")
    logits = jnp.einsum("bmd,de->bme", tokens, router, preferred_element_type=f32)
    dispatch = jax.nn.softmax(logits, axis=1)
    combine = jax.nn.softmax(logits, axis=2)
    dispatch_b = dispatch.astype(bf16)
    combine_b = combine.astype(bf16)
    slot_in = jnp.einsum("bme,bmd->bed", dispatch_b, tokens, preferred_element_type=f32).astype(
        bf16
    )
    slot_grad = jnp.einsum("bme,bmd->bed", combine_b, out_grad, preferred_element_type=f32).astype(
        bf16
    )
    def to_owner(part):
        part = part.reshape(images, owners, per_owner, D)
        return jnp.transpose(part, (1, 2, 0, 3))

    sent = jnp.stack((to_owner(slot_in), to_owner(slot_grad)), axis=2)
    recv = lax.all_to_all(sent, "expert", split_axis=0, concat_axis=0, tiled=True)
    spread = lax.all_gather(recv, "dp", axis=0, tiled=False)

    def expert_pass(slots, cotan):
        pre_act = jnp.einsum("kbd,kdf->kbf", slots, w_in, preferred_element_type=f32)
        value, slope = gelu_pair(pre_act)
        hid_grad = jnp.einsum("kbd,kdf->kbf", cotan, w_out, preferred_element_type=f32)
        return value.astype(bf16), (hid_grad * slope).astype(bf16)

    def by_expert(part):
        return jnp.moveaxis(part, -3, 0).reshape(per_owner, -1, D)

    hidden, pre_grad = expert_pass(by_expert(recv[:, :, 0]), by_expert(recv[:, :, 1]))
    slot_out = jnp.einsum("kbf,kdf->kbd", hidden, w_out, preferred_element_type=f32).astype(bf16)
    back_grad = jnp.einsum("kbf,kdf->kbd", pre_grad, w_in, preferred_element_type=f32).astype(bf16)
    back = jnp.stack((slot_out, back_grad), axis=1).reshape(per_owner, 2, owners, images, D)
    back = lax.all_to_all(
        jnp.transpose(back, (2, 0, 1, 3, 4)), "expert", split_axis=0, concat_axis=0, tiled=True
    )
    slot_back = jnp.transpose(back[:, :, 0].reshape(experts_all, images, D), (1, 0, 2))
    slot_in_grad = jnp.transpose(back[:, :, 1].reshape(experts_all, images, D), (1, 0, 2))

    all_in, all_cot = by_expert(spread[:, :, :, 0]), by_expert(spread[:, :, :, 1])
    all_hidden, all_pre_grad = expert_pass(all_in, all_cot)
    first_row = lax.axis_index("dp") * row_count
    own_in = lax.dynamic_slice_in_dim(all_in, first_row, row_count, 2)
    own_cot = lax.dynamic_slice_in_dim(all_cot, first_row, row_count, 2)
    w_in_grad = jnp.einsum("kbd,kbf->kdf", own_in, all_pre_grad, preferred_element_type=f32)
    w_out_grad = jnp.einsum("kbd,kbf->kdf", own_cot, all_hidden, preferred_element_type=f32)
    comb_grad = jnp.einsum("bmd,bed->bme", out_grad, slot_back, preferred_element_type=f32)
    disp_grad = jnp.einsum("bmd,bed->bme", tokens, slot_in_grad, preferred_element_type=f32)
    logit_grad = combine * (comb_grad - jnp.sum(combine * comb_grad, axis=2, keepdims=True))
    logit_grad = logit_grad + dispatch * (
        disp_grad - jnp.sum(dispatch * disp_grad, axis=1, keepdims=True)
    )
    logit_grad = logit_grad.astype(bf16)
    tokens_grad = jnp.einsum("bme,bed->bmd", dispatch_b, slot_in_grad, preferred_element_type=f32)
    tokens_grad = tokens_grad + jnp.einsum(
        "bme,de->bmd", logit_grad, router, preferred_element_type=f32
    )
    tokens_grad = tokens_grad.astype(bf16)
    router_local = jnp.einsum("bmd,bme->de", tokens, logit_grad, preferred_element_type=f32)
    router_full = lax.psum(router_local, ("expert", "dp"))
    router_grad = lax.dynamic_slice_in_dim(
        router_full, lax.axis_index("dp") * row_count, row_count, 0
    )
    return (tokens_grad, w_in_grad, w_out_grad, router_grad)


def solution(mesh):
    placed = (
        P(("expert", "dp"), None, None),
        P(),
        P("expert", None, None),
        P("expert", None, None),
        P(("expert", "dp"), None, None),
    )
    return jax.shard_map(
        on_device,
        mesh=mesh,
        in_specs=placed,
        out_specs=(
            P(("expert", "dp"), None, None),
            P("expert", "dp", None),
            P("expert", "dp", None),
            P("dp", None),
        ),
        check_vma=False,
    )
```

```python
import functools
import math

import jax
import jax.numpy as jnp
from jax import lax
from jax.experimental import pallas as pl
from jax.experimental.pallas import tpu as pltpu
from jax.sharding import PartitionSpec as P

F32 = jnp.float32
BF16 = jnp.bfloat16
VMEM_BYTES = 24 * 1024 * 1024


def gelu_pair(value):
    coef = math.sqrt(2.0 / math.pi)
    square = value * value
    tangent = jnp.tanh(coef * value * (1.0 + 0.044715 * square))
    half = 0.5 * (1.0 + tangent)
    slope = half + 0.5 * coef * value * (1.0 - tangent * tangent) * (1.0 + 3.0 * 0.044715 * square)
    return value * half, slope


def dot(left, right, left_dim, right_dim):
    return lax.dot_general(
        left, right, (((left_dim,), (right_dim,)), ((), ())), preferred_element_type=F32
    )


def own_image(experts, images, columns):
    shape = (experts, images, columns)
    image = lax.broadcasted_iota(jnp.int32, shape, 1)
    token = lax.broadcasted_iota(jnp.int32, shape, 2)
    low = image * (columns // images)
    inside = (token >= low) & (token < low + columns // images)
    return inside.reshape(experts * images, columns)


def spread_rows(compact, images):
    experts, columns = compact.shape
    wide = jnp.broadcast_to(compact[:, None, :], (experts, images, columns))
    return wide.reshape(experts * images, columns)


def fold_rows(block, images):
    rows, columns = block.shape
    return jnp.sum(block.reshape(rows // images, images, columns), axis=1)


def pair_rows(first, second, groups):
    images = first.shape[0] // groups
    first = first.reshape(groups, images, first.shape[1])
    second = second.reshape(groups, images, second.shape[1])
    return jnp.concatenate((first, second), axis=1).astype(BF16)


def split_rows(pairs):
    groups, both, width = pairs.shape
    wide = pairs.astype(F32)
    first = wide[:, : both // 2].reshape(groups * both // 2, width)
    second = wide[:, both // 2 :].reshape(groups * both // 2, width)
    return first.astype(BF16), second.astype(BF16)


def slots_kernel(images, tokens_ref, router_ref, grad_ref, sent_ref, soft_ref):
    tokens = tokens_ref[...]
    columns = tokens.shape[0]
    experts = router_ref.shape[0]
    logits = dot(router_ref[...], tokens, 1, 1)
    mask = own_image(experts, images, columns)
    top = jnp.max(logits, axis=0, keepdims=True)
    combine = jnp.exp(logits - top)
    combine = combine / jnp.sum(combine, axis=0, keepdims=True)
    block = jnp.where(mask, spread_rows(logits, images), -jnp.inf)
    block = jnp.exp(block - jnp.max(block, axis=1, keepdims=True))
    block = block / jnp.sum(block, axis=1, keepdims=True)
    soft_ref[0] = fold_rows(block, images)
    soft_ref[1] = combine
    combine_block = jnp.where(mask, spread_rows(combine, images), 0.0)
    slot_in = dot(block.astype(BF16), tokens, 1, 0)
    slot_grad = dot(combine_block.astype(BF16), grad_ref[...], 1, 0)
    sent_ref[...] = pair_rows(slot_in, slot_grad, experts)


def expert_kernel(recv_ref, win_ref, wout_ref, back_ref, *, step):
    slots, cotan = split_rows(recv_ref[...])
    out = jnp.zeros(slots.shape, F32)
    back = jnp.zeros(slots.shape, F32)
    for start in range(0, win_ref.shape[1], step):
        w_in = win_ref[:, start : start + step]
        w_out = wout_ref[:, start : start + step]
        value, slope = gelu_pair(dot(slots, w_in, 1, 0))
        pre_grad = dot(cotan, w_out, 1, 0) * slope
        out = out + dot(value.astype(BF16), w_out, 1, 1)
        back = back + dot(pre_grad.astype(BF16), w_in, 1, 1)
    back_ref[...] = pair_rows(out, back, recv_ref.shape[0])


def tokens_kernel(
    images, back_ref, tokens_ref, router_ref, grad_ref, soft_ref, out_ref, send_ref
):
    tokens = tokens_ref[...]
    columns = tokens.shape[0]
    experts = router_ref.shape[0]
    slot_out, slot_in_grad = split_rows(back_ref[...])
    dispatch, combine = soft_ref[0], soft_ref[1]
    mask = own_image(experts, images, columns)
    comb = fold_rows(jnp.where(mask, dot(slot_out, grad_ref[...], 1, 1), 0.0), images)
    disp = jnp.where(mask, dot(slot_in_grad, tokens, 1, 1), 0.0)
    dispatch_block = jnp.where(mask, spread_rows(dispatch, images), 0.0)
    mean = jnp.sum(dispatch_block * disp, axis=1, keepdims=True)
    from_dispatch = fold_rows(dispatch_block * (disp - mean), images)
    from_combine = combine * (comb - jnp.sum(combine * comb, axis=0, keepdims=True))
    logit_grad = (from_combine + from_dispatch).astype(BF16)
    out = dot(dispatch_block.astype(BF16), slot_in_grad, 0, 0)
    out = out + dot(logit_grad, router_ref[...], 0, 0)
    out_ref[...] = out.astype(BF16)
    part = dot(logit_grad, tokens, 1, 0)
    owners, shares, _, width = send_ref.shape
    for share in range(shares):
        piece = part[:, share * width : (share + 1) * width]
        for owner in range(owners):
            send_ref[owner, share] = piece


def weights_kernel(share_ref, spread_ref, win_ref, wout_ref, win_out, wout_out, *, step):
    width = spread_ref.shape[-1]
    row_count = win_out.shape[0]
    slots, cotan = split_rows(spread_ref[...].reshape((-1,) + spread_ref.shape[2:]))
    shape = (row_count, width)
    row = lax.broadcasted_iota(jnp.int32, shape, 0) + share_ref[0] * row_count
    pick = jnp.where(lax.broadcasted_iota(jnp.int32, shape, 1) == row, 1.0, 0.0).astype(BF16)
    own_slots = dot(pick, slots, 1, 1).astype(BF16)
    own_cotan = dot(pick, cotan, 1, 1).astype(BF16)

    @pl.when(pl.program_id(0) == 0)
    def _():
        win_out[...] = jnp.zeros_like(win_out)
        wout_out[...] = jnp.zeros_like(wout_out)

    for start in range(0, win_ref.shape[1], step):
        part = slice(start, start + step)
        value, slope = gelu_pair(dot(slots, win_ref[:, part], 1, 0))
        pre_grad = dot(cotan, wout_ref[:, part], 1, 0) * slope
        win_out[:, part] += dot(own_slots, pre_grad.astype(BF16), 1, 0)
        wout_out[:, part] += dot(own_cotan, value.astype(BF16), 1, 0)


def on_device(tokens, router, w_in, w_out, out_grad):
    owners, shares = lax.axis_size("expert"), lax.axis_size("dp")
    images, per_image, width = tokens.shape
    experts = router.shape[1]
    hidden = w_in.shape[2]
    columns = images * per_image
    row_count = width // shares
    tokens2 = tokens.reshape(columns, width)
    grad2 = out_grad.reshape(columns, width)
    router_rows = router.T
    w_in2, w_out2 = w_in.reshape(width, hidden), w_out.reshape(width, hidden)
    params = pltpu.CompilerParams(vmem_limit_bytes=VMEM_BYTES)

    def struct(shape, dtype):
        return jax.ShapeDtypeStruct(shape, dtype)

    sent, soft = pl.pallas_call(
        functools.partial(slots_kernel, images),
        out_shape=(
            struct((experts, 2 * images, width), BF16),
            struct((2, experts, columns), F32),
        ),
        compiler_params=params,
        name="slots",
    )(tokens2, router_rows, grad2)
    recv = lax.all_to_all(sent, "expert", split_axis=0, concat_axis=0, tiled=True)
    back = pl.pallas_call(
        functools.partial(expert_kernel, step=512),
        out_shape=struct(recv.shape, BF16),
        compiler_params=params,
        name="expert",
    )(recv, w_in2, w_out2)
    recv, back = lax.optimization_barrier((recv, back))
    slots_back = lax.all_to_all(back, "expert", split_axis=0, concat_axis=0, tiled=True)
    spread = lax.all_gather(recv, "dp", axis=0, tiled=False)

    tokens_grad, router_send = pl.pallas_call(
        functools.partial(tokens_kernel, images),
        out_shape=(
            struct((columns, width), BF16),
            struct((owners, shares, experts, row_count), F32),
        ),
        compiler_params=params,
        name="tokens",
    )(slots_back, tokens2, router_rows, grad2, soft)
    spread, router_send = lax.optimization_barrier((spread, router_send))
    router_parts = lax.all_to_all(
        router_send.reshape(owners * shares, experts, row_count),
        ("expert", "dp"),
        split_axis=0,
        concat_axis=0,
        tiled=True,
    )

    group = max(1, min(shares, 256 // (owners * images)))
    w_in_grad, w_out_grad = pl.pallas_call(
        functools.partial(weights_kernel, step=512),
        grid=(shares // group,),
        in_specs=[
            pl.BlockSpec(memory_space=pltpu.SMEM),
            pl.BlockSpec((group,) + recv.shape, lambda i: (i, 0, 0, 0)),
            pl.BlockSpec((width, hidden), lambda i: (0, 0)),
            pl.BlockSpec((width, hidden), lambda i: (0, 0)),
        ],
        out_specs=[pl.BlockSpec((row_count, hidden), lambda i: (0, 0))] * 2,
        out_shape=[struct((row_count, hidden), F32)] * 2,
        compiler_params=params,
        name="weights",
    )(lax.axis_index("dp").reshape(1), spread, w_in2, w_out2)
    router_grad = jnp.sum(router_parts, axis=0).T
    return (
        tokens_grad.reshape(tokens.shape),
        w_in_grad.reshape(1, row_count, hidden),
        w_out_grad.reshape(1, row_count, hidden),
        router_grad,
    )


def solution(mesh):
    placed = (
        P(("expert", "dp"), None, None),
        P(),
        P("expert", None, None),
        P("expert", None, None),
        P(("expert", "dp"), None, None),
    )
    return jax.shard_map(
        on_device,
        mesh=mesh,
        in_specs=placed,
        out_specs=(
            P(("expert", "dp"), None, None),
            P("expert", "dp", None),
            P("expert", "dp", None),
            P("dp", None),
        ),
        check_vma=False,
    )
```

```python
import functools
import math

import jax
import jax.numpy as jnp
from jax import lax
from jax.experimental import pallas as pl
from jax.experimental.pallas import tpu as pltpu
from jax.sharding import PartitionSpec as P

F32 = jnp.float32
BF16 = jnp.bfloat16
VMEM_BYTES = 24 * 1024 * 1024
WHOLE_BYTES = 56 * 1024 * 1024


def gelu_pair(value):
    coef = math.sqrt(2.0 / math.pi)
    square = value * value
    tangent = jnp.tanh(coef * value * (1.0 + 0.044715 * square))
    half = 0.5 * (1.0 + tangent)
    slope = half + 0.5 * coef * value * (1.0 - tangent * tangent) * (1.0 + 3.0 * 0.044715 * square)
    return value * half, slope


def dot(left, right, left_dim, right_dim):
    return lax.dot_general(
        left, right, (((left_dim,), (right_dim,)), ((), ())), preferred_element_type=F32
    )


def own_image(experts, images, columns):
    shape = (experts, images, columns)
    image = lax.broadcasted_iota(jnp.int32, shape, 1)
    token = lax.broadcasted_iota(jnp.int32, shape, 2)
    low = image * (columns // images)
    inside = (token >= low) & (token < low + columns // images)
    return inside.reshape(experts * images, columns)


def spread_rows(compact, images):
    experts, columns = compact.shape
    wide = jnp.broadcast_to(compact[:, None, :], (experts, images, columns))
    return wide.reshape(experts * images, columns)


def fold_rows(block, images):
    rows, columns = block.shape
    return jnp.sum(block.reshape(rows // images, images, columns), axis=1)


def split_rows(pairs):
    groups, both, width = pairs.shape
    wide = pairs.astype(F32)
    first = wide[:, : both // 2].reshape(groups * both // 2, width)
    second = wide[:, both // 2 :].reshape(groups * both // 2, width)
    return first.astype(BF16), second.astype(BF16)


def order_rows(me, rows):
    count = rows.shape[0]
    to = lax.broadcasted_iota(jnp.int32, (count, count), 0) ^ me
    pick = jnp.where(lax.broadcasted_iota(jnp.int32, (count, count), 1) == to, 1.0, 0.0)
    return dot(pick.astype(BF16), rows, 1, 0).astype(BF16)


def slots_kernel(images, me_ref, tokens_ref, router_ref, grad_ref, soft_ref, *sent):
    tokens = tokens_ref[...]
    columns = tokens.shape[0]
    experts = router_ref.shape[0]
    logits = dot(order_rows(me_ref[0], router_ref[...]), tokens, 1, 1)
    mask = own_image(experts, images, columns)
    top = jnp.max(logits, axis=0, keepdims=True)
    combine = jnp.exp(logits - top)
    combine = combine / jnp.sum(combine, axis=0, keepdims=True)
    block = jnp.where(mask, spread_rows(logits, images), -jnp.inf)
    block = jnp.exp(block - jnp.max(block, axis=1, keepdims=True))
    block = block / jnp.sum(block, axis=1, keepdims=True)
    soft_ref[0] = fold_rows(block, images)
    soft_ref[1] = combine
    combine_block = jnp.where(mask, spread_rows(combine, images), 0.0)
    slot_in = dot(block.astype(BF16), tokens, 1, 0)
    slot_grad = dot(combine_block.astype(BF16), grad_ref[...], 1, 0)
    write_pairs(sent, slot_in, slot_grad)


def write_pairs(refs, first, second):
    images = first.shape[0] // len(refs)
    for k, ref in enumerate(refs):
        rows = slice(k * images, (k + 1) * images)
        ref[...] = jnp.concatenate((first[rows], second[rows]), axis=0).astype(BF16)


def read_pairs(refs):
    parts = [ref[...].astype(F32) for ref in refs]
    half = parts[0].shape[0] // 2
    first = jnp.concatenate([part[:half] for part in parts], axis=0)
    second = jnp.concatenate([part[half:] for part in parts], axis=0)
    return first.astype(BF16), second.astype(BF16)


def expert_kernel(owners, step, *refs):
    recv, (win_hbm, wout_hbm) = refs[:owners], refs[owners : owners + 2]
    back_refs, all_ref = refs[owners + 2 : 2 * owners + 2], refs[2 * owners + 2]
    win_ref, wout_ref, sems = refs[2 * owners + 3 :]
    starts = range(0, win_ref.shape[1], step)

    def load(which, chunk):
        source, target = ((win_hbm, win_ref), (wout_hbm, wout_ref))[which]
        part = (slice(None), pl.ds(chunk * step, step))
        return pltpu.make_async_copy(source.at[part], target.at[part], sems.at[which, chunk])

    for chunk in range(len(starts)):
        load(0, chunk).start()
        load(1, chunk).start()
    for k, ref in enumerate(recv):
        all_ref[k] = ref[...]
    slots, cotan = read_pairs(recv)
    out = jnp.zeros(slots.shape, F32)
    back = jnp.zeros(slots.shape, F32)
    for chunk, start in enumerate(starts):
        load(0, chunk).wait()
        load(1, chunk).wait()
        w_in = win_ref[:, start : start + step]
        w_out = wout_ref[:, start : start + step]
        value, slope = gelu_pair(dot(slots, w_in, 1, 0))
        pre_grad = dot(cotan, w_out, 1, 0) * slope
        out = out + dot(value.astype(BF16), w_out, 1, 1)
        back = back + dot(pre_grad.astype(BF16), w_in, 1, 1)
    write_pairs(back_refs, out, back)


def tokens_kernel(
    images, me_ref, tokens_ref, router_ref, grad_ref, soft_ref, *refs
):
    back_refs, (out_ref, send_ref) = refs[:-2], refs[-2:]
    me = me_ref[0]
    tokens = tokens_ref[...]
    columns = tokens.shape[0]
    experts = router_ref.shape[0]
    slot_out, slot_in_grad = read_pairs(back_refs)
    dispatch, combine = soft_ref[0], soft_ref[1]
    mask = own_image(experts, images, columns)
    comb = fold_rows(jnp.where(mask, dot(slot_out, grad_ref[...], 1, 1), 0.0), images)
    disp = jnp.where(mask, dot(slot_in_grad, tokens, 1, 1), 0.0)
    dispatch_block = jnp.where(mask, spread_rows(dispatch, images), 0.0)
    mean = jnp.sum(dispatch_block * disp, axis=1, keepdims=True)
    from_dispatch = fold_rows(dispatch_block * (disp - mean), images)
    from_combine = combine * (comb - jnp.sum(combine * comb, axis=0, keepdims=True))
    logit_grad = order_rows(me, (from_combine + from_dispatch).astype(BF16))
    part = dot(logit_grad, tokens, 1, 0)
    owners, shares, _, width = send_ref.shape
    for share in range(shares):
        piece = part[:, share * width : (share + 1) * width]
        for owner in range(owners):
            send_ref[owner, share] = piece
    out = dot(dispatch_block.astype(BF16), slot_in_grad, 0, 0)
    out = out + dot(logit_grad, router_ref[...], 0, 0)
    out_ref[...] = out.astype(BF16)


def weights_kernel(share_ref, *refs, step):
    spread, (win_ref, wout_ref, win_out, wout_out) = refs[:-4], refs[-4:]
    row_count = win_out.shape[0]
    pairs = [
        split_rows(ref[...].reshape((-1,) + ref.shape[-2:])) for ref in spread
    ]
    slots = jnp.concatenate([pair[0] for pair in pairs], axis=0)
    cotan = jnp.concatenate([pair[1] for pair in pairs], axis=0)
    shape = (row_count, slots.shape[1])
    row = lax.broadcasted_iota(jnp.int32, shape, 0) + share_ref[0] * row_count
    pick = jnp.where(lax.broadcasted_iota(jnp.int32, shape, 1) == row, 1.0, 0.0).astype(BF16)
    own_slots = dot(pick, slots, 1, 1).astype(BF16)
    own_cotan = dot(pick, cotan, 1, 1).astype(BF16)

    @pl.when(pl.program_id(0) == 0)
    def _():
        win_out[...] = jnp.zeros_like(win_out)
        wout_out[...] = jnp.zeros_like(wout_out)

    for start in range(0, win_ref.shape[1], step):
        part = slice(start, start + step)
        value, slope = gelu_pair(dot(slots, win_ref[:, part], 1, 0))
        pre_grad = dot(cotan, wout_ref[:, part], 1, 0) * slope
        win_out[:, part] += dot(own_slots, pre_grad.astype(BF16), 1, 0)
        wout_out[:, part] += dot(own_cotan, value.astype(BF16), 1, 0)


def exchange(chunks, axis):
    count = len(chunks)
    got = [None] * count
    got[0] = chunks[0]
    for k in range(count - 1, 0, -1):
        got[k] = lax.ppermute(chunks[k], axis, [(i, i ^ k) for i in range(count)])
    return got


def on_device(tokens, router, w_in, w_out, out_grad):
    owners, shares = lax.axis_size("expert"), lax.axis_size("dp")
    images, per_image, width = tokens.shape
    experts = router.shape[1]
    hidden = w_in.shape[2]
    columns = images * per_image
    row_count = width // shares
    tokens2 = tokens.reshape(columns, width)
    grad2 = out_grad.reshape(columns, width)
    router_rows = router.T
    w_in2, w_out2 = w_in.reshape(width, hidden), w_out.reshape(width, hidden)
    params = pltpu.CompilerParams(vmem_limit_bytes=VMEM_BYTES)
    whole = pltpu.CompilerParams(vmem_limit_bytes=WHOLE_BYTES)

    def struct(shape, dtype):
        return jax.ShapeDtypeStruct(shape, dtype)

    me = lax.axis_index("expert").reshape(1)
    share = lax.axis_index("dp").reshape(1)
    in_smem = pl.BlockSpec(memory_space=pltpu.SMEM)
    in_vmem = pl.BlockSpec(memory_space=pltpu.VMEM)
    in_place = pl.BlockSpec(memory_space=pl.ANY)
    chunk = struct((2 * images, width), BF16)
    soft, *sent = pl.pallas_call(
        functools.partial(slots_kernel, images),
        in_specs=[in_smem] + [in_vmem] * 3,
        out_shape=[struct((2, experts, columns), F32)] + [chunk] * owners,
        compiler_params=whole,
        name="slots",
    )(me, tokens2, router_rows, grad2)
    recv = exchange(sent, "expert")
    step = 512
    *back, recv_all = pl.pallas_call(
        functools.partial(expert_kernel, owners, step),
        in_specs=[in_vmem] * owners + [in_place] * 2,
        out_shape=[chunk] * owners + [struct((owners, 2 * images, width), BF16)],
        scratch_shapes=[
            pltpu.VMEM((width, hidden), BF16),
            pltpu.VMEM((width, hidden), BF16),
            pltpu.SemaphoreType.DMA((2, hidden // step)),
        ],
        compiler_params=whole,
        name="expert",
    )(*recv, w_in2, w_out2)
    slots_back = exchange(back, "expert")
    few = shares * owners * images <= 512
    if few:
        spread = exchange([recv_all] * shares, "dp")
    else:
        spread = [lax.all_gather(recv_all, "dp", axis=0, tiled=False)]

    tokens_grad, router_send = pl.pallas_call(
        functools.partial(tokens_kernel, images),
        in_specs=[in_smem] + [in_vmem] * (4 + owners),
        out_shape=(
            struct((columns, width), BF16),
            struct((owners, shares, experts, row_count), F32),
        ),
        compiler_params=params,
        name="tokens",
    )(me, tokens2, router_rows, grad2, soft, *slots_back)
    *spread, router_send = lax.optimization_barrier((*spread, router_send))
    router_parts = lax.all_to_all(
        router_send.reshape(owners * shares, experts, row_count),
        ("expert", "dp"),
        split_axis=0,
        concat_axis=0,
        tiled=True,
    )

    if few:
        blocks = [pl.BlockSpec(recv_all.shape, lambda i: (0, 0, 0))] * shares
    else:
        blocks = [pl.BlockSpec((1,) + recv_all.shape, lambda i: (i, 0, 0, 0))]
    w_in_grad, w_out_grad = pl.pallas_call(
        functools.partial(weights_kernel, step=512),
        grid=(1 if few else shares,),
        in_specs=[
            in_smem,
            *blocks,
            pl.BlockSpec((width, hidden), lambda i: (0, 0)),
            pl.BlockSpec((width, hidden), lambda i: (0, 0)),
        ],
        out_specs=[pl.BlockSpec((row_count, hidden), lambda i: (0, 0))] * 2,
        out_shape=[struct((row_count, hidden), F32)] * 2,
        compiler_params=params,
        name="weights",
    )(share, *spread, w_in2, w_out2)
    router_grad = jnp.sum(router_parts, axis=0).T
    return (
        tokens_grad.reshape(tokens.shape),
        w_in_grad.reshape(1, row_count, hidden),
        w_out_grad.reshape(1, row_count, hidden),
        router_grad,
    )


def solution(mesh):
    placed = (
        P(("expert", "dp"), None, None),
        P(),
        P("expert", None, None),
        P("expert", None, None),
        P(("expert", "dp"), None, None),
    )
    return jax.shard_map(
        on_device,
        mesh=mesh,
        in_specs=placed,
        out_specs=(
            P(("expert", "dp"), None, None),
            P("expert", "dp", None),
            P("expert", "dp", None),
            P("dp", None),
        ),
        check_vma=False,
    )
```

```python
import functools
import math

import jax
import jax.numpy as jnp
from jax import lax
from jax.experimental import pallas as pl
from jax.experimental.pallas import tpu as pltpu
from jax.sharding import PartitionSpec as P

F32 = jnp.float32
BF16 = jnp.bfloat16
VMEM_BYTES = 24 * 1024 * 1024
WHOLE_BYTES = 56 * 1024 * 1024


def gelu_pair(value):
    coef = math.sqrt(2.0 / math.pi)
    square = value * value
    tangent = jnp.tanh(coef * value * (1.0 + 0.044715 * square))
    half = 0.5 * (1.0 + tangent)
    slope = half + 0.5 * coef * value * (1.0 - tangent * tangent) * (1.0 + 3.0 * 0.044715 * square)
    return value * half, slope


def dot(left, right, left_dim, right_dim):
    return lax.dot_general(
        left, right, (((left_dim,), (right_dim,)), ((), ())), preferred_element_type=F32
    )


def own_image(experts, images, columns):
    shape = (experts, images, columns)
    image = lax.broadcasted_iota(jnp.int32, shape, 1)
    token = lax.broadcasted_iota(jnp.int32, shape, 2)
    low = image * (columns // images)
    inside = (token >= low) & (token < low + columns // images)
    return inside.reshape(experts * images, columns)


def spread_rows(compact, images):
    experts, columns = compact.shape
    wide = jnp.broadcast_to(compact[:, None, :], (experts, images, columns))
    return wide.reshape(experts * images, columns)


def fold_rows(block, images):
    rows, columns = block.shape
    return jnp.sum(block.reshape(rows // images, images, columns), axis=1)


def pair_rows(first, second, groups):
    images = first.shape[0] // groups
    first = first.reshape(groups, images, first.shape[1])
    second = second.reshape(groups, images, second.shape[1])
    return jnp.concatenate((first, second), axis=1).astype(BF16)


def split_rows(pairs):
    groups, both, width = pairs.shape
    wide = pairs.astype(F32)
    first = wide[:, : both // 2].reshape(groups * both // 2, width)
    second = wide[:, both // 2 :].reshape(groups * both // 2, width)
    return first.astype(BF16), second.astype(BF16)


def softmaxes(router, tokens, images):
    logits = dot(router, tokens, 1, 1)
    experts, columns = logits.shape
    mask = own_image(experts, images, columns)
    combine = jnp.exp(logits - jnp.max(logits, axis=0, keepdims=True))
    combine = combine / jnp.sum(combine, axis=0, keepdims=True)
    block = jnp.where(mask, spread_rows(logits, images), -jnp.inf)
    block = jnp.exp(block - jnp.max(block, axis=1, keepdims=True))
    block = block / jnp.sum(block, axis=1, keepdims=True)
    return block, combine, mask


def slots_kernel(images, tokens_hbm, router_hbm, grad_hbm, sent_ref, *scratch):
    tokens_ref, router_ref, grad_ref, sems = scratch
    loads = [
        pltpu.make_async_copy(source, target, sems.at[i])
        for i, (source, target) in enumerate(
            ((tokens_hbm, tokens_ref), (router_hbm, router_ref), (grad_hbm, grad_ref))
        )
    ]
    for load in loads:
        load.start()
    loads[0].wait()
    loads[1].wait()
    tokens = tokens_ref[...]
    block, combine, mask = softmaxes(router_ref[...], tokens, images)
    combine_block = jnp.where(mask, spread_rows(combine, images), 0.0)
    slot_in = dot(block.astype(BF16), tokens, 1, 0)
    loads[2].wait()
    slot_grad = dot(combine_block.astype(BF16), grad_ref[...], 1, 0)
    sent_ref[...] = pair_rows(slot_in, slot_grad, combine.shape[0])


def stage_kernel(win_hbm, wout_hbm, win_ref, wout_ref, sems):
    loads = (
        pltpu.make_async_copy(win_hbm, win_ref, sems.at[0]),
        pltpu.make_async_copy(wout_hbm, wout_ref, sems.at[1]),
    )
    for load in loads:
        load.start()
    for load in loads:
        load.wait()


def expert_kernel(recv_ref, win_ref, wout_ref, back_ref, *, step):
    slots, cotan = split_rows(recv_ref[...])
    out = jnp.zeros(slots.shape, F32)
    back = jnp.zeros(slots.shape, F32)
    for start in range(0, win_ref.shape[1], step):
        w_in = win_ref[:, start : start + step]
        w_out = wout_ref[:, start : start + step]
        value, slope = gelu_pair(dot(slots, w_in, 1, 0))
        pre_grad = dot(cotan, w_out, 1, 0) * slope
        out = out + dot(value.astype(BF16), w_out, 1, 1)
        back = back + dot(pre_grad.astype(BF16), w_in, 1, 1)
    back_ref[...] = pair_rows(out, back, recv_ref.shape[0])


def tokens_kernel(
    images, back_ref, tokens_ref, router_ref, grad_ref, out_ref, send_ref
):
    tokens = tokens_ref[...]
    slot_out, slot_in_grad = split_rows(back_ref[...])
    dispatch_block, combine, mask = softmaxes(router_ref[...], tokens, images)
    comb = fold_rows(jnp.where(mask, dot(slot_out, grad_ref[...], 1, 1), 0.0), images)
    disp = jnp.where(mask, dot(slot_in_grad, tokens, 1, 1), 0.0)
    mean = jnp.sum(dispatch_block * disp, axis=1, keepdims=True)
    from_dispatch = fold_rows(dispatch_block * (disp - mean), images)
    from_combine = combine * (comb - jnp.sum(combine * comb, axis=0, keepdims=True))
    logit_grad = (from_combine + from_dispatch).astype(BF16)
    out = dot(dispatch_block.astype(BF16), slot_in_grad, 0, 0)
    out = out + dot(logit_grad, router_ref[...], 0, 0)
    out_ref[...] = out.astype(BF16)
    part = dot(logit_grad, tokens, 1, 0)
    owners, shares, _, width = send_ref.shape
    for share in range(shares):
        piece = part[:, share * width : (share + 1) * width]
        for owner in range(owners):
            send_ref[owner, share] = piece


def weights_kernel(share_ref, spread_ref, win_ref, wout_ref, win_out, wout_out, *, step):
    width = spread_ref.shape[-1]
    row_count = win_out.shape[0]
    slots, cotan = split_rows(spread_ref[...].reshape((-1,) + spread_ref.shape[2:]))
    shape = (row_count, width)
    row = lax.broadcasted_iota(jnp.int32, shape, 0) + share_ref[0] * row_count
    pick = jnp.where(lax.broadcasted_iota(jnp.int32, shape, 1) == row, 1.0, 0.0).astype(BF16)
    own_slots = dot(pick, slots, 1, 1).astype(BF16)
    own_cotan = dot(pick, cotan, 1, 1).astype(BF16)

    @pl.when(pl.program_id(0) == 0)
    def _():
        win_out[...] = jnp.zeros_like(win_out)
        wout_out[...] = jnp.zeros_like(wout_out)

    for start in range(0, win_ref.shape[1], step):
        part = slice(start, start + step)
        value, slope = gelu_pair(dot(slots, win_ref[:, part], 1, 0))
        pre_grad = dot(cotan, wout_ref[:, part], 1, 0) * slope
        win_out[:, part] += dot(own_slots, pre_grad.astype(BF16), 1, 0)
        wout_out[:, part] += dot(own_cotan, value.astype(BF16), 1, 0)


def on_device(tokens, router, w_in, w_out, out_grad):
    owners, shares = lax.axis_size("expert"), lax.axis_size("dp")
    images, per_image, width = tokens.shape
    experts = router.shape[1]
    hidden = w_in.shape[2]
    columns = images * per_image
    row_count = width // shares
    tokens2 = tokens.reshape(columns, width)
    grad2 = out_grad.reshape(columns, width)
    router_rows = router.T
    w_in2, w_out2 = w_in.reshape(width, hidden), w_out.reshape(width, hidden)
    params = pltpu.CompilerParams(vmem_limit_bytes=VMEM_BYTES)
    whole = pltpu.CompilerParams(vmem_limit_bytes=WHOLE_BYTES)

    def struct(shape, dtype):
        return jax.ShapeDtypeStruct(shape, dtype)

    in_place = pl.BlockSpec(memory_space=pl.ANY)
    sent = pl.pallas_call(
        functools.partial(slots_kernel, images),
        in_specs=[in_place] * 3,
        out_shape=struct((experts, 2 * images, width), BF16),
        scratch_shapes=[
            pltpu.VMEM((columns, width), BF16),
            pltpu.VMEM((experts, width), BF16),
            pltpu.VMEM((columns, width), BF16),
            pltpu.SemaphoreType.DMA((3,)),
        ],
        compiler_params=whole,
        name="slots",
    )(tokens2, router_rows, grad2)
    w_in2, w_out2 = pl.pallas_call(
        stage_kernel,
        in_specs=[in_place] * 2,
        out_specs=[in_place] * 2,
        out_shape=[struct((width, hidden), BF16)] * 2,
        scratch_shapes=[pltpu.SemaphoreType.DMA((2,))],
        compiler_params=pltpu.CompilerParams(vmem_limit_bytes=1024 * 1024),
        cost_estimate=pl.CostEstimate(
            flops=0, bytes_accessed=8 * width * hidden, transcendentals=0
        ),
        name="stage",
    )(w_in2, w_out2)
    recv = lax.all_to_all(sent, "expert", split_axis=0, concat_axis=0, tiled=True)
    back = pl.pallas_call(
        functools.partial(expert_kernel, step=512),
        out_shape=struct(recv.shape, BF16),
        compiler_params=params,
        name="expert",
    )(recv, w_in2, w_out2)
    recv, back = lax.optimization_barrier((recv, back))
    slots_back = lax.all_to_all(back, "expert", split_axis=0, concat_axis=0, tiled=True)
    spread = lax.all_gather(recv, "dp", axis=0, tiled=False)

    tokens_grad, router_send = pl.pallas_call(
        functools.partial(tokens_kernel, images),
        out_shape=(
            struct((columns, width), BF16),
            struct((owners, shares, experts, row_count), F32),
        ),
        compiler_params=params,
        name="tokens",
    )(slots_back, tokens2, router_rows, grad2)
    spread, router_send = lax.optimization_barrier((spread, router_send))
    router_parts = lax.all_to_all(
        router_send.reshape(owners * shares, experts, row_count),
        ("expert", "dp"),
        split_axis=0,
        concat_axis=0,
        tiled=True,
    )

    group = max(1, min(shares, 256 // (owners * images)))
    w_in_grad, w_out_grad = pl.pallas_call(
        functools.partial(weights_kernel, step=512),
        grid=(shares // group,),
        in_specs=[
            pl.BlockSpec(memory_space=pltpu.SMEM),
            pl.BlockSpec((group,) + recv.shape, lambda i: (i, 0, 0, 0)),
            pl.BlockSpec((width, hidden), lambda i: (0, 0)),
            pl.BlockSpec((width, hidden), lambda i: (0, 0)),
        ],
        out_specs=[pl.BlockSpec((row_count, hidden), lambda i: (0, 0))] * 2,
        out_shape=[struct((row_count, hidden), F32)] * 2,
        compiler_params=params,
        name="weights",
    )(lax.axis_index("dp").reshape(1), spread, w_in2, w_out2)
    router_grad = jnp.sum(router_parts, axis=0).T
    return (
        tokens_grad.reshape(tokens.shape),
        w_in_grad.reshape(1, row_count, hidden),
        w_out_grad.reshape(1, row_count, hidden),
        router_grad,
    )


def solution(mesh):
    placed = (
        P(("expert", "dp"), None, None),
        P(),
        P("expert", None, None),
        P("expert", None, None),
        P(("expert", "dp"), None, None),
    )
    return jax.shard_map(
        on_device,
        mesh=mesh,
        in_specs=placed,
        out_specs=(
            P(("expert", "dp"), None, None),
            P("expert", "dp", None),
            P("expert", "dp", None),
            P("dp", None),
        ),
        check_vma=False,
    )
```

```python
import functools
import math

import jax
import jax.numpy as jnp
from jax import lax
from jax.experimental import pallas as pl
from jax.experimental.pallas import tpu as pltpu
from jax.sharding import PartitionSpec as P

F32 = jnp.float32
BF16 = jnp.bfloat16
VMEM_BYTES = 24 * 1024 * 1024
WHOLE_BYTES = 56 * 1024 * 1024


def gelu_pair(value):
    coef = math.sqrt(2.0 / math.pi)
    square = value * value
    tangent = jnp.tanh(coef * value * (1.0 + 0.044715 * square))
    half = 0.5 * (1.0 + tangent)
    slope = half + 0.5 * coef * value * (1.0 - tangent * tangent) * (1.0 + 3.0 * 0.044715 * square)
    return value * half, slope


def dot(left, right, left_dim, right_dim):
    return lax.dot_general(
        left, right, (((left_dim,), (right_dim,)), ((), ())), preferred_element_type=F32
    )


def own_image(experts, images, columns):
    shape = (experts, images, columns)
    image = lax.broadcasted_iota(jnp.int32, shape, 1)
    token = lax.broadcasted_iota(jnp.int32, shape, 2)
    low = image * (columns // images)
    inside = (token >= low) & (token < low + columns // images)
    return inside.reshape(experts * images, columns)


def spread_rows(compact, images):
    experts, columns = compact.shape
    wide = jnp.broadcast_to(compact[:, None, :], (experts, images, columns))
    return wide.reshape(experts * images, columns)


def fold_rows(block, images):
    rows, columns = block.shape
    return jnp.sum(block.reshape(rows // images, images, columns), axis=1)


def pair_rows(first, second, groups):
    images = first.shape[0] // groups
    first = first.reshape(groups, images, first.shape[1])
    second = second.reshape(groups, images, second.shape[1])
    return jnp.concatenate((first, second), axis=1).astype(BF16)


def split_rows(pairs):
    groups, both, width = pairs.shape
    wide = pairs.astype(F32)
    first = wide[:, : both // 2].reshape(groups * both // 2, width)
    second = wide[:, both // 2 :].reshape(groups * both // 2, width)
    return first.astype(BF16), second.astype(BF16)


def softmaxes(router, tokens, images):
    logits = dot(router, tokens, 1, 1)
    experts, columns = logits.shape
    mask = own_image(experts, images, columns)
    combine = jnp.exp(logits - jnp.max(logits, axis=0, keepdims=True))
    combine = combine / jnp.sum(combine, axis=0, keepdims=True)
    block = jnp.where(mask, spread_rows(logits, images), -jnp.inf)
    block = jnp.exp(block - jnp.max(block, axis=1, keepdims=True))
    block = block / jnp.sum(block, axis=1, keepdims=True)
    return block, combine, mask


def slots_kernel(images, tokens_hbm, router_hbm, grad_hbm, sent_ref, *scratch):
    tokens_ref, router_ref, grad_ref, sems = scratch
    pieces = sems.shape[1]
    rows = tokens_ref.shape[0] // pieces

    def loads(which, source, target):
        parts = (pl.ds(i * rows, rows) for i in range(pieces))
        return [
            pltpu.make_async_copy(source.at[part], target.at[part], sems.at[which, i])
            for i, part in enumerate(parts)
        ]

    first = loads(0, tokens_hbm, tokens_ref)
    first.append(pltpu.make_async_copy(router_hbm, router_ref, sems.at[2, 0]))
    second = loads(1, grad_hbm, grad_ref)
    for load in first + second:
        load.start()
    for load in first:
        load.wait()
    tokens = tokens_ref[...]
    block, combine, mask = softmaxes(router_ref[...], tokens, images)
    combine_block = jnp.where(mask, spread_rows(combine, images), 0.0)
    slot_in = dot(block.astype(BF16), tokens, 1, 0)
    for load in second:
        load.wait()
    slot_grad = dot(combine_block.astype(BF16), grad_ref[...], 1, 0)
    sent_ref[...] = pair_rows(slot_in, slot_grad, combine.shape[0])


def stage_kernel(win_hbm, wout_hbm, win_ref, wout_ref, sems):
    loads = (
        pltpu.make_async_copy(win_hbm, win_ref, sems.at[0]),
        pltpu.make_async_copy(wout_hbm, wout_ref, sems.at[1]),
    )
    for load in loads:
        load.start()
    for load in loads:
        load.wait()


def expert_kernel(recv_ref, win_ref, wout_ref, back_ref, *, step):
    slots, cotan = split_rows(recv_ref[...])
    out = jnp.zeros(slots.shape, F32)
    back = jnp.zeros(slots.shape, F32)
    for start in range(0, win_ref.shape[1], step):
        w_in = win_ref[:, start : start + step]
        w_out = wout_ref[:, start : start + step]
        value, slope = gelu_pair(dot(slots, w_in, 1, 0))
        pre_grad = dot(cotan, w_out, 1, 0) * slope
        out = out + dot(value.astype(BF16), w_out, 1, 1)
        back = back + dot(pre_grad.astype(BF16), w_in, 1, 1)
    back_ref[...] = pair_rows(out, back, recv_ref.shape[0])


def logits_kernel(
    images, back_hbm, tokens_ref, router_ref, grad_ref, send_ref, logit_ref, back_ref, sem
):
    load = pltpu.make_async_copy(back_hbm, back_ref, sem)
    load.start()
    tokens = tokens_ref[...]
    dispatch, combine, mask = softmaxes(router_ref[...], tokens, images)
    load.wait()
    slot_out, slot_in_grad = split_rows(back_ref[...])
    disp = jnp.where(mask, dot(slot_in_grad, tokens, 1, 1), 0.0)
    comb = fold_rows(jnp.where(mask, dot(slot_out, grad_ref[...], 1, 1), 0.0), images)
    mean = jnp.sum(dispatch * disp, axis=1, keepdims=True)
    from_dispatch = fold_rows(dispatch * (disp - mean), images)
    from_combine = combine * (comb - jnp.sum(combine * comb, axis=0, keepdims=True))
    logit_grad = (from_combine + from_dispatch).astype(BF16)
    logit_ref[...] = logit_grad
    part = dot(logit_grad, tokens, 1, 0)
    owners, shares, _, width = send_ref.shape
    for share in range(shares):
        piece = part[:, share * width : (share + 1) * width]
        for owner in range(owners):
            send_ref[owner, share] = piece


def tokens_kernel(images, back_ref, tokens_ref, router_ref, logit_ref, out_ref):
    router = router_ref[...]
    dispatch, _, _ = softmaxes(router, tokens_ref[...], images)
    _, slot_in_grad = split_rows(back_ref[...])
    out = dot(dispatch.astype(BF16), slot_in_grad, 0, 0)
    out = out + dot(logit_ref[...], router, 0, 0)
    out_ref[...] = out.astype(BF16)


def weights_kernel(share_ref, spread_ref, win_ref, wout_ref, win_out, wout_out, *, step):
    width = spread_ref.shape[-1]
    row_count = win_out.shape[0]
    slots, cotan = split_rows(spread_ref[...].reshape((-1,) + spread_ref.shape[2:]))
    shape = (row_count, width)
    row = lax.broadcasted_iota(jnp.int32, shape, 0) + share_ref[0] * row_count
    pick = jnp.where(lax.broadcasted_iota(jnp.int32, shape, 1) == row, 1.0, 0.0).astype(BF16)
    own_slots = dot(pick, slots, 1, 1).astype(BF16)
    own_cotan = dot(pick, cotan, 1, 1).astype(BF16)

    @pl.when(pl.program_id(0) == 0)
    def _():
        win_out[...] = jnp.zeros_like(win_out)
        wout_out[...] = jnp.zeros_like(wout_out)

    for start in range(0, win_ref.shape[1], step):
        part = slice(start, start + step)
        value, slope = gelu_pair(dot(slots, win_ref[:, part], 1, 0))
        pre_grad = dot(cotan, wout_ref[:, part], 1, 0) * slope
        win_out[:, part] += dot(own_slots, pre_grad.astype(BF16), 1, 0)
        wout_out[:, part] += dot(own_cotan, value.astype(BF16), 1, 0)


def on_device(tokens, router, w_in, w_out, out_grad):
    owners, shares = lax.axis_size("expert"), lax.axis_size("dp")
    images, per_image, width = tokens.shape
    experts = router.shape[1]
    hidden = w_in.shape[2]
    columns = images * per_image
    row_count = width // shares
    tokens2 = tokens.reshape(columns, width)
    grad2 = out_grad.reshape(columns, width)
    router_rows = router.T
    w_in2, w_out2 = w_in.reshape(width, hidden), w_out.reshape(width, hidden)
    params = pltpu.CompilerParams(vmem_limit_bytes=VMEM_BYTES)
    whole = pltpu.CompilerParams(vmem_limit_bytes=WHOLE_BYTES)

    def struct(shape, dtype):
        return jax.ShapeDtypeStruct(shape, dtype)

    in_place = pl.BlockSpec(memory_space=pl.ANY)
    sent = pl.pallas_call(
        functools.partial(slots_kernel, images),
        in_specs=[in_place] * 3,
        out_shape=struct((experts, 2 * images, width), BF16),
        scratch_shapes=[
            pltpu.VMEM((columns, width), BF16),
            pltpu.VMEM((experts, width), BF16),
            pltpu.VMEM((columns, width), BF16),
            pltpu.SemaphoreType.DMA((3, 4)),
        ],
        compiler_params=whole,
        name="slots",
    )(tokens2, router_rows, grad2)
    w_in2, w_out2 = pl.pallas_call(
        stage_kernel,
        in_specs=[in_place] * 2,
        out_specs=[in_place] * 2,
        out_shape=[struct((width, hidden), BF16)] * 2,
        scratch_shapes=[pltpu.SemaphoreType.DMA((2,))],
        compiler_params=pltpu.CompilerParams(vmem_limit_bytes=1024 * 1024),
        cost_estimate=pl.CostEstimate(
            flops=0, bytes_accessed=8 * width * hidden, transcendentals=0
        ),
        name="stage",
    )(w_in2, w_out2)
    recv = lax.all_to_all(sent, "expert", split_axis=0, concat_axis=0, tiled=True)
    back = pl.pallas_call(
        functools.partial(expert_kernel, step=512),
        out_shape=struct(recv.shape, BF16),
        compiler_params=params,
        name="expert",
    )(recv, w_in2, w_out2)
    recv, back = lax.optimization_barrier((recv, back))
    slots_back = lax.all_to_all(back, "expert", split_axis=0, concat_axis=0, tiled=True)
    spread = lax.all_gather(recv, "dp", axis=0, tiled=False)

    in_vmem = pl.BlockSpec(memory_space=pltpu.VMEM)
    router_send, logit_grad = pl.pallas_call(
        functools.partial(logits_kernel, images),
        in_specs=[in_place] + [in_vmem] * 3,
        out_shape=(
            struct((owners, shares, experts, row_count), F32),
            struct((experts, columns), BF16),
        ),
        scratch_shapes=[pltpu.VMEM(back.shape, BF16), pltpu.SemaphoreType.DMA],
        compiler_params=params,
        name="logits",
    )(slots_back, tokens2, router_rows, grad2)
    spread, router_send = lax.optimization_barrier((spread, router_send))
    router_parts = lax.all_to_all(
        router_send.reshape(owners * shares, experts, row_count),
        ("expert", "dp"),
        split_axis=0,
        concat_axis=0,
        tiled=True,
    )

    tokens_grad = pl.pallas_call(
        functools.partial(tokens_kernel, images),
        out_shape=struct((columns, width), BF16),
        compiler_params=params,
        name="tokens",
    )(slots_back, tokens2, router_rows, logit_grad)
    group = max(1, min(shares, 256 // (owners * images)))
    w_in_grad, w_out_grad = pl.pallas_call(
        functools.partial(weights_kernel, step=512),
        grid=(shares // group,),
        in_specs=[
            pl.BlockSpec(memory_space=pltpu.SMEM),
            pl.BlockSpec((group,) + recv.shape, lambda i: (i, 0, 0, 0)),
            pl.BlockSpec((width, hidden), lambda i: (0, 0)),
            pl.BlockSpec((width, hidden), lambda i: (0, 0)),
        ],
        out_specs=[pl.BlockSpec((row_count, hidden), lambda i: (0, 0))] * 2,
        out_shape=[struct((row_count, hidden), F32)] * 2,
        compiler_params=params,
        name="weights",
    )(lax.axis_index("dp").reshape(1), spread, w_in2, w_out2)
    router_grad = jnp.sum(router_parts, axis=0).T
    return (
        tokens_grad.reshape(tokens.shape),
        w_in_grad.reshape(1, row_count, hidden),
        w_out_grad.reshape(1, row_count, hidden),
        router_grad,
    )


def solution(mesh):
    placed = (
        P(("expert", "dp"), None, None),
        P(),
        P("expert", None, None),
        P("expert", None, None),
        P(("expert", "dp"), None, None),
    )
    return jax.shard_map(
        on_device,
        mesh=mesh,
        in_specs=placed,
        out_specs=(
            P(("expert", "dp"), None, None),
            P("expert", "dp", None),
            P("expert", "dp", None),
            P("dp", None),
        ),
        check_vma=False,
    )
```

```python
import functools
import math

import jax
import jax.numpy as jnp
from jax import lax
from jax.experimental import pallas as pl
from jax.experimental.pallas import tpu as pltpu
from jax.sharding import PartitionSpec as P

F32 = jnp.float32
BF16 = jnp.bfloat16
VMEM_BYTES = 24 * 1024 * 1024
WHOLE_BYTES = 56 * 1024 * 1024


def gelu_pair(value):
    coef = math.sqrt(2.0 / math.pi)
    square = value * value
    tangent = jnp.tanh(coef * value * (1.0 + 0.044715 * square))
    half = 0.5 * (1.0 + tangent)
    slope = half + 0.5 * coef * value * (1.0 - tangent * tangent) * (1.0 + 3.0 * 0.044715 * square)
    return value * half, slope


def dot(left, right, left_dim, right_dim):
    return lax.dot_general(
        left, right, (((left_dim,), (right_dim,)), ((), ())), preferred_element_type=F32
    )


def own_image(experts, images, columns):
    shape = (experts, images, columns)
    image = lax.broadcasted_iota(jnp.int32, shape, 1)
    token = lax.broadcasted_iota(jnp.int32, shape, 2)
    low = image * (columns // images)
    inside = (token >= low) & (token < low + columns // images)
    return inside.reshape(experts * images, columns)


def spread_rows(compact, images):
    experts, columns = compact.shape
    wide = jnp.broadcast_to(compact[:, None, :], (experts, images, columns))
    return wide.reshape(experts * images, columns)


def fold_rows(block, images):
    rows, columns = block.shape
    return jnp.sum(block.reshape(rows // images, images, columns), axis=1)


def pair_rows(first, second, groups):
    images = first.shape[0] // groups
    first = first.reshape(groups, images, first.shape[1])
    second = second.reshape(groups, images, second.shape[1])
    return jnp.concatenate((first, second), axis=1).astype(BF16)


def split_rows(pairs):
    groups, both, width = pairs.shape
    wide = pairs.astype(F32)
    first = wide[:, : both // 2].reshape(groups * both // 2, width)
    second = wide[:, both // 2 :].reshape(groups * both // 2, width)
    return first.astype(BF16), second.astype(BF16)


def softmaxes(router, tokens, images):
    logits = dot(router, tokens, 1, 1)
    experts, columns = logits.shape
    mask = own_image(experts, images, columns)
    combine = jnp.exp(logits - jnp.max(logits, axis=0, keepdims=True))
    combine = combine / jnp.sum(combine, axis=0, keepdims=True)
    block = jnp.where(mask, spread_rows(logits, images), -jnp.inf)
    block = jnp.exp(block - jnp.max(block, axis=1, keepdims=True))
    block = block / jnp.sum(block, axis=1, keepdims=True)
    return block, combine, mask


def slots_kernel(images, tokens_hbm, router_hbm, grad_hbm, sent_ref, *scratch):
    tokens_ref, router_ref, grad_ref, sems = scratch
    pieces = sems.shape[1]
    rows = tokens_ref.shape[0] // pieces

    def loads(which, source, target):
        parts = (pl.ds(i * rows, rows) for i in range(pieces))
        return [
            pltpu.make_async_copy(source.at[part], target.at[part], sems.at[which, i])
            for i, part in enumerate(parts)
        ]

    first = loads(0, tokens_hbm, tokens_ref)
    first.append(pltpu.make_async_copy(router_hbm, router_ref, sems.at[2, 0]))
    second = loads(1, grad_hbm, grad_ref)
    for load in first + second:
        load.start()
    for load in first:
        load.wait()
    tokens = tokens_ref[...]
    block, combine, mask = softmaxes(router_ref[...], tokens, images)
    combine_block = jnp.where(mask, spread_rows(combine, images), 0.0)
    slot_in = dot(block.astype(BF16), tokens, 1, 0)
    for load in second:
        load.wait()
    slot_grad = dot(combine_block.astype(BF16), grad_ref[...], 1, 0)
    sent_ref[...] = pair_rows(slot_in, slot_grad, combine.shape[0])


def stage_kernel(win_hbm, wout_hbm, win_ref, wout_ref, sems):
    loads = (
        pltpu.make_async_copy(win_hbm, win_ref, sems.at[0]),
        pltpu.make_async_copy(wout_hbm, wout_ref, sems.at[1]),
    )
    for load in loads:
        load.start()
    for load in loads:
        load.wait()


def expert_kernel(recv_ref, win_ref, wout_ref, back_ref, *, step):
    slots, cotan = split_rows(recv_ref[...])
    out = jnp.zeros(slots.shape, F32)
    back = jnp.zeros(slots.shape, F32)
    for start in range(0, win_ref.shape[1], step):
        w_in = win_ref[:, start : start + step]
        w_out = wout_ref[:, start : start + step]
        value, slope = gelu_pair(dot(slots, w_in, 1, 0))
        pre_grad = dot(cotan, w_out, 1, 0) * slope
        out = out + dot(value.astype(BF16), w_out, 1, 1)
        back = back + dot(pre_grad.astype(BF16), w_in, 1, 1)
    back_ref[...] = pair_rows(out, back, recv_ref.shape[0])


def logits_kernel(
    images, back_hbm, tokens_ref, router_ref, grad_ref, send_ref, logit_ref, back_ref, sem
):
    load = pltpu.make_async_copy(back_hbm, back_ref, sem)
    load.start()
    tokens = tokens_ref[...]
    dispatch, combine, mask = softmaxes(router_ref[...], tokens, images)
    load.wait()
    slot_out, slot_in_grad = split_rows(back_ref[...])
    disp = jnp.where(mask, dot(slot_in_grad, tokens, 1, 1), 0.0)
    comb = fold_rows(jnp.where(mask, dot(slot_out, grad_ref[...], 1, 1), 0.0), images)
    mean = jnp.sum(dispatch * disp, axis=1, keepdims=True)
    from_dispatch = fold_rows(dispatch * (disp - mean), images)
    from_combine = combine * (comb - jnp.sum(combine * comb, axis=0, keepdims=True))
    logit_grad = (from_combine + from_dispatch).astype(BF16)
    logit_ref[...] = logit_grad
    part = dot(logit_grad, tokens, 1, 0)
    owners, shares, _, width = send_ref.shape
    for share in range(shares):
        piece = part[:, share * width : (share + 1) * width].astype(BF16)
        for owner in range(owners):
            send_ref[owner, share] = piece


def tokens_kernel(images, back_ref, tokens_ref, router_ref, logit_ref, out_ref):
    router = router_ref[...]
    dispatch, _, _ = softmaxes(router, tokens_ref[...], images)
    _, slot_in_grad = split_rows(back_ref[...])
    out = dot(dispatch.astype(BF16), slot_in_grad, 0, 0)
    out = out + dot(logit_ref[...], router, 0, 0)
    out_ref[...] = out.astype(BF16)


def weights_kernel(share_ref, *refs, step):
    spread, (win_ref, wout_ref, win_out, wout_out) = refs[:-4], refs[-4:]
    row_count, width = win_out.shape[0], win_ref.shape[0]
    pairs = [split_rows(ref[...].reshape((-1,) + ref.shape[-2:])) for ref in spread]
    slots = jnp.concatenate([pair[0] for pair in pairs], axis=0)
    cotan = jnp.concatenate([pair[1] for pair in pairs], axis=0)
    shape = (row_count, width)
    row = lax.broadcasted_iota(jnp.int32, shape, 0) + share_ref[0] * row_count
    pick = jnp.where(lax.broadcasted_iota(jnp.int32, shape, 1) == row, 1.0, 0.0).astype(BF16)
    own_slots = dot(pick, slots, 1, 1).astype(BF16)
    own_cotan = dot(pick, cotan, 1, 1).astype(BF16)

    @pl.when(pl.program_id(0) == 0)
    def _():
        win_out[...] = jnp.zeros_like(win_out)
        wout_out[...] = jnp.zeros_like(wout_out)

    for start in range(0, win_ref.shape[1], step):
        part = slice(start, start + step)
        value, slope = gelu_pair(dot(slots, win_ref[:, part], 1, 0))
        pre_grad = dot(cotan, wout_ref[:, part], 1, 0) * slope
        win_out[:, part] += dot(own_slots, pre_grad.astype(BF16), 1, 0)
        wout_out[:, part] += dot(own_cotan, value.astype(BF16), 1, 0)


def on_device(tokens, router, w_in, w_out, out_grad):
    owners, shares = lax.axis_size("expert"), lax.axis_size("dp")
    images, per_image, width = tokens.shape
    experts = router.shape[1]
    hidden = w_in.shape[2]
    columns = images * per_image
    row_count = width // shares
    tokens2 = tokens.reshape(columns, width)
    grad2 = out_grad.reshape(columns, width)
    router_rows = router.T
    w_in2, w_out2 = w_in.reshape(width, hidden), w_out.reshape(width, hidden)
    params = pltpu.CompilerParams(vmem_limit_bytes=VMEM_BYTES)
    whole = pltpu.CompilerParams(vmem_limit_bytes=WHOLE_BYTES)

    def struct(shape, dtype):
        return jax.ShapeDtypeStruct(shape, dtype)

    in_place = pl.BlockSpec(memory_space=pl.ANY)
    sent = pl.pallas_call(
        functools.partial(slots_kernel, images),
        in_specs=[in_place] * 3,
        out_shape=struct((experts, 2 * images, width), BF16),
        scratch_shapes=[
            pltpu.VMEM((columns, width), BF16),
            pltpu.VMEM((experts, width), BF16),
            pltpu.VMEM((columns, width), BF16),
            pltpu.SemaphoreType.DMA((3, 4)),
        ],
        compiler_params=whole,
        name="slots",
    )(tokens2, router_rows, grad2)
    w_in2, w_out2 = pl.pallas_call(
        stage_kernel,
        in_specs=[in_place] * 2,
        out_specs=[in_place] * 2,
        out_shape=[struct((width, hidden), BF16)] * 2,
        scratch_shapes=[pltpu.SemaphoreType.DMA((2,))],
        compiler_params=pltpu.CompilerParams(vmem_limit_bytes=1024 * 1024),
        cost_estimate=pl.CostEstimate(
            flops=0, bytes_accessed=8 * width * hidden, transcendentals=0
        ),
        name="stage",
    )(w_in2, w_out2)
    recv = lax.all_to_all(sent, "expert", split_axis=0, concat_axis=0, tiled=True)
    back = pl.pallas_call(
        functools.partial(expert_kernel, step=512),
        out_shape=struct(recv.shape, BF16),
        compiler_params=params,
        name="expert",
    )(recv, w_in2, w_out2)
    recv, back = lax.optimization_barrier((recv, back))
    slots_back = lax.all_to_all(back, "expert", split_axis=0, concat_axis=0, tiled=True)
    few = shares * owners * images <= 512
    if few:
        spread = [recv] + [
            lax.ppermute(recv, "dp", [(i, i ^ k) for i in range(shares)])
            for k in range(1, shares)
        ]
    else:
        spread = [lax.all_gather(recv, "dp", axis=0, tiled=False)]

    in_vmem = pl.BlockSpec(memory_space=pltpu.VMEM)
    router_send, logit_grad = pl.pallas_call(
        functools.partial(logits_kernel, images),
        in_specs=[in_place] + [in_vmem] * 3,
        out_shape=(
            struct((owners, shares, experts, row_count), BF16),
            struct((experts, columns), BF16),
        ),
        scratch_shapes=[pltpu.VMEM(back.shape, BF16), pltpu.SemaphoreType.DMA],
        compiler_params=params,
        name="logits",
    )(slots_back, tokens2, router_rows, grad2)
    share, router_send = lax.optimization_barrier((lax.axis_index("dp").reshape(1), router_send))
    router_parts = lax.all_to_all(
        router_send.reshape(owners * shares, experts, row_count),
        ("expert", "dp"),
        split_axis=0,
        concat_axis=0,
        tiled=True,
    )

    tokens_grad = pl.pallas_call(
        functools.partial(tokens_kernel, images),
        out_shape=struct((columns, width), BF16),
        compiler_params=params,
        name="tokens",
    )(slots_back, tokens2, router_rows, logit_grad)
    if few:
        blocks = [pl.BlockSpec(recv.shape, lambda i: (0, 0, 0))] * shares
    else:
        blocks = [pl.BlockSpec((1,) + recv.shape, lambda i: (i, 0, 0, 0))]
    w_in_grad, w_out_grad = pl.pallas_call(
        functools.partial(weights_kernel, step=512),
        grid=(1 if few else shares,),
        in_specs=[
            pl.BlockSpec(memory_space=pltpu.SMEM),
            *blocks,
            pl.BlockSpec((width, hidden), lambda i: (0, 0)),
            pl.BlockSpec((width, hidden), lambda i: (0, 0)),
        ],
        out_specs=[pl.BlockSpec((row_count, hidden), lambda i: (0, 0))] * 2,
        out_shape=[struct((row_count, hidden), F32)] * 2,
        compiler_params=params,
        name="weights",
    )(share, *spread, w_in2, w_out2)
    router_grad = jnp.sum(router_parts.astype(F32), axis=0).T
    return (
        tokens_grad.reshape(tokens.shape),
        w_in_grad.reshape(1, row_count, hidden),
        w_out_grad.reshape(1, row_count, hidden),
        router_grad,
    )


def solution(mesh):
    placed = (
        P(("expert", "dp"), None, None),
        P(),
        P("expert", None, None),
        P("expert", None, None),
        P(("expert", "dp"), None, None),
    )
    return jax.shard_map(
        on_device,
        mesh=mesh,
        in_specs=placed,
        out_specs=(
            P(("expert", "dp"), None, None),
            P("expert", "dp", None),
            P("expert", "dp", None),
            P("dp", None),
        ),
        check_vma=False,
    )
```

```python
import functools
import math

import jax
import jax.numpy as jnp
from jax import lax
from jax.experimental import pallas as pl
from jax.experimental.pallas import tpu as pltpu
from jax.sharding import PartitionSpec as P

F32 = jnp.float32
BF16 = jnp.bfloat16
VMEM_BYTES = 24 * 1024 * 1024
WHOLE_BYTES = 56 * 1024 * 1024


def gelu_pair(value):
    coef = math.sqrt(2.0 / math.pi)
    cubic = 0.044715 * coef
    square = value * value
    half = 0.5 * jnp.tanh(value * (coef + cubic * square)) + 0.5
    steep = value * (2.0 * coef + 6.0 * cubic * square) * (1.0 - half)
    return value * half, half + half * steep


def dot(left, right, left_dim, right_dim):
    return lax.dot_general(
        left, right, (((left_dim,), (right_dim,)), ((), ())), preferred_element_type=F32
    )


def own_image(experts, images, columns):
    shape = (experts, images, columns)
    image = lax.broadcasted_iota(jnp.int32, shape, 1)
    token = lax.broadcasted_iota(jnp.int32, shape, 2)
    low = image * (columns // images)
    inside = (token >= low) & (token < low + columns // images)
    return inside.reshape(experts * images, columns)


def spread_rows(compact, images):
    experts, columns = compact.shape
    wide = jnp.broadcast_to(compact[:, None, :], (experts, images, columns))
    return wide.reshape(experts * images, columns)


def fold_rows(block, images):
    rows, columns = block.shape
    return jnp.sum(block.reshape(rows // images, images, columns), axis=1)


def pair_rows(first, second, groups):
    images = first.shape[0] // groups
    first = first.reshape(groups, images, first.shape[1])
    second = second.reshape(groups, images, second.shape[1])
    return jnp.concatenate((first, second), axis=1).astype(BF16)


def split_rows(pairs):
    groups, both, width = pairs.shape
    wide = pairs.astype(F32)
    first = wide[:, : both // 2].reshape(groups * both // 2, width)
    second = wide[:, both // 2 :].reshape(groups * both // 2, width)
    return first.astype(BF16), second.astype(BF16)


def softmaxes(router, tokens, images):
    logits = dot(router, tokens, 1, 1)
    experts, columns = logits.shape
    mask = own_image(experts, images, columns)
    combine = jnp.exp(logits - jnp.max(logits, axis=0, keepdims=True))
    combine = combine / jnp.sum(combine, axis=0, keepdims=True)
    block = jnp.where(mask, spread_rows(logits, images), -jnp.inf)
    block = jnp.exp(block - jnp.max(block, axis=1, keepdims=True))
    block = block / jnp.sum(block, axis=1, keepdims=True)
    return block, combine, mask


def slots_kernel(images, tokens_hbm, router_hbm, grad_hbm, sent_ref, *scratch):
    tokens_ref, router_ref, grad_ref, sems = scratch
    first = [
        pltpu.make_async_copy(tokens_hbm, tokens_ref, sems.at[0]),
        pltpu.make_async_copy(router_hbm, router_ref, sems.at[1]),
    ]
    second = [pltpu.make_async_copy(grad_hbm, grad_ref, sems.at[2])]
    for load in first + second:
        load.start()
    for load in first:
        load.wait()
    tokens = tokens_ref[...]
    block, combine, mask = softmaxes(router_ref[...], tokens, images)
    combine_block = jnp.where(mask, spread_rows(combine, images), 0.0)
    slot_in = dot(block.astype(BF16), tokens, 1, 0)
    for load in second:
        load.wait()
    slot_grad = dot(combine_block.astype(BF16), grad_ref[...], 1, 0)
    sent_ref[...] = pair_rows(slot_in, slot_grad, combine.shape[0])


def stage_kernel(win_hbm, wout_hbm, win_ref, wout_ref, sems):
    loads = (
        pltpu.make_async_copy(win_hbm, win_ref, sems.at[0]),
        pltpu.make_async_copy(wout_hbm, wout_ref, sems.at[1]),
    )
    for load in loads:
        load.start()
    for load in loads:
        load.wait()


def expert_kernel(recv_ref, win_ref, wout_ref, back_ref, *, step):
    slots, cotan = split_rows(recv_ref[...])
    out = jnp.zeros(slots.shape, F32)
    back = jnp.zeros(slots.shape, F32)
    for start in range(0, win_ref.shape[1], step):
        w_in = win_ref[:, start : start + step]
        w_out = wout_ref[:, start : start + step]
        value, slope = gelu_pair(dot(slots, w_in, 1, 0))
        pre_grad = dot(cotan, w_out, 1, 0) * slope
        out = out + dot(value.astype(BF16), w_out, 1, 1)
        back = back + dot(pre_grad.astype(BF16), w_in, 1, 1)
    back_ref[...] = pair_rows(out, back, recv_ref.shape[0])


def logits_kernel(
    images, back_hbm, tokens_ref, router_ref, grad_ref, send_ref, logit_ref, back_ref, sem
):
    load = pltpu.make_async_copy(back_hbm, back_ref, sem)
    load.start()
    tokens = tokens_ref[...]
    dispatch, combine, mask = softmaxes(router_ref[...], tokens, images)
    load.wait()
    slot_out, slot_in_grad = split_rows(back_ref[...])
    disp = jnp.where(mask, dot(slot_in_grad, tokens, 1, 1), 0.0)
    comb = fold_rows(jnp.where(mask, dot(slot_out, grad_ref[...], 1, 1), 0.0), images)
    mean = jnp.sum(dispatch * disp, axis=1, keepdims=True)
    from_dispatch = fold_rows(dispatch * (disp - mean), images)
    from_combine = combine * (comb - jnp.sum(combine * comb, axis=0, keepdims=True))
    logit_grad = (from_combine + from_dispatch).astype(BF16)
    logit_ref[...] = logit_grad
    part = dot(logit_grad, tokens, 1, 0)
    devices, _, width = send_ref.shape
    shares = part.shape[1] // width
    for share in range(shares):
        piece = part[:, share * width : (share + 1) * width].astype(BF16)
        for device in range(share, devices, shares):
            send_ref[device] = piece


def tokens_kernel(images, back_ref, tokens_ref, router_ref, logit_ref, out_ref):
    router = router_ref[...]
    dispatch, _, _ = softmaxes(router, tokens_ref[...], images)
    _, slot_in_grad = split_rows(back_ref[...])
    out = dot(dispatch.astype(BF16), slot_in_grad, 0, 0)
    out = out + dot(logit_ref[...], router, 0, 0)
    out_ref[...] = out.astype(BF16)


def own_rows(share, rows, row_count):
    shape = (row_count, rows.shape[1])
    row = lax.broadcasted_iota(jnp.int32, shape, 0) + share * row_count
    pick = jnp.where(lax.broadcasted_iota(jnp.int32, shape, 1) == row, 1.0, 0.0)
    return dot(pick.astype(BF16), rows, 1, 1).astype(BF16)


def weights_kernel(count, share_ref, *refs):
    spread, (win_ref, wout_ref, win_hbm, wout_hbm) = refs[:count], refs[count : count + 4]
    rows_ref, win_out, wout_out, load_sems, store_sems = refs[count + 4 :]
    chunks, row_count, step = win_out.shape
    loads = [
        pltpu.make_async_copy(ref, rows_ref.at[k], load_sems.at[k])
        for k, ref in enumerate(spread)
    ]
    for load in loads:
        load.start()
    for load in loads:
        load.wait()
    slots, cotan = split_rows(rows_ref[...].reshape((-1,) + rows_ref.shape[2:]))
    own_slots = own_rows(share_ref[0], slots, row_count)
    own_cotan = own_rows(share_ref[0], cotan, row_count)
    stores = []
    for chunk in range(chunks):
        part = slice(chunk * step, (chunk + 1) * step)
        value, slope = gelu_pair(dot(slots, win_ref[:, part], 1, 0))
        pre_grad = dot(cotan, wout_ref[:, part], 1, 0) * slope
        win_out[chunk] = dot(own_slots, pre_grad.astype(BF16), 1, 0)
        wout_out[chunk] = dot(own_cotan, value.astype(BF16), 1, 0)
        where = (slice(None), pl.ds(chunk * step, step))
        for which, (source, target) in enumerate(((win_out, win_hbm), (wout_out, wout_hbm))):
            store = pltpu.make_async_copy(
                source.at[chunk], target.at[where], store_sems.at[which, chunk]
            )
            store.start()
            stores.append(store)
    for store in stores:
        store.wait()


def long_weights_kernel(share_ref, spread_ref, win_ref, wout_ref, win_out, wout_out, *, step):
    slots, cotan = split_rows(spread_ref[...].reshape((-1,) + spread_ref.shape[2:]))
    own_slots = own_rows(share_ref[0], slots, win_out.shape[0])
    own_cotan = own_rows(share_ref[0], cotan, win_out.shape[0])

    @pl.when(pl.program_id(0) == 0)
    def _():
        win_out[...] = jnp.zeros_like(win_out)
        wout_out[...] = jnp.zeros_like(wout_out)

    for start in range(0, win_ref.shape[1], step):
        part = slice(start, start + step)
        value, slope = gelu_pair(dot(slots, win_ref[:, part], 1, 0))
        pre_grad = dot(cotan, wout_ref[:, part], 1, 0) * slope
        win_out[:, part] += dot(own_slots, pre_grad.astype(BF16), 1, 0)
        wout_out[:, part] += dot(own_cotan, value.astype(BF16), 1, 0)


def on_device(tokens, router, w_in, w_out, out_grad):
    owners, shares = lax.axis_size("expert"), lax.axis_size("dp")
    images, per_image, width = tokens.shape
    experts = router.shape[1]
    hidden = w_in.shape[2]
    columns = images * per_image
    row_count = width // shares
    tokens2 = tokens.reshape(columns, width)
    grad2 = out_grad.reshape(columns, width)
    router_rows = router.T
    w_in2, w_out2 = w_in.reshape(width, hidden), w_out.reshape(width, hidden)
    params = pltpu.CompilerParams(vmem_limit_bytes=VMEM_BYTES)
    whole = pltpu.CompilerParams(vmem_limit_bytes=WHOLE_BYTES)

    def struct(shape, dtype):
        return jax.ShapeDtypeStruct(shape, dtype)

    in_place = pl.BlockSpec(memory_space=pl.ANY)
    sent = pl.pallas_call(
        functools.partial(slots_kernel, images),
        in_specs=[in_place] * 3,
        out_shape=struct((experts, 2 * images, width), BF16),
        scratch_shapes=[
            pltpu.VMEM((columns, width), BF16),
            pltpu.VMEM((experts, width), BF16),
            pltpu.VMEM((columns, width), BF16),
            pltpu.SemaphoreType.DMA((3,)),
        ],
        compiler_params=whole,
        name="slots",
    )(tokens2, router_rows, grad2)
    w_in2, w_out2 = pl.pallas_call(
        stage_kernel,
        in_specs=[in_place] * 2,
        out_specs=[in_place] * 2,
        out_shape=[struct((width, hidden), BF16)] * 2,
        scratch_shapes=[pltpu.SemaphoreType.DMA((2,))],
        compiler_params=pltpu.CompilerParams(vmem_limit_bytes=1024 * 1024),
        cost_estimate=pl.CostEstimate(
            flops=0, bytes_accessed=8 * width * hidden, transcendentals=0
        ),
        name="stage",
    )(w_in2, w_out2)
    recv = lax.all_to_all(sent, "expert", split_axis=0, concat_axis=0, tiled=True)
    back = pl.pallas_call(
        functools.partial(expert_kernel, step=512),
        out_shape=struct(recv.shape, BF16),
        compiler_params=params,
        name="expert",
    )(recv, w_in2, w_out2)
    recv, back = lax.optimization_barrier((recv, back))
    slots_back = lax.all_to_all(back, "expert", split_axis=0, concat_axis=0, tiled=True)
    few = shares * owners * images <= 512
    if few:
        spread = [recv] + [
            lax.ppermute(recv, "dp", [(i, i ^ k) for i in range(shares)])
            for k in range(1, shares)
        ]
    else:
        spread = [lax.all_gather(recv, "dp", axis=0, tiled=False)]

    in_vmem = pl.BlockSpec(memory_space=pltpu.VMEM)
    router_send, logit_grad = pl.pallas_call(
        functools.partial(logits_kernel, images),
        in_specs=[in_place] + [in_vmem] * 3,
        out_shape=(
            struct((owners * shares, experts, row_count), BF16),
            struct((experts, columns), BF16),
        ),
        scratch_shapes=[pltpu.VMEM(back.shape, BF16), pltpu.SemaphoreType.DMA],
        compiler_params=params,
        name="logits",
    )(slots_back, tokens2, router_rows, grad2)
    share, router_send = lax.optimization_barrier((lax.axis_index("dp").reshape(1), router_send))
    router_parts = lax.all_to_all(
        router_send,
        ("expert", "dp"),
        split_axis=0,
        concat_axis=0,
        tiled=True,
    )

    tokens_grad = pl.pallas_call(
        functools.partial(tokens_kernel, images),
        out_shape=struct((columns, width), BF16),
        compiler_params=params,
        name="tokens",
    )(slots_back, tokens2, router_rows, logit_grad)
    in_smem = pl.BlockSpec(memory_space=pltpu.SMEM)
    out_shape = [struct((row_count, hidden), F32)] * 2
    if few:
        chunks, step = hidden // 512, 512
        w_in_grad, w_out_grad = pl.pallas_call(
            functools.partial(weights_kernel, shares),
            in_specs=[in_smem] + [in_place] * shares + [in_vmem] * 2,
            out_specs=[in_place] * 2,
            out_shape=out_shape,
            scratch_shapes=[
                pltpu.VMEM((shares,) + recv.shape, BF16),
                pltpu.VMEM((chunks, row_count, step), F32),
                pltpu.VMEM((chunks, row_count, step), F32),
                pltpu.SemaphoreType.DMA((shares,)),
                pltpu.SemaphoreType.DMA((2, chunks)),
            ],
            compiler_params=params,
            name="weights",
        )(share, *spread, w_in2, w_out2)
    else:
        w_in_grad, w_out_grad = pl.pallas_call(
            functools.partial(long_weights_kernel, step=512),
            grid=(shares,),
            in_specs=[
                in_smem,
                pl.BlockSpec((1,) + recv.shape, lambda i: (i, 0, 0, 0)),
                pl.BlockSpec((width, hidden), lambda i: (0, 0)),
                pl.BlockSpec((width, hidden), lambda i: (0, 0)),
            ],
            out_specs=[pl.BlockSpec((row_count, hidden), lambda i: (0, 0))] * 2,
            out_shape=out_shape,
            compiler_params=params,
            name="weights",
        )(share, *spread, w_in2, w_out2)
    router_grad = jnp.sum(router_parts.astype(F32), axis=0).T
    return (
        tokens_grad.reshape(tokens.shape),
        w_in_grad.reshape(1, row_count, hidden),
        w_out_grad.reshape(1, row_count, hidden),
        router_grad,
    )


def solution(mesh):
    placed = (
        P(("expert", "dp"), None, None),
        P(),
        P("expert", None, None),
        P("expert", None, None),
        P(("expert", "dp"), None, None),
    )
    return jax.shard_map(
        on_device,
        mesh=mesh,
        in_specs=placed,
        out_specs=(
            P(("expert", "dp"), None, None),
            P("expert", "dp", None),
            P("expert", "dp", None),
            P("dp", None),
        ),
        check_vma=False,
    )
```

```python
import functools
import math

import jax
import jax.numpy as jnp
from jax import lax
from jax.experimental import pallas as pl
from jax.experimental.pallas import tpu as pltpu
from jax.sharding import PartitionSpec as P

F32 = jnp.float32
BF16 = jnp.bfloat16
VMEM_BYTES = 24 * 1024 * 1024
WHOLE_BYTES = 56 * 1024 * 1024


def gelu_pair(value):
    coef = math.sqrt(2.0 / math.pi)
    cubic = 0.044715 * coef
    square = value * value
    half = 0.5 * jnp.tanh(value * (coef + cubic * square)) + 0.5
    steep = value * (2.0 * coef + 6.0 * cubic * square) * (1.0 - half)
    return value * half, half + half * steep


def dot(left, right, left_dim, right_dim):
    return lax.dot_general(
        left, right, (((left_dim,), (right_dim,)), ((), ())), preferred_element_type=F32
    )


def own_image(experts, images, columns):
    shape = (experts, images, columns)
    image = lax.broadcasted_iota(jnp.int32, shape, 1)
    token = lax.broadcasted_iota(jnp.int32, shape, 2)
    low = image * (columns // images)
    inside = (token >= low) & (token < low + columns // images)
    return inside.reshape(experts * images, columns)


def spread_rows(compact, images):
    experts, columns = compact.shape
    wide = jnp.broadcast_to(compact[:, None, :], (experts, images, columns))
    return wide.reshape(experts * images, columns)


def fold_rows(block, images):
    rows, columns = block.shape
    return jnp.sum(block.reshape(rows // images, images, columns), axis=1)


def pair_rows(first, second, groups):
    images = first.shape[0] // groups
    first = first.reshape(groups, images, first.shape[1])
    second = second.reshape(groups, images, second.shape[1])
    return jnp.concatenate((first, second), axis=1).astype(BF16)


def split_rows(pairs):
    groups, both, width = pairs.shape
    wide = pairs.astype(F32)
    first = wide[:, : both // 2].reshape(groups * both // 2, width)
    second = wide[:, both // 2 :].reshape(groups * both // 2, width)
    return first.astype(BF16), second.astype(BF16)


def softmaxes(router, tokens, images):
    logits = dot(router, tokens, 1, 1)
    experts, columns = logits.shape
    mask = own_image(experts, images, columns)
    combine = jnp.exp(logits - jnp.max(logits, axis=0, keepdims=True))
    combine = combine / jnp.sum(combine, axis=0, keepdims=True)
    block = jnp.where(mask, spread_rows(logits, images), -jnp.inf)
    block = jnp.exp(block - jnp.max(block, axis=1, keepdims=True))
    block = block / jnp.sum(block, axis=1, keepdims=True)
    return block, combine, mask


def slots_kernel(images, tokens_hbm, router_hbm, grad_hbm, sent_ref, *scratch):
    tokens_ref, router_ref, grad_ref, sems = scratch
    first = [
        pltpu.make_async_copy(tokens_hbm, tokens_ref, sems.at[0]),
        pltpu.make_async_copy(router_hbm, router_ref, sems.at[1]),
    ]
    second = [pltpu.make_async_copy(grad_hbm, grad_ref, sems.at[2])]
    for load in first + second:
        load.start()
    for load in first:
        load.wait()
    tokens = tokens_ref[...]
    block, combine, mask = softmaxes(router_ref[...], tokens, images)
    combine_block = jnp.where(mask, spread_rows(combine, images), 0.0)
    slot_in = dot(block.astype(BF16), tokens, 1, 0)
    for load in second:
        load.wait()
    slot_grad = dot(combine_block.astype(BF16), grad_ref[...], 1, 0)
    sent_ref[...] = pair_rows(slot_in, slot_grad, combine.shape[0])


def stage_kernel(win_hbm, wout_hbm, win_ref, wout_ref, sems):
    loads = (
        pltpu.make_async_copy(win_hbm, win_ref, sems.at[0]),
        pltpu.make_async_copy(wout_hbm, wout_ref, sems.at[1]),
    )
    for load in loads:
        load.start()
    for load in loads:
        load.wait()


def expert_kernel(recv_ref, win_ref, wout_ref, back_ref, *, step):
    slots, cotan = split_rows(recv_ref[...])
    out = jnp.zeros(slots.shape, F32)
    back = jnp.zeros(slots.shape, F32)
    for start in range(0, win_ref.shape[1], step):
        w_in = win_ref[:, start : start + step]
        w_out = wout_ref[:, start : start + step]
        value, slope = gelu_pair(dot(slots, w_in, 1, 0))
        pre_grad = dot(cotan, w_out, 1, 0) * slope
        out = out + dot(value.astype(BF16), w_out, 1, 1)
        back = back + dot(pre_grad.astype(BF16), w_in, 1, 1)
    back_ref[...] = pair_rows(out, back, recv_ref.shape[0])


def logits_grad(router, tokens, grad, images, read_back):
    dispatch, combine, mask = softmaxes(router, tokens, images)
    slot_out, slot_in_grad = split_rows(read_back())
    disp = jnp.where(mask, dot(slot_in_grad, tokens, 1, 1), 0.0)
    comb = fold_rows(jnp.where(mask, dot(slot_out, grad, 1, 1), 0.0), images)
    mean = jnp.sum(dispatch * disp, axis=1, keepdims=True)
    from_dispatch = fold_rows(dispatch * (disp - mean), images)
    from_combine = combine * (comb - jnp.sum(combine * comb, axis=0, keepdims=True))
    return (from_combine + from_dispatch).astype(BF16), dispatch, slot_in_grad


def logits_kernel(
    images, back_hbm, tokens_ref, router_ref, grad_ref, send_ref, back_ref, sem
):
    load = pltpu.make_async_copy(back_hbm, back_ref, sem)
    load.start()

    def read_back():
        load.wait()
        return back_ref[...]

    tokens = tokens_ref[...]
    logit_grad, _, _ = logits_grad(router_ref[...], tokens, grad_ref[...], images, read_back)
    part = dot(logit_grad, tokens, 1, 0)
    devices, _, width = send_ref.shape
    shares = part.shape[1] // width
    for share in range(shares):
        piece = part[:, share * width : (share + 1) * width].astype(BF16)
        for device in range(share, devices, shares):
            send_ref[device] = piece


def tokens_kernel(images, back_ref, tokens_ref, router_ref, grad_ref, out_ref):
    router = router_ref[...]
    logit_grad, dispatch, slot_in_grad = logits_grad(
        router, tokens_ref[...], grad_ref[...], images, lambda: back_ref[...]
    )
    out = dot(dispatch.astype(BF16), slot_in_grad, 0, 0)
    out = out + dot(logit_grad, router, 0, 0)
    out_ref[...] = out.astype(BF16)


def own_rows(share, rows, row_count):
    shape = (row_count, rows.shape[1])
    row = lax.broadcasted_iota(jnp.int32, shape, 0) + share * row_count
    pick = jnp.where(lax.broadcasted_iota(jnp.int32, shape, 1) == row, 1.0, 0.0)
    return dot(pick.astype(BF16), rows, 1, 1).astype(BF16)


def weights_kernel(count, share_ref, *refs):
    spread, (win_ref, wout_ref, win_hbm, wout_hbm) = refs[:count], refs[count : count + 4]
    rows_ref, win_out, wout_out, load_sems, store_sems = refs[count + 4 :]
    chunks, row_count, step = win_out.shape
    loads = [
        pltpu.make_async_copy(ref, rows_ref.at[k], load_sems.at[k])
        for k, ref in enumerate(spread)
    ]
    for load in loads:
        load.start()
    for load in loads:
        load.wait()
    slots, cotan = split_rows(rows_ref[...].reshape((-1,) + rows_ref.shape[2:]))
    own_slots = own_rows(share_ref[0], slots, row_count)
    own_cotan = own_rows(share_ref[0], cotan, row_count)
    stores = []
    for chunk in range(chunks):
        part = slice(chunk * step, (chunk + 1) * step)
        value, slope = gelu_pair(dot(slots, win_ref[:, part], 1, 0))
        pre_grad = dot(cotan, wout_ref[:, part], 1, 0) * slope
        win_out[chunk] = dot(own_slots, pre_grad.astype(BF16), 1, 0)
        wout_out[chunk] = dot(own_cotan, value.astype(BF16), 1, 0)
        where = (slice(None), pl.ds(chunk * step, step))
        for which, (source, target) in enumerate(((win_out, win_hbm), (wout_out, wout_hbm))):
            store = pltpu.make_async_copy(
                source.at[chunk], target.at[where], store_sems.at[which, chunk]
            )
            store.start()
            stores.append(store)
    for store in stores:
        store.wait()


def long_weights_kernel(share_ref, spread_ref, win_ref, wout_ref, win_out, wout_out, *, step):
    slots, cotan = split_rows(spread_ref[...].reshape((-1,) + spread_ref.shape[2:]))
    own_slots = own_rows(share_ref[0], slots, win_out.shape[0])
    own_cotan = own_rows(share_ref[0], cotan, win_out.shape[0])

    @pl.when(pl.program_id(0) == 0)
    def _():
        win_out[...] = jnp.zeros_like(win_out)
        wout_out[...] = jnp.zeros_like(wout_out)

    for start in range(0, win_ref.shape[1], step):
        part = slice(start, start + step)
        value, slope = gelu_pair(dot(slots, win_ref[:, part], 1, 0))
        pre_grad = dot(cotan, wout_ref[:, part], 1, 0) * slope
        win_out[:, part] += dot(own_slots, pre_grad.astype(BF16), 1, 0)
        wout_out[:, part] += dot(own_cotan, value.astype(BF16), 1, 0)


def on_device(tokens, router, w_in, w_out, out_grad):
    owners, shares = lax.axis_size("expert"), lax.axis_size("dp")
    images, per_image, width = tokens.shape
    experts = router.shape[1]
    hidden = w_in.shape[2]
    columns = images * per_image
    row_count = width // shares
    tokens2 = tokens.reshape(columns, width)
    grad2 = out_grad.reshape(columns, width)
    router_rows = router.T
    w_in2, w_out2 = w_in.reshape(width, hidden), w_out.reshape(width, hidden)
    params = pltpu.CompilerParams(vmem_limit_bytes=VMEM_BYTES)
    whole = pltpu.CompilerParams(vmem_limit_bytes=WHOLE_BYTES)

    def struct(shape, dtype):
        return jax.ShapeDtypeStruct(shape, dtype)

    in_place = pl.BlockSpec(memory_space=pl.ANY)
    sent = pl.pallas_call(
        functools.partial(slots_kernel, images),
        in_specs=[in_place] * 3,
        out_shape=struct((experts, 2 * images, width), BF16),
        scratch_shapes=[
            pltpu.VMEM((columns, width), BF16),
            pltpu.VMEM((experts, width), BF16),
            pltpu.VMEM((columns, width), BF16),
            pltpu.SemaphoreType.DMA((3,)),
        ],
        compiler_params=whole,
        name="slots",
    )(tokens2, router_rows, grad2)
    w_in2, w_out2 = pl.pallas_call(
        stage_kernel,
        in_specs=[in_place] * 2,
        out_specs=[in_place] * 2,
        out_shape=[struct((width, hidden), BF16)] * 2,
        scratch_shapes=[pltpu.SemaphoreType.DMA((2,))],
        compiler_params=pltpu.CompilerParams(vmem_limit_bytes=1024 * 1024),
        cost_estimate=pl.CostEstimate(
            flops=0, bytes_accessed=8 * width * hidden, transcendentals=0
        ),
        name="stage",
    )(w_in2, w_out2)
    recv = lax.all_to_all(sent, "expert", split_axis=0, concat_axis=0, tiled=True)
    back = pl.pallas_call(
        functools.partial(expert_kernel, step=512),
        out_shape=struct(recv.shape, BF16),
        compiler_params=params,
        name="expert",
    )(recv, w_in2, w_out2)
    recv, back = lax.optimization_barrier((recv, back))
    slots_back = lax.all_to_all(back, "expert", split_axis=0, concat_axis=0, tiled=True)
    few = shares * owners * images <= 512
    if few:
        spread = [recv] + [
            lax.ppermute(recv, "dp", [(i, i ^ k) for i in range(shares)])
            for k in range(1, shares)
        ]
    else:
        spread = [lax.all_gather(recv, "dp", axis=0, tiled=False)]

    in_vmem = pl.BlockSpec(memory_space=pltpu.VMEM)
    router_send = pl.pallas_call(
        functools.partial(logits_kernel, images),
        in_specs=[in_place] + [in_vmem] * 3,
        out_shape=struct((owners * shares, experts, row_count), BF16),
        scratch_shapes=[pltpu.VMEM(back.shape, BF16), pltpu.SemaphoreType.DMA],
        compiler_params=params,
        name="logits",
    )(slots_back, tokens2, router_rows, grad2)
    share, slots_back, router_send = lax.optimization_barrier(
        (lax.axis_index("dp").reshape(1), slots_back, router_send)
    )
    router_parts = lax.all_to_all(
        router_send,
        ("expert", "dp"),
        split_axis=0,
        concat_axis=0,
        tiled=True,
    )

    tokens_grad = pl.pallas_call(
        functools.partial(tokens_kernel, images),
        out_shape=struct((columns, width), BF16),
        compiler_params=params,
        name="tokens",
    )(slots_back, tokens2, router_rows, grad2)
    in_smem = pl.BlockSpec(memory_space=pltpu.SMEM)
    out_shape = [struct((row_count, hidden), F32)] * 2
    if few:
        chunks, step = hidden // 512, 512
        w_in_grad, w_out_grad = pl.pallas_call(
            functools.partial(weights_kernel, shares),
            in_specs=[in_smem] + [in_place] * shares + [in_vmem] * 2,
            out_specs=[in_place] * 2,
            out_shape=out_shape,
            scratch_shapes=[
                pltpu.VMEM((shares,) + recv.shape, BF16),
                pltpu.VMEM((chunks, row_count, step), F32),
                pltpu.VMEM((chunks, row_count, step), F32),
                pltpu.SemaphoreType.DMA((shares,)),
                pltpu.SemaphoreType.DMA((2, chunks)),
            ],
            compiler_params=params,
            name="weights",
        )(share, *spread, w_in2, w_out2)
    else:
        w_in_grad, w_out_grad = pl.pallas_call(
            functools.partial(long_weights_kernel, step=512),
            grid=(shares,),
            in_specs=[
                in_smem,
                pl.BlockSpec((1,) + recv.shape, lambda i: (i, 0, 0, 0)),
                pl.BlockSpec((width, hidden), lambda i: (0, 0)),
                pl.BlockSpec((width, hidden), lambda i: (0, 0)),
            ],
            out_specs=[pl.BlockSpec((row_count, hidden), lambda i: (0, 0))] * 2,
            out_shape=out_shape,
            compiler_params=params,
            name="weights",
        )(share, *spread, w_in2, w_out2)
    router_grad = jnp.sum(router_parts.astype(F32), axis=0).T
    return (
        tokens_grad.reshape(tokens.shape),
        w_in_grad.reshape(1, row_count, hidden),
        w_out_grad.reshape(1, row_count, hidden),
        router_grad,
    )


def solution(mesh):
    placed = (
        P(("expert", "dp"), None, None),
        P(),
        P("expert", None, None),
        P("expert", None, None),
        P(("expert", "dp"), None, None),
    )
    return jax.shard_map(
        on_device,
        mesh=mesh,
        in_specs=placed,
        out_specs=(
            P(("expert", "dp"), None, None),
            P("expert", "dp", None),
            P("expert", "dp", None),
            P("dp", None),
        ),
        check_vma=False,
    )
```

```python
import functools
import math

import jax
import jax.numpy as jnp
from jax import lax
from jax.experimental import pallas as pl
from jax.experimental.pallas import tpu as pltpu
from jax.sharding import PartitionSpec as P

F32 = jnp.float32
BF16 = jnp.bfloat16
VMEM_BYTES = 24 * 1024 * 1024
WHOLE_BYTES = 56 * 1024 * 1024


def gelu_pair(value):
    coef = math.sqrt(2.0 / math.pi)
    cubic = 0.044715 * coef
    square = value * value
    half = 0.5 * jnp.tanh(value * (coef + cubic * square)) + 0.5
    steep = value * (2.0 * coef + 6.0 * cubic * square) * (1.0 - half)
    return value * half, half + half * steep


def dot(left, right, left_dim, right_dim):
    return lax.dot_general(
        left, right, (((left_dim,), (right_dim,)), ((), ())), preferred_element_type=F32
    )


def own_image(experts, images, columns):
    shape = (experts, images, columns)
    image = lax.broadcasted_iota(jnp.int32, shape, 1)
    token = lax.broadcasted_iota(jnp.int32, shape, 2)
    low = image * (columns // images)
    inside = (token >= low) & (token < low + columns // images)
    return inside.reshape(experts * images, columns)


def spread_rows(compact, images):
    experts, columns = compact.shape
    wide = jnp.broadcast_to(compact[:, None, :], (experts, images, columns))
    return wide.reshape(experts * images, columns)


def fold_rows(block, images):
    rows, columns = block.shape
    return jnp.sum(block.reshape(rows // images, images, columns), axis=1)


def pair_rows(first, second, groups):
    images = first.shape[0] // groups
    first = first.reshape(groups, images, first.shape[1])
    second = second.reshape(groups, images, second.shape[1])
    return jnp.concatenate((first, second), axis=1).astype(BF16)


def split_rows(pairs):
    groups, both, width = pairs.shape
    wide = pairs.astype(F32)
    first = wide[:, : both // 2].reshape(groups * both // 2, width)
    second = wide[:, both // 2 :].reshape(groups * both // 2, width)
    return first.astype(BF16), second.astype(BF16)


def softmaxes(router, tokens, images):
    logits = dot(router, tokens, 1, 1)
    experts, columns = logits.shape
    mask = own_image(experts, images, columns)
    combine = jnp.exp(logits - jnp.max(logits, axis=0, keepdims=True))
    combine = combine / jnp.sum(combine, axis=0, keepdims=True)
    block = jnp.where(mask, spread_rows(logits, images), -jnp.inf)
    block = jnp.exp(block - jnp.max(block, axis=1, keepdims=True))
    block = block / jnp.sum(block, axis=1, keepdims=True)
    return block, combine, mask


def slots_kernel(
    images, tokens_hbm, router_hbm, grad_hbm, win_hbm, wout_hbm, sent_ref, win_out, wout_out, *scratch
):
    tokens_ref, router_ref, grad_ref, sems = scratch
    pairs = (
        (tokens_hbm, tokens_ref),
        (router_hbm, router_ref),
        (grad_hbm, grad_ref),
        (win_hbm, win_out),
        (wout_hbm, wout_out),
    )
    loads = [
        pltpu.make_async_copy(source, target, sems.at[i])
        for i, (source, target) in enumerate(pairs)
    ]
    for load in loads:
        load.start()
    loads[0].wait()
    loads[1].wait()
    tokens = tokens_ref[...]
    block, combine, mask = softmaxes(router_ref[...], tokens, images)
    combine_block = jnp.where(mask, spread_rows(combine, images), 0.0)
    slot_in = dot(block.astype(BF16), tokens, 1, 0)
    loads[2].wait()
    slot_grad = dot(combine_block.astype(BF16), grad_ref[...], 1, 0)
    sent_ref[...] = pair_rows(slot_in, slot_grad, combine.shape[0])
    loads[3].wait()
    loads[4].wait()


def expert_kernel(recv_ref, win_ref, wout_ref, back_ref, *, step):
    slots, cotan = split_rows(recv_ref[...])
    out = jnp.zeros(slots.shape, F32)
    back = jnp.zeros(slots.shape, F32)
    for start in range(0, win_ref.shape[1], step):
        w_in = win_ref[:, start : start + step]
        w_out = wout_ref[:, start : start + step]
        value, slope = gelu_pair(dot(slots, w_in, 1, 0))
        pre_grad = dot(cotan, w_out, 1, 0) * slope
        out = out + dot(value.astype(BF16), w_out, 1, 1)
        back = back + dot(pre_grad.astype(BF16), w_in, 1, 1)
    back_ref[...] = pair_rows(out, back, recv_ref.shape[0])


def logits_kernel(
    images, back_hbm, tokens_ref, router_ref, grad_ref, send_ref, logit_ref, back_ref, sem
):
    load = pltpu.make_async_copy(back_hbm, back_ref, sem)
    load.start()
    tokens = tokens_ref[...]
    dispatch, combine, mask = softmaxes(router_ref[...], tokens, images)
    load.wait()
    slot_out, slot_in_grad = split_rows(back_ref[...])
    disp = jnp.where(mask, dot(slot_in_grad, tokens, 1, 1), 0.0)
    comb = fold_rows(jnp.where(mask, dot(slot_out, grad_ref[...], 1, 1), 0.0), images)
    mean = jnp.sum(dispatch * disp, axis=1, keepdims=True)
    from_dispatch = fold_rows(dispatch * (disp - mean), images)
    from_combine = combine * (comb - jnp.sum(combine * comb, axis=0, keepdims=True))
    logit_grad = (from_combine + from_dispatch).astype(BF16)
    logit_ref[...] = logit_grad
    part = dot(logit_grad, tokens, 1, 0)
    devices, _, width = send_ref.shape
    shares = part.shape[1] // width
    for share in range(shares):
        piece = part[:, share * width : (share + 1) * width].astype(BF16)
        for device in range(share, devices, shares):
            send_ref[device] = piece


def tokens_kernel(images, back_ref, tokens_ref, router_ref, logit_ref, out_ref):
    router = router_ref[...]
    dispatch, _, _ = softmaxes(router, tokens_ref[...], images)
    _, slot_in_grad = split_rows(back_ref[...])
    out = dot(dispatch.astype(BF16), slot_in_grad, 0, 0)
    out = out + dot(logit_ref[...], router, 0, 0)
    out_ref[...] = out.astype(BF16)


def own_rows(share, rows, row_count):
    shape = (row_count, rows.shape[1])
    row = lax.broadcasted_iota(jnp.int32, shape, 0) + share * row_count
    pick = jnp.where(lax.broadcasted_iota(jnp.int32, shape, 1) == row, 1.0, 0.0)
    return dot(pick.astype(BF16), rows, 1, 1).astype(BF16)


def weights_kernel(count, share_ref, *refs):
    spread, (win_ref, wout_ref, win_hbm, wout_hbm) = refs[:count], refs[count : count + 4]
    rows_ref, win_out, wout_out, load_sems, store_sems = refs[count + 4 :]
    chunks, row_count, step = win_out.shape
    loads = [
        pltpu.make_async_copy(ref, rows_ref.at[k], load_sems.at[k])
        for k, ref in enumerate(spread)
    ]
    for load in loads:
        load.start()
    for load in loads:
        load.wait()
    slots, cotan = split_rows(rows_ref[...].reshape((-1,) + rows_ref.shape[2:]))
    own_slots = own_rows(share_ref[0], slots, row_count)
    own_cotan = own_rows(share_ref[0], cotan, row_count)
    stores = []
    for chunk in range(chunks):
        part = slice(chunk * step, (chunk + 1) * step)
        value, slope = gelu_pair(dot(slots, win_ref[:, part], 1, 0))
        pre_grad = dot(cotan, wout_ref[:, part], 1, 0) * slope
        win_out[chunk] = dot(own_slots, pre_grad.astype(BF16), 1, 0)
        wout_out[chunk] = dot(own_cotan, value.astype(BF16), 1, 0)
        where = (slice(None), pl.ds(chunk * step, step))
        for which, (source, target) in enumerate(((win_out, win_hbm), (wout_out, wout_hbm))):
            store = pltpu.make_async_copy(
                source.at[chunk], target.at[where], store_sems.at[which, chunk]
            )
            store.start()
            stores.append(store)
    for store in stores:
        store.wait()


def long_weights_kernel(share_ref, spread_ref, win_ref, wout_ref, win_out, wout_out, *, step):
    slots, cotan = split_rows(spread_ref[...].reshape((-1,) + spread_ref.shape[2:]))
    own_slots = own_rows(share_ref[0], slots, win_out.shape[0])
    own_cotan = own_rows(share_ref[0], cotan, win_out.shape[0])

    @pl.when(pl.program_id(0) == 0)
    def _():
        win_out[...] = jnp.zeros_like(win_out)
        wout_out[...] = jnp.zeros_like(wout_out)

    for start in range(0, win_ref.shape[1], step):
        part = slice(start, start + step)
        value, slope = gelu_pair(dot(slots, win_ref[:, part], 1, 0))
        pre_grad = dot(cotan, wout_ref[:, part], 1, 0) * slope
        win_out[:, part] += dot(own_slots, pre_grad.astype(BF16), 1, 0)
        wout_out[:, part] += dot(own_cotan, value.astype(BF16), 1, 0)


def on_device(tokens, router, w_in, w_out, out_grad):
    owners, shares = lax.axis_size("expert"), lax.axis_size("dp")
    images, per_image, width = tokens.shape
    experts = router.shape[1]
    hidden = w_in.shape[2]
    columns = images * per_image
    row_count = width // shares
    tokens2 = tokens.reshape(columns, width)
    grad2 = out_grad.reshape(columns, width)
    router_rows = router.T
    w_in2, w_out2 = w_in.reshape(width, hidden), w_out.reshape(width, hidden)
    params = pltpu.CompilerParams(vmem_limit_bytes=VMEM_BYTES)
    whole = pltpu.CompilerParams(vmem_limit_bytes=WHOLE_BYTES)

    def struct(shape, dtype):
        return jax.ShapeDtypeStruct(shape, dtype)

    in_place = pl.BlockSpec(memory_space=pl.ANY)
    sent, w_in2, w_out2 = pl.pallas_call(
        functools.partial(slots_kernel, images),
        in_specs=[in_place] * 5,
        out_specs=[pl.BlockSpec(memory_space=pltpu.VMEM), in_place, in_place],
        out_shape=[
            struct((experts, 2 * images, width), BF16),
            struct((width, hidden), BF16),
            struct((width, hidden), BF16),
        ],
        scratch_shapes=[
            pltpu.VMEM((columns, width), BF16),
            pltpu.VMEM((experts, width), BF16),
            pltpu.VMEM((columns, width), BF16),
            pltpu.SemaphoreType.DMA((5,)),
        ],
        compiler_params=whole,
        name="slots",
    )(tokens2, router_rows, grad2, w_in2, w_out2)
    recv = lax.all_to_all(sent, "expert", split_axis=0, concat_axis=0, tiled=True)
    back = pl.pallas_call(
        functools.partial(expert_kernel, step=512),
        out_shape=struct(recv.shape, BF16),
        compiler_params=params,
        name="expert",
    )(recv, w_in2, w_out2)
    recv, back = lax.optimization_barrier((recv, back))
    slots_back = lax.all_to_all(back, "expert", split_axis=0, concat_axis=0, tiled=True)
    few = shares * owners * images <= 512
    if few:
        spread = [recv] + [
            lax.ppermute(recv, "dp", [(i, i ^ k) for i in range(shares)])
            for k in range(1, shares)
        ]
    else:
        spread = [lax.all_gather(recv, "dp", axis=0, tiled=False)]

    in_vmem = pl.BlockSpec(memory_space=pltpu.VMEM)
    router_send, logit_grad = pl.pallas_call(
        functools.partial(logits_kernel, images),
        in_specs=[in_place] + [in_vmem] * 3,
        out_shape=(
            struct((owners * shares, experts, row_count), BF16),
            struct((experts, columns), BF16),
        ),
        scratch_shapes=[pltpu.VMEM(back.shape, BF16), pltpu.SemaphoreType.DMA],
        compiler_params=params,
        name="logits",
    )(slots_back, tokens2, router_rows, grad2)
    share, router_send = lax.optimization_barrier((lax.axis_index("dp").reshape(1), router_send))
    router_parts = lax.all_to_all(
        router_send,
        ("expert", "dp"),
        split_axis=0,
        concat_axis=0,
        tiled=True,
    )

    tokens_grad = pl.pallas_call(
        functools.partial(tokens_kernel, images),
        out_shape=struct((columns, width), BF16),
        compiler_params=params,
        name="tokens",
    )(slots_back, tokens2, router_rows, logit_grad)
    in_smem = pl.BlockSpec(memory_space=pltpu.SMEM)
    out_shape = [struct((row_count, hidden), F32)] * 2
    if few:
        chunks, step = hidden // 512, 512
        w_in_grad, w_out_grad = pl.pallas_call(
            functools.partial(weights_kernel, shares),
            in_specs=[in_smem] + [in_place] * shares + [in_vmem] * 2,
            out_specs=[in_place] * 2,
            out_shape=out_shape,
            scratch_shapes=[
                pltpu.VMEM((shares,) + recv.shape, BF16),
                pltpu.VMEM((chunks, row_count, step), F32),
                pltpu.VMEM((chunks, row_count, step), F32),
                pltpu.SemaphoreType.DMA((shares,)),
                pltpu.SemaphoreType.DMA((2, chunks)),
            ],
            compiler_params=params,
            name="weights",
        )(share, *spread, w_in2, w_out2)
    else:
        w_in_grad, w_out_grad = pl.pallas_call(
            functools.partial(long_weights_kernel, step=512),
            grid=(shares,),
            in_specs=[
                in_smem,
                pl.BlockSpec((1,) + recv.shape, lambda i: (i, 0, 0, 0)),
                pl.BlockSpec((width, hidden), lambda i: (0, 0)),
                pl.BlockSpec((width, hidden), lambda i: (0, 0)),
            ],
            out_specs=[pl.BlockSpec((row_count, hidden), lambda i: (0, 0))] * 2,
            out_shape=out_shape,
            compiler_params=params,
            name="weights",
        )(share, *spread, w_in2, w_out2)
    router_grad = jnp.sum(router_parts.astype(F32), axis=0).T
    return (
        tokens_grad.reshape(tokens.shape),
        w_in_grad.reshape(1, row_count, hidden),
        w_out_grad.reshape(1, row_count, hidden),
        router_grad,
    )


def solution(mesh):
    placed = (
        P(("expert", "dp"), None, None),
        P(),
        P("expert", None, None),
        P("expert", None, None),
        P(("expert", "dp"), None, None),
    )
    return jax.shard_map(
        on_device,
        mesh=mesh,
        in_specs=placed,
        out_specs=(
            P(("expert", "dp"), None, None),
            P("expert", "dp", None),
            P("expert", "dp", None),
            P("dp", None),
        ),
        check_vma=False,
    )
```

```python
import functools
import math

import jax
import jax.numpy as jnp
from jax import lax
from jax.experimental import pallas as pl
from jax.experimental.pallas import tpu as pltpu
from jax.sharding import PartitionSpec as P

F32 = jnp.float32
BF16 = jnp.bfloat16
VMEM_BYTES = 24 * 1024 * 1024
WHOLE_BYTES = 56 * 1024 * 1024


def gelu_pair(value):
    coef = math.sqrt(2.0 / math.pi)
    cubic = 0.044715 * coef
    square = value * value
    half = 0.5 * jnp.tanh(value * (coef + cubic * square)) + 0.5
    steep = value * (2.0 * coef + 6.0 * cubic * square) * (1.0 - half)
    return value * half, half + half * steep


def dot(left, right, left_dim, right_dim):
    return lax.dot_general(
        left, right, (((left_dim,), (right_dim,)), ((), ())), preferred_element_type=F32
    )


def own_image(experts, images, columns):
    shape = (experts, images, columns)
    image = lax.broadcasted_iota(jnp.int32, shape, 1)
    token = lax.broadcasted_iota(jnp.int32, shape, 2)
    low = image * (columns // images)
    inside = (token >= low) & (token < low + columns // images)
    return inside.reshape(experts * images, columns)


def spread_rows(compact, images):
    experts, columns = compact.shape
    wide = jnp.broadcast_to(compact[:, None, :], (experts, images, columns))
    return wide.reshape(experts * images, columns)


def fold_rows(block, images):
    rows, columns = block.shape
    return jnp.sum(block.reshape(rows // images, images, columns), axis=1)


def pair_rows(first, second, groups):
    images = first.shape[0] // groups
    first = first.reshape(groups, images, first.shape[1])
    second = second.reshape(groups, images, second.shape[1])
    return jnp.concatenate((first, second), axis=1).astype(BF16)


def split_rows(pairs):
    groups, both, width = pairs.shape
    wide = pairs.astype(F32)
    first = wide[:, : both // 2].reshape(groups * both // 2, width)
    second = wide[:, both // 2 :].reshape(groups * both // 2, width)
    return first.astype(BF16), second.astype(BF16)


def softmaxes(router, tokens, images):
    logits = dot(router, tokens, 1, 1)
    experts, columns = logits.shape
    mask = own_image(experts, images, columns)
    combine = jnp.exp(logits - jnp.max(logits, axis=0, keepdims=True))
    combine = combine / jnp.sum(combine, axis=0, keepdims=True)
    block = jnp.where(mask, spread_rows(logits, images), -jnp.inf)
    block = jnp.exp(block - jnp.max(block, axis=1, keepdims=True))
    block = block * (1.0 / jnp.sum(block, axis=1, keepdims=True))
    return block, combine, mask


def slots_kernel(images, tokens_hbm, router_hbm, grad_hbm, sent_ref, *scratch):
    tokens_ref, router_ref, grad_ref, sems = scratch
    first = [
        pltpu.make_async_copy(tokens_hbm, tokens_ref, sems.at[0]),
        pltpu.make_async_copy(router_hbm, router_ref, sems.at[1]),
    ]
    second = [pltpu.make_async_copy(grad_hbm, grad_ref, sems.at[2])]
    for load in first + second:
        load.start()
    for load in first:
        load.wait()
    tokens = tokens_ref[...]
    block, combine, mask = softmaxes(router_ref[...], tokens, images)
    combine_block = jnp.where(mask, spread_rows(combine, images), 0.0)
    slot_in = dot(block.astype(BF16), tokens, 1, 0)
    for load in second:
        load.wait()
    slot_grad = dot(combine_block.astype(BF16), grad_ref[...], 1, 0)
    sent_ref[...] = pair_rows(slot_in, slot_grad, combine.shape[0])


def stage_kernel(win_hbm, wout_hbm, win_ref, wout_ref, sems):
    loads = (
        pltpu.make_async_copy(win_hbm, win_ref, sems.at[0]),
        pltpu.make_async_copy(wout_hbm, wout_ref, sems.at[1]),
    )
    for load in loads:
        load.start()
    for load in loads:
        load.wait()


def expert_kernel(recv_ref, win_ref, wout_ref, back_ref, *, step):
    slots, cotan = split_rows(recv_ref[...])
    out = jnp.zeros(slots.shape, F32)
    back = jnp.zeros(slots.shape, F32)
    parts = [slice(start, start + step) for start in range(0, win_ref.shape[1], step)]

    def first(part):
        return dot(slots, win_ref[:, part], 1, 0), dot(cotan, wout_ref[:, part], 1, 0)

    ahead = first(parts[0])
    for k, part in enumerate(parts):
        pre_act, hid_grad = ahead
        if k + 1 < len(parts):
            ahead = first(parts[k + 1])
        value, slope = gelu_pair(pre_act)
        out = out + dot(value.astype(BF16), wout_ref[:, part], 1, 1)
        back = back + dot((hid_grad * slope).astype(BF16), win_ref[:, part], 1, 1)
    back_ref[...] = pair_rows(out, back, recv_ref.shape[0])


def logits_kernel(
    images, back_hbm, tokens_ref, router_ref, grad_ref, send_ref, logit_ref, back_ref, sem
):
    load = pltpu.make_async_copy(back_hbm, back_ref, sem)
    load.start()
    tokens = tokens_ref[...]
    dispatch, combine, mask = softmaxes(router_ref[...], tokens, images)
    load.wait()
    slot_out, slot_in_grad = split_rows(back_ref[...])
    disp = dot(slot_in_grad, tokens, 1, 1)
    comb = fold_rows(jnp.where(mask, dot(slot_out, grad_ref[...], 1, 1), 0.0), images)
    mean = jnp.sum(dispatch * disp, axis=1, keepdims=True)
    from_dispatch = fold_rows(dispatch * (disp - mean), images)
    from_combine = combine * (comb - jnp.sum(combine * comb, axis=0, keepdims=True))
    logit_grad = (from_combine + from_dispatch).astype(BF16)
    logit_ref[...] = logit_grad
    part = dot(logit_grad, tokens, 1, 0)
    devices, _, width = send_ref.shape
    shares = part.shape[1] // width
    for share in range(shares):
        piece = part[:, share * width : (share + 1) * width].astype(BF16)
        for device in range(share, devices, shares):
            send_ref[device] = piece


def tokens_kernel(images, back_ref, tokens_ref, router_ref, logit_ref, out_ref):
    router = router_ref[...]
    dispatch, _, _ = softmaxes(router, tokens_ref[...], images)
    _, slot_in_grad = split_rows(back_ref[...])
    out = dot(dispatch.astype(BF16), slot_in_grad, 0, 0)
    out = out + dot(logit_ref[...], router, 0, 0)
    out_ref[...] = out.astype(BF16)


def own_rows(share, rows, row_count):
    shape = (row_count, rows.shape[1])
    row = lax.broadcasted_iota(jnp.int32, shape, 0) + share * row_count
    pick = jnp.where(lax.broadcasted_iota(jnp.int32, shape, 1) == row, 1.0, 0.0)
    return dot(pick.astype(BF16), rows, 1, 1).astype(BF16)


def weights_kernel(count, share_ref, *refs):
    spread, (win_ref, wout_ref, win_hbm, wout_hbm) = refs[:count], refs[count : count + 4]
    rows_ref, win_out, wout_out, load_sems, store_sems = refs[count + 4 :]
    chunks, row_count, step = win_out.shape
    loads = [
        pltpu.make_async_copy(ref, rows_ref.at[k], load_sems.at[k])
        for k, ref in enumerate(spread)
    ]
    for load in loads:
        load.start()
    for load in loads:
        load.wait()
    slots, cotan = split_rows(rows_ref[...].reshape((-1,) + rows_ref.shape[2:]))
    own_slots = own_rows(share_ref[0], slots, row_count)
    own_cotan = own_rows(share_ref[0], cotan, row_count)
    stores = []
    for chunk in range(chunks):
        part = slice(chunk * step, (chunk + 1) * step)
        value, slope = gelu_pair(dot(slots, win_ref[:, part], 1, 0))
        pre_grad = dot(cotan, wout_ref[:, part], 1, 0) * slope
        win_out[chunk] = dot(own_slots, pre_grad.astype(BF16), 1, 0)
        wout_out[chunk] = dot(own_cotan, value.astype(BF16), 1, 0)
        where = (slice(None), pl.ds(chunk * step, step))
        for which, (source, target) in enumerate(((win_out, win_hbm), (wout_out, wout_hbm))):
            store = pltpu.make_async_copy(
                source.at[chunk], target.at[where], store_sems.at[which, chunk]
            )
            store.start()
            stores.append(store)
    for store in stores:
        store.wait()


def long_weights_kernel(share_ref, spread_ref, win_ref, wout_ref, win_out, wout_out, *, step):
    slots, cotan = split_rows(spread_ref[...].reshape((-1,) + spread_ref.shape[2:]))
    own_slots = own_rows(share_ref[0], slots, win_out.shape[0])
    own_cotan = own_rows(share_ref[0], cotan, win_out.shape[0])

    @pl.when(pl.program_id(0) == 0)
    def _():
        win_out[...] = jnp.zeros_like(win_out)
        wout_out[...] = jnp.zeros_like(wout_out)

    for start in range(0, win_ref.shape[1], step):
        part = slice(start, start + step)
        value, slope = gelu_pair(dot(slots, win_ref[:, part], 1, 0))
        pre_grad = dot(cotan, wout_ref[:, part], 1, 0) * slope
        win_out[:, part] += dot(own_slots, pre_grad.astype(BF16), 1, 0)
        wout_out[:, part] += dot(own_cotan, value.astype(BF16), 1, 0)


def on_device(tokens, router, w_in, w_out, out_grad):
    owners, shares = lax.axis_size("expert"), lax.axis_size("dp")
    images, per_image, width = tokens.shape
    experts = router.shape[1]
    hidden = w_in.shape[2]
    columns = images * per_image
    row_count = width // shares
    tokens2 = tokens.reshape(columns, width)
    grad2 = out_grad.reshape(columns, width)
    router_rows = router.T
    w_in2, w_out2 = w_in.reshape(width, hidden), w_out.reshape(width, hidden)
    params = pltpu.CompilerParams(vmem_limit_bytes=VMEM_BYTES)
    whole = pltpu.CompilerParams(vmem_limit_bytes=WHOLE_BYTES)

    def struct(shape, dtype):
        return jax.ShapeDtypeStruct(shape, dtype)

    in_place = pl.BlockSpec(memory_space=pl.ANY)
    sent = pl.pallas_call(
        functools.partial(slots_kernel, images),
        in_specs=[in_place] * 3,
        out_shape=struct((experts, 2 * images, width), BF16),
        scratch_shapes=[
            pltpu.VMEM((columns, width), BF16),
            pltpu.VMEM((experts, width), BF16),
            pltpu.VMEM((columns, width), BF16),
            pltpu.SemaphoreType.DMA((3,)),
        ],
        compiler_params=whole,
        name="slots",
    )(tokens2, router_rows, grad2)
    w_in2, w_out2 = pl.pallas_call(
        stage_kernel,
        in_specs=[in_place] * 2,
        out_specs=[in_place] * 2,
        out_shape=[struct((width, hidden), BF16)] * 2,
        scratch_shapes=[pltpu.SemaphoreType.DMA((2,))],
        compiler_params=pltpu.CompilerParams(vmem_limit_bytes=1024 * 1024),
        cost_estimate=pl.CostEstimate(
            flops=0, bytes_accessed=8 * width * hidden, transcendentals=0
        ),
        name="stage",
    )(w_in2, w_out2)
    recv = lax.all_to_all(sent, "expert", split_axis=0, concat_axis=0, tiled=True)
    back = pl.pallas_call(
        functools.partial(expert_kernel, step=256),
        out_shape=struct(recv.shape, BF16),
        compiler_params=params,
        name="expert",
    )(recv, w_in2, w_out2)
    recv, back = lax.optimization_barrier((recv, back))
    slots_back = lax.all_to_all(back, "expert", split_axis=0, concat_axis=0, tiled=True)
    few = shares * owners * images <= 512
    if few:
        spread = [recv] + [
            lax.ppermute(recv, "dp", [(i, i ^ k) for i in range(shares)])
            for k in range(1, shares)
        ]
    else:
        spread = [lax.all_gather(recv, "dp", axis=0, tiled=False)]

    in_vmem = pl.BlockSpec(memory_space=pltpu.VMEM)
    router_send, logit_grad = pl.pallas_call(
        functools.partial(logits_kernel, images),
        in_specs=[in_place] + [in_vmem] * 3,
        out_shape=(
            struct((owners * shares, experts, row_count), BF16),
            struct((experts, columns), BF16),
        ),
        scratch_shapes=[pltpu.VMEM(back.shape, BF16), pltpu.SemaphoreType.DMA],
        compiler_params=params,
        name="logits",
    )(slots_back, tokens2, router_rows, grad2)
    share, router_send = lax.optimization_barrier((lax.axis_index("dp").reshape(1), router_send))
    router_parts = lax.all_to_all(
        router_send,
        ("expert", "dp"),
        split_axis=0,
        concat_axis=0,
        tiled=True,
    )

    tokens_grad = pl.pallas_call(
        functools.partial(tokens_kernel, images),
        out_shape=struct((columns, width), BF16),
        compiler_params=params,
        name="tokens",
    )(slots_back, tokens2, router_rows, logit_grad)
    in_smem = pl.BlockSpec(memory_space=pltpu.SMEM)
    out_shape = [struct((row_count, hidden), F32)] * 2
    if few:
        chunks, step = hidden // 512, 512
        w_in_grad, w_out_grad = pl.pallas_call(
            functools.partial(weights_kernel, shares),
            in_specs=[in_smem] + [in_place] * shares + [in_vmem] * 2,
            out_specs=[in_place] * 2,
            out_shape=out_shape,
            scratch_shapes=[
                pltpu.VMEM((shares,) + recv.shape, BF16),
                pltpu.VMEM((chunks, row_count, step), F32),
                pltpu.VMEM((chunks, row_count, step), F32),
                pltpu.SemaphoreType.DMA((shares,)),
                pltpu.SemaphoreType.DMA((2, chunks)),
            ],
            compiler_params=params,
            name="weights",
        )(share, *spread, w_in2, w_out2)
    else:
        w_in_grad, w_out_grad = pl.pallas_call(
            functools.partial(long_weights_kernel, step=512),
            grid=(shares,),
            in_specs=[
                in_smem,
                pl.BlockSpec((1,) + recv.shape, lambda i: (i, 0, 0, 0)),
                pl.BlockSpec((width, hidden), lambda i: (0, 0)),
                pl.BlockSpec((width, hidden), lambda i: (0, 0)),
            ],
            out_specs=[pl.BlockSpec((row_count, hidden), lambda i: (0, 0))] * 2,
            out_shape=out_shape,
            compiler_params=params,
            name="weights",
        )(share, *spread, w_in2, w_out2)
    router_grad = jnp.sum(router_parts.astype(F32), axis=0).T
    return (
        tokens_grad.reshape(tokens.shape),
        w_in_grad.reshape(1, row_count, hidden),
        w_out_grad.reshape(1, row_count, hidden),
        router_grad,
    )


def solution(mesh):
    placed = (
        P(("expert", "dp"), None, None),
        P(),
        P("expert", None, None),
        P("expert", None, None),
        P(("expert", "dp"), None, None),
    )
    return jax.shard_map(
        on_device,
        mesh=mesh,
        in_specs=placed,
        out_specs=(
            P(("expert", "dp"), None, None),
            P("expert", "dp", None),
            P("expert", "dp", None),
            P("dp", None),
        ),
        check_vma=False,
    )
```

```python
import functools
import math

import jax
import jax.numpy as jnp
from jax import lax
from jax.experimental import pallas as pl
from jax.experimental.pallas import tpu as pltpu
from jax.sharding import PartitionSpec as P

F32 = jnp.float32
BF16 = jnp.bfloat16
VMEM_BYTES = 24 * 1024 * 1024
WHOLE_BYTES = 56 * 1024 * 1024


def gelu_pair(value):
    coef = math.sqrt(2.0 / math.pi)
    cubic = 0.044715 * coef
    square = value * value
    half = 0.5 * jnp.tanh(value * (coef + cubic * square)) + 0.5
    steep = value * (2.0 * coef + 6.0 * cubic * square) * (1.0 - half)
    return value * half, half + half * steep


def dot(left, right, left_dim, right_dim):
    return lax.dot_general(
        left, right, (((left_dim,), (right_dim,)), ((), ())), preferred_element_type=F32
    )


def own_image(experts, images, columns):
    shape = (experts, images, columns)
    image = lax.broadcasted_iota(jnp.int32, shape, 1)
    token = lax.broadcasted_iota(jnp.int32, shape, 2)
    low = image * (columns // images)
    inside = (token >= low) & (token < low + columns // images)
    return inside.reshape(experts * images, columns)


def spread_rows(compact, images):
    experts, columns = compact.shape
    wide = jnp.broadcast_to(compact[:, None, :], (experts, images, columns))
    return wide.reshape(experts * images, columns)


def fold_rows(block, images):
    rows, columns = block.shape
    return jnp.sum(block.reshape(rows // images, images, columns), axis=1)


def pair_rows(first, second, groups):
    images = first.shape[0] // groups
    first = first.reshape(groups, images, first.shape[1])
    second = second.reshape(groups, images, second.shape[1])
    return jnp.concatenate((first, second), axis=1).astype(BF16)


def split_rows(pairs):
    groups, both, width = pairs.shape
    wide = pairs.astype(F32)
    first = wide[:, : both // 2].reshape(groups * both // 2, width)
    second = wide[:, both // 2 :].reshape(groups * both // 2, width)
    return first.astype(BF16), second.astype(BF16)


def centre_out(count):
    return sorted(range(count), key=lambda i: (abs(2 * i - count + 1), i))


def in_expert_order(ref):
    order = centre_out(ref.shape[0])
    return jnp.stack([ref[order.index(i)] for i in range(len(order))], axis=0)


def exchange(chunks):
    order = centre_out(lax.axis_size("expert"))
    return lax.all_to_all(
        chunks, "expert", split_axis=0, concat_axis=0, tiled=True, axis_index_groups=[order]
    )


def softmaxes(router, tokens, images):
    logits = dot(router, tokens, 1, 1)
    experts, columns = logits.shape
    mask = own_image(experts, images, columns)
    combine = jnp.exp(logits - jnp.max(logits, axis=0, keepdims=True))
    combine = combine / jnp.sum(combine, axis=0, keepdims=True)
    block = jnp.where(mask, spread_rows(logits, images), -jnp.inf)
    block = jnp.exp(block - jnp.max(block, axis=1, keepdims=True))
    block = block / jnp.sum(block, axis=1, keepdims=True)
    return block, combine, mask


def slots_kernel(images, tokens_hbm, router_hbm, grad_hbm, sent_ref, *scratch):
    tokens_ref, router_ref, grad_ref, sems = scratch
    first = [
        pltpu.make_async_copy(tokens_hbm, tokens_ref, sems.at[0]),
        pltpu.make_async_copy(router_hbm, router_ref, sems.at[1]),
    ]
    second = [pltpu.make_async_copy(grad_hbm, grad_ref, sems.at[2])]
    for load in first + second:
        load.start()
    for load in first:
        load.wait()
    tokens = tokens_ref[...]
    block, combine, mask = softmaxes(router_ref[...], tokens, images)
    combine_block = jnp.where(mask, spread_rows(combine, images), 0.0)
    slot_in = dot(block.astype(BF16), tokens, 1, 0)
    for load in second:
        load.wait()
    slot_grad = dot(combine_block.astype(BF16), grad_ref[...], 1, 0)
    pairs = pair_rows(slot_in, slot_grad, combine.shape[0])
    for k, i in enumerate(centre_out(pairs.shape[0])):
        sent_ref[k] = pairs[i]


def stage_kernel(win_hbm, wout_hbm, win_ref, wout_ref, sems):
    loads = (
        pltpu.make_async_copy(win_hbm, win_ref, sems.at[0]),
        pltpu.make_async_copy(wout_hbm, wout_ref, sems.at[1]),
    )
    for load in loads:
        load.start()
    for load in loads:
        load.wait()


def expert_kernel(recv_ref, win_ref, wout_ref, back_ref, *, step):
    slots, cotan = split_rows(recv_ref[...])
    out = jnp.zeros(slots.shape, F32)
    back = jnp.zeros(slots.shape, F32)
    for start in range(0, win_ref.shape[1], step):
        w_in = win_ref[:, start : start + step]
        w_out = wout_ref[:, start : start + step]
        value, slope = gelu_pair(dot(slots, w_in, 1, 0))
        pre_grad = dot(cotan, w_out, 1, 0) * slope
        out = out + dot(value.astype(BF16), w_out, 1, 1)
        back = back + dot(pre_grad.astype(BF16), w_in, 1, 1)
    back_ref[...] = pair_rows(out, back, recv_ref.shape[0])


def logits_kernel(
    images, back_hbm, tokens_ref, router_ref, grad_ref, send_ref, logit_ref, back_ref, sem
):
    load = pltpu.make_async_copy(back_hbm, back_ref, sem)
    load.start()
    tokens = tokens_ref[...]
    dispatch, combine, mask = softmaxes(router_ref[...], tokens, images)
    load.wait()
    slot_out, slot_in_grad = split_rows(in_expert_order(back_ref))
    disp = jnp.where(mask, dot(slot_in_grad, tokens, 1, 1), 0.0)
    comb = fold_rows(jnp.where(mask, dot(slot_out, grad_ref[...], 1, 1), 0.0), images)
    mean = jnp.sum(dispatch * disp, axis=1, keepdims=True)
    from_dispatch = fold_rows(dispatch * (disp - mean), images)
    from_combine = combine * (comb - jnp.sum(combine * comb, axis=0, keepdims=True))
    logit_grad = (from_combine + from_dispatch).astype(BF16)
    logit_ref[...] = logit_grad
    part = dot(logit_grad, tokens, 1, 0)
    devices, _, width = send_ref.shape
    shares = part.shape[1] // width
    for share in range(shares):
        piece = part[:, share * width : (share + 1) * width].astype(BF16)
        for device in range(share, devices, shares):
            send_ref[device] = piece


def tokens_kernel(images, back_ref, tokens_ref, router_ref, logit_ref, out_ref):
    router = router_ref[...]
    dispatch, _, _ = softmaxes(router, tokens_ref[...], images)
    _, slot_in_grad = split_rows(in_expert_order(back_ref))
    out = dot(dispatch.astype(BF16), slot_in_grad, 0, 0)
    out = out + dot(logit_ref[...], router, 0, 0)
    out_ref[...] = out.astype(BF16)


def own_rows(share, rows, row_count):
    shape = (row_count, rows.shape[1])
    row = lax.broadcasted_iota(jnp.int32, shape, 0) + share * row_count
    pick = jnp.where(lax.broadcasted_iota(jnp.int32, shape, 1) == row, 1.0, 0.0)
    return dot(pick.astype(BF16), rows, 1, 1).astype(BF16)


def weights_kernel(count, share_ref, *refs):
    spread, (win_ref, wout_ref, win_hbm, wout_hbm) = refs[:count], refs[count : count + 4]
    rows_ref, win_out, wout_out, load_sems, store_sems = refs[count + 4 :]
    chunks, row_count, step = win_out.shape
    loads = [
        pltpu.make_async_copy(ref, rows_ref.at[k], load_sems.at[k])
        for k, ref in enumerate(spread)
    ]
    for load in loads:
        load.start()
    for load in loads:
        load.wait()
    slots, cotan = split_rows(rows_ref[...].reshape((-1,) + rows_ref.shape[2:]))
    own_slots = own_rows(share_ref[0], slots, row_count)
    own_cotan = own_rows(share_ref[0], cotan, row_count)
    stores = []
    for chunk in range(chunks):
        part = slice(chunk * step, (chunk + 1) * step)
        value, slope = gelu_pair(dot(slots, win_ref[:, part], 1, 0))
        pre_grad = dot(cotan, wout_ref[:, part], 1, 0) * slope
        win_out[chunk] = dot(own_slots, pre_grad.astype(BF16), 1, 0)
        wout_out[chunk] = dot(own_cotan, value.astype(BF16), 1, 0)
        where = (slice(None), pl.ds(chunk * step, step))
        for which, (source, target) in enumerate(((win_out, win_hbm), (wout_out, wout_hbm))):
            store = pltpu.make_async_copy(
                source.at[chunk], target.at[where], store_sems.at[which, chunk]
            )
            store.start()
            stores.append(store)
    for store in stores:
        store.wait()


def long_weights_kernel(share_ref, spread_ref, win_ref, wout_ref, win_out, wout_out, *, step):
    slots, cotan = split_rows(spread_ref[...].reshape((-1,) + spread_ref.shape[2:]))
    own_slots = own_rows(share_ref[0], slots, win_out.shape[0])
    own_cotan = own_rows(share_ref[0], cotan, win_out.shape[0])

    @pl.when(pl.program_id(0) == 0)
    def _():
        win_out[...] = jnp.zeros_like(win_out)
        wout_out[...] = jnp.zeros_like(wout_out)

    for start in range(0, win_ref.shape[1], step):
        part = slice(start, start + step)
        value, slope = gelu_pair(dot(slots, win_ref[:, part], 1, 0))
        pre_grad = dot(cotan, wout_ref[:, part], 1, 0) * slope
        win_out[:, part] += dot(own_slots, pre_grad.astype(BF16), 1, 0)
        wout_out[:, part] += dot(own_cotan, value.astype(BF16), 1, 0)


def on_device(tokens, router, w_in, w_out, out_grad):
    owners, shares = lax.axis_size("expert"), lax.axis_size("dp")
    images, per_image, width = tokens.shape
    experts = router.shape[1]
    hidden = w_in.shape[2]
    columns = images * per_image
    row_count = width // shares
    tokens2 = tokens.reshape(columns, width)
    grad2 = out_grad.reshape(columns, width)
    router_rows = router.T
    w_in2, w_out2 = w_in.reshape(width, hidden), w_out.reshape(width, hidden)
    params = pltpu.CompilerParams(vmem_limit_bytes=VMEM_BYTES)
    whole = pltpu.CompilerParams(vmem_limit_bytes=WHOLE_BYTES)

    def struct(shape, dtype):
        return jax.ShapeDtypeStruct(shape, dtype)

    in_place = pl.BlockSpec(memory_space=pl.ANY)
    sent = pl.pallas_call(
        functools.partial(slots_kernel, images),
        in_specs=[in_place] * 3,
        out_shape=struct((experts, 2 * images, width), BF16),
        scratch_shapes=[
            pltpu.VMEM((columns, width), BF16),
            pltpu.VMEM((experts, width), BF16),
            pltpu.VMEM((columns, width), BF16),
            pltpu.SemaphoreType.DMA((3,)),
        ],
        compiler_params=whole,
        name="slots",
    )(tokens2, router_rows, grad2)
    w_in2, w_out2 = pl.pallas_call(
        stage_kernel,
        in_specs=[in_place] * 2,
        out_specs=[in_place] * 2,
        out_shape=[struct((width, hidden), BF16)] * 2,
        scratch_shapes=[pltpu.SemaphoreType.DMA((2,))],
        compiler_params=pltpu.CompilerParams(vmem_limit_bytes=1024 * 1024),
        cost_estimate=pl.CostEstimate(
            flops=0, bytes_accessed=8 * width * hidden, transcendentals=0
        ),
        name="stage",
    )(w_in2, w_out2)
    recv = exchange(sent)
    back = pl.pallas_call(
        functools.partial(expert_kernel, step=512),
        out_shape=struct(recv.shape, BF16),
        compiler_params=params,
        name="expert",
    )(recv, w_in2, w_out2)
    recv, back = lax.optimization_barrier((recv, back))
    slots_back = exchange(back)
    few = shares * owners * images <= 512
    if few:
        spread = [recv] + [
            lax.ppermute(recv, "dp", [(i, i ^ k) for i in range(shares)])
            for k in range(1, shares)
        ]
    else:
        spread = [lax.all_gather(recv, "dp", axis=0, tiled=False)]

    in_vmem = pl.BlockSpec(memory_space=pltpu.VMEM)
    router_send, logit_grad = pl.pallas_call(
        functools.partial(logits_kernel, images),
        in_specs=[in_place] + [in_vmem] * 3,
        out_shape=(
            struct((owners * shares, experts, row_count), BF16),
            struct((experts, columns), BF16),
        ),
        scratch_shapes=[pltpu.VMEM(back.shape, BF16), pltpu.SemaphoreType.DMA],
        compiler_params=params,
        name="logits",
    )(slots_back, tokens2, router_rows, grad2)
    share, router_send = lax.optimization_barrier((lax.axis_index("dp").reshape(1), router_send))
    router_parts = lax.all_to_all(
        router_send,
        ("expert", "dp"),
        split_axis=0,
        concat_axis=0,
        tiled=True,
    )

    tokens_grad = pl.pallas_call(
        functools.partial(tokens_kernel, images),
        out_shape=struct((columns, width), BF16),
        compiler_params=params,
        name="tokens",
    )(slots_back, tokens2, router_rows, logit_grad)
    in_smem = pl.BlockSpec(memory_space=pltpu.SMEM)
    out_shape = [struct((row_count, hidden), F32)] * 2
    if few:
        chunks, step = hidden // 512, 512
        w_in_grad, w_out_grad = pl.pallas_call(
            functools.partial(weights_kernel, shares),
            in_specs=[in_smem] + [in_place] * shares + [in_vmem] * 2,
            out_specs=[in_place] * 2,
            out_shape=out_shape,
            scratch_shapes=[
                pltpu.VMEM((shares,) + recv.shape, BF16),
                pltpu.VMEM((chunks, row_count, step), F32),
                pltpu.VMEM((chunks, row_count, step), F32),
                pltpu.SemaphoreType.DMA((shares,)),
                pltpu.SemaphoreType.DMA((2, chunks)),
            ],
            compiler_params=params,
            name="weights",
        )(share, *spread, w_in2, w_out2)
    else:
        w_in_grad, w_out_grad = pl.pallas_call(
            functools.partial(long_weights_kernel, step=512),
            grid=(shares,),
            in_specs=[
                in_smem,
                pl.BlockSpec((1,) + recv.shape, lambda i: (i, 0, 0, 0)),
                pl.BlockSpec((width, hidden), lambda i: (0, 0)),
                pl.BlockSpec((width, hidden), lambda i: (0, 0)),
            ],
            out_specs=[pl.BlockSpec((row_count, hidden), lambda i: (0, 0))] * 2,
            out_shape=out_shape,
            compiler_params=params,
            name="weights",
        )(share, *spread, w_in2, w_out2)
    router_grad = jnp.sum(router_parts.astype(F32), axis=0).T
    return (
        tokens_grad.reshape(tokens.shape),
        w_in_grad.reshape(1, row_count, hidden),
        w_out_grad.reshape(1, row_count, hidden),
        router_grad,
    )


def solution(mesh):
    placed = (
        P(("expert", "dp"), None, None),
        P(),
        P("expert", None, None),
        P("expert", None, None),
        P(("expert", "dp"), None, None),
    )
    return jax.shard_map(
        on_device,
        mesh=mesh,
        in_specs=placed,
        out_specs=(
            P(("expert", "dp"), None, None),
            P("expert", "dp", None),
            P("expert", "dp", None),
            P("dp", None),
        ),
        check_vma=False,
    )
```

```python
import functools
import math

import jax
import jax.numpy as jnp
from jax import lax
from jax.experimental import pallas as pl
from jax.experimental.pallas import tpu as pltpu
from jax.sharding import PartitionSpec as P

F32 = jnp.float32
BF16 = jnp.bfloat16
VMEM_BYTES = 24 * 1024 * 1024
WHOLE_BYTES = 56 * 1024 * 1024


def gelu_pair(value):
    coef = math.sqrt(2.0 / math.pi)
    cubic = 0.044715 * coef
    square = value * value
    half = 0.5 * jnp.tanh(value * (coef + cubic * square)) + 0.5
    steep = value * (2.0 * coef + 6.0 * cubic * square) * (1.0 - half)
    return value * half, half + half * steep


def dot(left, right, left_dim, right_dim):
    return lax.dot_general(
        left, right, (((left_dim,), (right_dim,)), ((), ())), preferred_element_type=F32
    )


def own_image(experts, images, columns):
    shape = (experts, images, columns)
    image = lax.broadcasted_iota(jnp.int32, shape, 1)
    token = lax.broadcasted_iota(jnp.int32, shape, 2)
    low = image * (columns // images)
    inside = (token >= low) & (token < low + columns // images)
    return inside.reshape(experts * images, columns)


def spread_rows(compact, images):
    experts, columns = compact.shape
    wide = jnp.broadcast_to(compact[:, None, :], (experts, images, columns))
    return wide.reshape(experts * images, columns)


def fold_rows(block, images):
    rows, columns = block.shape
    return jnp.sum(block.reshape(rows // images, images, columns), axis=1)


def pair_rows(first, second, groups):
    images = first.shape[0] // groups
    first = first.reshape(groups, images, first.shape[1])
    second = second.reshape(groups, images, second.shape[1])
    return jnp.concatenate((first, second), axis=1).astype(BF16)


def split_rows(pairs):
    groups, both, width = pairs.shape
    wide = pairs.astype(F32)
    first = wide[:, : both // 2].reshape(groups * both // 2, width)
    second = wide[:, both // 2 :].reshape(groups * both // 2, width)
    return first.astype(BF16), second.astype(BF16)


def centre_out(count):
    return sorted(range(count), key=lambda i: (abs(2 * i - count + 1), i))


def in_expert_order(ref):
    order = centre_out(ref.shape[0])
    return jnp.stack([ref[order.index(i)] for i in range(len(order))], axis=0)


def exchange(chunks, axis, order):
    return lax.all_to_all(
        chunks, axis, split_axis=0, concat_axis=0, tiled=True, axis_index_groups=[order]
    )


def softmaxes(router, tokens, images):
    logits = dot(router, tokens, 1, 1)
    experts, columns = logits.shape
    mask = own_image(experts, images, columns)
    combine = jnp.exp(logits - jnp.max(logits, axis=0, keepdims=True))
    combine = combine / jnp.sum(combine, axis=0, keepdims=True)
    block = jnp.where(mask, spread_rows(logits, images), -jnp.inf)
    block = jnp.exp(block - jnp.max(block, axis=1, keepdims=True))
    block = block / jnp.sum(block, axis=1, keepdims=True)
    return block, combine, mask


def slots_kernel(images, tokens_hbm, router_hbm, grad_hbm, sent_ref, *scratch):
    tokens_ref, router_ref, grad_ref, sems = scratch
    first = [
        pltpu.make_async_copy(tokens_hbm, tokens_ref, sems.at[0]),
        pltpu.make_async_copy(router_hbm, router_ref, sems.at[1]),
    ]
    second = [pltpu.make_async_copy(grad_hbm, grad_ref, sems.at[2])]
    for load in first + second:
        load.start()
    for load in first:
        load.wait()
    tokens = tokens_ref[...]
    block, combine, mask = softmaxes(router_ref[...], tokens, images)
    combine_block = jnp.where(mask, spread_rows(combine, images), 0.0)
    slot_in = dot(block.astype(BF16), tokens, 1, 0)
    for load in second:
        load.wait()
    slot_grad = dot(combine_block.astype(BF16), grad_ref[...], 1, 0)
    pairs = pair_rows(slot_in, slot_grad, combine.shape[0])
    for k, i in enumerate(centre_out(pairs.shape[0])):
        sent_ref[k] = pairs[i]


def stage_kernel(win_hbm, wout_hbm, win_ref, wout_ref, sems):
    loads = (
        pltpu.make_async_copy(win_hbm, win_ref, sems.at[0]),
        pltpu.make_async_copy(wout_hbm, wout_ref, sems.at[1]),
    )
    for load in loads:
        load.start()
    for load in loads:
        load.wait()


def expert_kernel(recv_ref, win_ref, wout_ref, back_ref, *, step):
    slots, cotan = split_rows(recv_ref[...])
    out = jnp.zeros(slots.shape, F32)
    back = jnp.zeros(slots.shape, F32)
    for start in range(0, win_ref.shape[1], step):
        w_in = win_ref[:, start : start + step]
        w_out = wout_ref[:, start : start + step]
        value, slope = gelu_pair(dot(slots, w_in, 1, 0))
        pre_grad = dot(cotan, w_out, 1, 0) * slope
        out = out + dot(value.astype(BF16), w_out, 1, 1)
        back = back + dot(pre_grad.astype(BF16), w_in, 1, 1)
    back_ref[...] = pair_rows(out, back, recv_ref.shape[0])


def logits_kernel(
    images, share_order, back_hbm, tokens_ref, router_ref, grad_ref, send_ref, logit_ref, back_ref, sem
):
    load = pltpu.make_async_copy(back_hbm, back_ref, sem)
    load.start()
    tokens = tokens_ref[...]
    dispatch, combine, mask = softmaxes(router_ref[...], tokens, images)
    load.wait()
    slot_out, slot_in_grad = split_rows(in_expert_order(back_ref))
    disp = jnp.where(mask, dot(slot_in_grad, tokens, 1, 1), 0.0)
    comb = fold_rows(jnp.where(mask, dot(slot_out, grad_ref[...], 1, 1), 0.0), images)
    mean = jnp.sum(dispatch * disp, axis=1, keepdims=True)
    from_dispatch = fold_rows(dispatch * (disp - mean), images)
    from_combine = combine * (comb - jnp.sum(combine * comb, axis=0, keepdims=True))
    logit_grad = (from_combine + from_dispatch).astype(BF16)
    logit_ref[...] = logit_grad
    part = dot(logit_grad, tokens, 1, 0)
    devices, _, width = send_ref.shape
    shares = len(share_order)
    for place, share in enumerate(share_order):
        piece = part[:, share * width : (share + 1) * width].astype(BF16)
        for device in range(place, devices, shares):
            send_ref[device] = piece


def tokens_kernel(images, back_ref, tokens_ref, router_ref, logit_ref, out_ref):
    router = router_ref[...]
    dispatch, _, _ = softmaxes(router, tokens_ref[...], images)
    _, slot_in_grad = split_rows(in_expert_order(back_ref))
    out = dot(dispatch.astype(BF16), slot_in_grad, 0, 0)
    out = out + dot(logit_ref[...], router, 0, 0)
    out_ref[...] = out.astype(BF16)


def own_rows(share, rows, row_count):
    shape = (row_count, rows.shape[1])
    row = lax.broadcasted_iota(jnp.int32, shape, 0) + share * row_count
    pick = jnp.where(lax.broadcasted_iota(jnp.int32, shape, 1) == row, 1.0, 0.0)
    return dot(pick.astype(BF16), rows, 1, 1).astype(BF16)


def weights_kernel(count, share_ref, *refs):
    spread, (win_ref, wout_ref, win_hbm, wout_hbm) = refs[:count], refs[count : count + 4]
    rows_ref, win_out, wout_out, load_sems, store_sems = refs[count + 4 :]
    chunks, row_count, step = win_out.shape
    loads = [
        pltpu.make_async_copy(ref, rows_ref.at[k], load_sems.at[k])
        for k, ref in enumerate(spread)
    ]
    for load in loads:
        load.start()
    for load in loads:
        load.wait()
    slots, cotan = split_rows(rows_ref[...].reshape((-1,) + rows_ref.shape[2:]))
    own_slots = own_rows(share_ref[0], slots, row_count)
    own_cotan = own_rows(share_ref[0], cotan, row_count)
    stores = []
    for chunk in range(chunks):
        part = slice(chunk * step, (chunk + 1) * step)
        value, slope = gelu_pair(dot(slots, win_ref[:, part], 1, 0))
        pre_grad = dot(cotan, wout_ref[:, part], 1, 0) * slope
        win_out[chunk] = dot(own_slots, pre_grad.astype(BF16), 1, 0)
        wout_out[chunk] = dot(own_cotan, value.astype(BF16), 1, 0)
        where = (slice(None), pl.ds(chunk * step, step))
        for which, (source, target) in enumerate(((win_out, win_hbm), (wout_out, wout_hbm))):
            store = pltpu.make_async_copy(
                source.at[chunk], target.at[where], store_sems.at[which, chunk]
            )
            store.start()
            stores.append(store)
    for store in stores:
        store.wait()


def long_weights_kernel(share_ref, spread_ref, win_ref, wout_ref, win_out, wout_out, *, step):
    slots, cotan = split_rows(spread_ref[...].reshape((-1,) + spread_ref.shape[2:]))
    own_slots = own_rows(share_ref[0], slots, win_out.shape[0])
    own_cotan = own_rows(share_ref[0], cotan, win_out.shape[0])

    @pl.when(pl.program_id(0) == 0)
    def _():
        win_out[...] = jnp.zeros_like(win_out)
        wout_out[...] = jnp.zeros_like(wout_out)

    for start in range(0, win_ref.shape[1], step):
        part = slice(start, start + step)
        value, slope = gelu_pair(dot(slots, win_ref[:, part], 1, 0))
        pre_grad = dot(cotan, wout_ref[:, part], 1, 0) * slope
        win_out[:, part] += dot(own_slots, pre_grad.astype(BF16), 1, 0)
        wout_out[:, part] += dot(own_cotan, value.astype(BF16), 1, 0)


def on_device(tokens, router, w_in, w_out, out_grad):
    owners, shares = lax.axis_size("expert"), lax.axis_size("dp")
    experts_order = centre_out(owners)
    share_order = [*range(1, shares, 2), *range(0, shares, 2)]
    images, per_image, width = tokens.shape
    experts = router.shape[1]
    hidden = w_in.shape[2]
    columns = images * per_image
    row_count = width // shares
    tokens2 = tokens.reshape(columns, width)
    grad2 = out_grad.reshape(columns, width)
    router_rows = router.T
    w_in2, w_out2 = w_in.reshape(width, hidden), w_out.reshape(width, hidden)
    params = pltpu.CompilerParams(vmem_limit_bytes=VMEM_BYTES)
    whole = pltpu.CompilerParams(vmem_limit_bytes=WHOLE_BYTES)

    def struct(shape, dtype):
        return jax.ShapeDtypeStruct(shape, dtype)

    in_place = pl.BlockSpec(memory_space=pl.ANY)
    sent = pl.pallas_call(
        functools.partial(slots_kernel, images),
        in_specs=[in_place] * 3,
        out_shape=struct((experts, 2 * images, width), BF16),
        scratch_shapes=[
            pltpu.VMEM((columns, width), BF16),
            pltpu.VMEM((experts, width), BF16),
            pltpu.VMEM((columns, width), BF16),
            pltpu.SemaphoreType.DMA((3,)),
        ],
        compiler_params=whole,
        name="slots",
    )(tokens2, router_rows, grad2)
    w_in2, w_out2 = pl.pallas_call(
        stage_kernel,
        in_specs=[in_place] * 2,
        out_specs=[in_place] * 2,
        out_shape=[struct((width, hidden), BF16)] * 2,
        scratch_shapes=[pltpu.SemaphoreType.DMA((2,))],
        compiler_params=pltpu.CompilerParams(vmem_limit_bytes=1024 * 1024),
        cost_estimate=pl.CostEstimate(
            flops=0, bytes_accessed=8 * width * hidden, transcendentals=0
        ),
        name="stage",
    )(w_in2, w_out2)
    recv = exchange(sent, "expert", experts_order)
    back = pl.pallas_call(
        functools.partial(expert_kernel, step=512),
        out_shape=struct(recv.shape, BF16),
        compiler_params=params,
        name="expert",
    )(recv, w_in2, w_out2)
    recv, back = lax.optimization_barrier((recv, back))
    slots_back = exchange(back, "expert", experts_order)
    few = shares * owners * images <= 512
    if few:
        spread = [recv] + [
            lax.ppermute(recv, "dp", [(i, i ^ k) for i in range(shares)])
            for k in range(1, shares)
        ]
    else:
        spread = [lax.all_gather(recv, "dp", axis=0, tiled=False)]

    in_vmem = pl.BlockSpec(memory_space=pltpu.VMEM)
    router_send, logit_grad = pl.pallas_call(
        functools.partial(logits_kernel, images, share_order),
        in_specs=[in_place] + [in_vmem] * 3,
        out_shape=(
            struct((owners * shares, experts, row_count), BF16),
            struct((experts, columns), BF16),
        ),
        scratch_shapes=[pltpu.VMEM(back.shape, BF16), pltpu.SemaphoreType.DMA],
        compiler_params=params,
        name="logits",
    )(slots_back, tokens2, router_rows, grad2)
    share, router_send = lax.optimization_barrier((lax.axis_index("dp").reshape(1), router_send))
    router_parts = exchange(
        router_send,
        ("expert", "dp"),
        [owner * shares + i for owner in experts_order for i in share_order],
    )
    tokens_grad = pl.pallas_call(
        functools.partial(tokens_kernel, images),
        out_shape=struct((columns, width), BF16),
        compiler_params=params,
        name="tokens",
    )(slots_back, tokens2, router_rows, logit_grad)
    in_smem = pl.BlockSpec(memory_space=pltpu.SMEM)
    out_shape = [struct((row_count, hidden), F32)] * 2
    if few:
        chunks, step = hidden // 512, 512
        w_in_grad, w_out_grad = pl.pallas_call(
            functools.partial(weights_kernel, shares),
            in_specs=[in_smem] + [in_place] * shares + [in_vmem] * 2,
            out_specs=[in_place] * 2,
            out_shape=out_shape,
            scratch_shapes=[
                pltpu.VMEM((shares,) + recv.shape, BF16),
                pltpu.VMEM((chunks, row_count, step), F32),
                pltpu.VMEM((chunks, row_count, step), F32),
                pltpu.SemaphoreType.DMA((shares,)),
                pltpu.SemaphoreType.DMA((2, chunks)),
            ],
            compiler_params=params,
            name="weights",
        )(share, *spread, w_in2, w_out2)
    else:
        w_in_grad, w_out_grad = pl.pallas_call(
            functools.partial(long_weights_kernel, step=512),
            grid=(shares,),
            in_specs=[
                in_smem,
                pl.BlockSpec((1,) + recv.shape, lambda i: (i, 0, 0, 0)),
                pl.BlockSpec((width, hidden), lambda i: (0, 0)),
                pl.BlockSpec((width, hidden), lambda i: (0, 0)),
            ],
            out_specs=[pl.BlockSpec((row_count, hidden), lambda i: (0, 0))] * 2,
            out_shape=out_shape,
            compiler_params=params,
            name="weights",
        )(share, *spread, w_in2, w_out2)
    router_grad = jnp.sum(router_parts.astype(F32), axis=0).T
    return (
        tokens_grad.reshape(tokens.shape),
        w_in_grad.reshape(1, row_count, hidden),
        w_out_grad.reshape(1, row_count, hidden),
        router_grad,
    )


def solution(mesh):
    placed = (
        P(("expert", "dp"), None, None),
        P(),
        P("expert", None, None),
        P("expert", None, None),
        P(("expert", "dp"), None, None),
    )
    return jax.shard_map(
        on_device,
        mesh=mesh,
        in_specs=placed,
        out_specs=(
            P(("expert", "dp"), None, None),
            P("expert", "dp", None),
            P("expert", "dp", None),
            P("dp", None),
        ),
        check_vma=False,
    )
```

```python
import functools
import math

import jax
import jax.numpy as jnp
from jax import lax
from jax.experimental import pallas as pl
from jax.experimental.pallas import tpu as pltpu
from jax.sharding import PartitionSpec as P

F32 = jnp.float32
BF16 = jnp.bfloat16
VMEM_BYTES = 24 * 1024 * 1024
WHOLE_BYTES = 56 * 1024 * 1024


def gelu_pair(value):
    coef = math.sqrt(2.0 / math.pi)
    cubic = 0.044715 * coef
    square = value * value
    half = 0.5 * jnp.tanh(value * (coef + cubic * square)) + 0.5
    steep = value * (2.0 * coef + 6.0 * cubic * square) * (1.0 - half)
    return value * half, half + half * steep


def dot(left, right, left_dim, right_dim):
    return lax.dot_general(
        left, right, (((left_dim,), (right_dim,)), ((), ())), preferred_element_type=F32
    )


def own_image(experts, images, columns):
    shape = (experts, images, columns)
    image = lax.broadcasted_iota(jnp.int32, shape, 1)
    token = lax.broadcasted_iota(jnp.int32, shape, 2)
    low = image * (columns // images)
    inside = (token >= low) & (token < low + columns // images)
    return inside.reshape(experts * images, columns)


def spread_rows(compact, images):
    experts, columns = compact.shape
    wide = jnp.broadcast_to(compact[:, None, :], (experts, images, columns))
    return wide.reshape(experts * images, columns)


def fold_rows(block, images):
    rows, columns = block.shape
    return jnp.sum(block.reshape(rows // images, images, columns), axis=1)


def pair_rows(first, second, groups):
    images = first.shape[0] // groups
    first = first.reshape(groups, images, first.shape[1])
    second = second.reshape(groups, images, second.shape[1])
    return jnp.concatenate((first, second), axis=1).astype(BF16)


def split_rows(pairs):
    groups, both, width = pairs.shape
    wide = pairs.astype(F32)
    first = wide[:, : both // 2].reshape(groups * both // 2, width)
    second = wide[:, both // 2 :].reshape(groups * both // 2, width)
    return first.astype(BF16), second.astype(BF16)


def exchange_order(count):
    first = 5 * count // 8
    others = sorted(range(count), key=lambda i: (-abs(2 * i - count + 1), i))
    return [first] + [i for i in others if i != first]


def in_expert_order(ref):
    order = exchange_order(ref.shape[0])
    return jnp.stack([ref[order.index(i)] for i in range(len(order))], axis=0)


def exchange(chunks, axis, order):
    return lax.all_to_all(
        chunks, axis, split_axis=0, concat_axis=0, tiled=True, axis_index_groups=[order]
    )


def softmaxes(router, tokens, images):
    logits = dot(router, tokens, 1, 1)
    experts, columns = logits.shape
    mask = own_image(experts, images, columns)
    combine = jnp.exp(logits - jnp.max(logits, axis=0, keepdims=True))
    combine = combine / jnp.sum(combine, axis=0, keepdims=True)
    block = jnp.where(mask, spread_rows(logits, images), -jnp.inf)
    block = jnp.exp(block - jnp.max(block, axis=1, keepdims=True))
    block = block / jnp.sum(block, axis=1, keepdims=True)
    return block, combine, mask


def slots_kernel(images, tokens_hbm, router_hbm, grad_hbm, sent_ref, *scratch):
    tokens_ref, router_ref, grad_ref, sems = scratch
    first = [
        pltpu.make_async_copy(tokens_hbm, tokens_ref, sems.at[0]),
        pltpu.make_async_copy(router_hbm, router_ref, sems.at[1]),
    ]
    second = [pltpu.make_async_copy(grad_hbm, grad_ref, sems.at[2])]
    for load in first + second:
        load.start()
    for load in first:
        load.wait()
    tokens = tokens_ref[...]
    block, combine, mask = softmaxes(router_ref[...], tokens, images)
    combine_block = jnp.where(mask, spread_rows(combine, images), 0.0)
    slot_in = dot(block.astype(BF16), tokens, 1, 0)
    for load in second:
        load.wait()
    slot_grad = dot(combine_block.astype(BF16), grad_ref[...], 1, 0)
    pairs = pair_rows(slot_in, slot_grad, combine.shape[0])
    for k, i in enumerate(exchange_order(pairs.shape[0])):
        sent_ref[k] = pairs[i]


def stage_kernel(win_hbm, wout_hbm, win_ref, wout_ref, sems):
    loads = (
        pltpu.make_async_copy(win_hbm, win_ref, sems.at[0]),
        pltpu.make_async_copy(wout_hbm, wout_ref, sems.at[1]),
    )
    for load in loads:
        load.start()
    for load in loads:
        load.wait()


def expert_kernel(recv_ref, win_ref, wout_ref, back_ref, *, step):
    slots, cotan = split_rows(recv_ref[...])
    out = jnp.zeros(slots.shape, F32)
    back = jnp.zeros(slots.shape, F32)
    for start in range(0, win_ref.shape[1], step):
        w_in = win_ref[:, start : start + step]
        w_out = wout_ref[:, start : start + step]
        value, slope = gelu_pair(dot(slots, w_in, 1, 0))
        pre_grad = dot(cotan, w_out, 1, 0) * slope
        out = out + dot(value.astype(BF16), w_out, 1, 1)
        back = back + dot(pre_grad.astype(BF16), w_in, 1, 1)
    back_ref[...] = pair_rows(out, back, recv_ref.shape[0])


def logits_kernel(
    images, share_order, back_hbm, tokens_ref, router_ref, grad_ref, send_ref, logit_ref, back_ref, sem
):
    load = pltpu.make_async_copy(back_hbm, back_ref, sem)
    load.start()
    tokens = tokens_ref[...]
    dispatch, combine, mask = softmaxes(router_ref[...], tokens, images)
    load.wait()
    slot_out, slot_in_grad = split_rows(in_expert_order(back_ref))
    disp = jnp.where(mask, dot(slot_in_grad, tokens, 1, 1), 0.0)
    comb = fold_rows(jnp.where(mask, dot(slot_out, grad_ref[...], 1, 1), 0.0), images)
    mean = jnp.sum(dispatch * disp, axis=1, keepdims=True)
    from_dispatch = fold_rows(dispatch * (disp - mean), images)
    from_combine = combine * (comb - jnp.sum(combine * comb, axis=0, keepdims=True))
    logit_grad = (from_combine + from_dispatch).astype(BF16)
    logit_ref[...] = logit_grad
    part = dot(logit_grad, tokens, 1, 0)
    devices, _, width = send_ref.shape
    shares = len(share_order)
    for place, share in enumerate(share_order):
        piece = part[:, share * width : (share + 1) * width].astype(BF16)
        for device in range(place, devices, shares):
            send_ref[device] = piece


def tokens_kernel(images, back_ref, tokens_ref, router_ref, logit_ref, out_ref):
    router = router_ref[...]
    dispatch, _, _ = softmaxes(router, tokens_ref[...], images)
    _, slot_in_grad = split_rows(in_expert_order(back_ref))
    out = dot(dispatch.astype(BF16), slot_in_grad, 0, 0)
    out = out + dot(logit_ref[...], router, 0, 0)
    out_ref[...] = out.astype(BF16)


def own_rows(share, rows, row_count):
    shape = (row_count, rows.shape[1])
    row = lax.broadcasted_iota(jnp.int32, shape, 0) + share * row_count
    pick = jnp.where(lax.broadcasted_iota(jnp.int32, shape, 1) == row, 1.0, 0.0)
    return dot(pick.astype(BF16), rows, 1, 1).astype(BF16)


def weights_kernel(count, share_ref, *refs):
    spread, (win_ref, wout_ref, win_hbm, wout_hbm) = refs[:count], refs[count : count + 4]
    rows_ref, win_out, wout_out, load_sems, store_sems = refs[count + 4 :]
    chunks, row_count, step = win_out.shape
    loads = [
        pltpu.make_async_copy(ref, rows_ref.at[k], load_sems.at[k])
        for k, ref in enumerate(spread)
    ]
    for load in loads:
        load.start()
    for load in loads:
        load.wait()
    slots, cotan = split_rows(rows_ref[...].reshape((-1,) + rows_ref.shape[2:]))
    own_slots = own_rows(share_ref[0], slots, row_count)
    own_cotan = own_rows(share_ref[0], cotan, row_count)
    stores = []
    for chunk in range(chunks):
        part = slice(chunk * step, (chunk + 1) * step)
        value, slope = gelu_pair(dot(slots, win_ref[:, part], 1, 0))
        pre_grad = dot(cotan, wout_ref[:, part], 1, 0) * slope
        win_out[chunk] = dot(own_slots, pre_grad.astype(BF16), 1, 0)
        wout_out[chunk] = dot(own_cotan, value.astype(BF16), 1, 0)
        where = (slice(None), pl.ds(chunk * step, step))
        for which, (source, target) in enumerate(((win_out, win_hbm), (wout_out, wout_hbm))):
            store = pltpu.make_async_copy(
                source.at[chunk], target.at[where], store_sems.at[which, chunk]
            )
            store.start()
            stores.append(store)
    for store in stores:
        store.wait()


def long_weights_kernel(share_ref, spread_ref, win_ref, wout_ref, win_out, wout_out, *, step):
    slots, cotan = split_rows(spread_ref[...].reshape((-1,) + spread_ref.shape[2:]))
    own_slots = own_rows(share_ref[0], slots, win_out.shape[0])
    own_cotan = own_rows(share_ref[0], cotan, win_out.shape[0])

    @pl.when(pl.program_id(0) == 0)
    def _():
        win_out[...] = jnp.zeros_like(win_out)
        wout_out[...] = jnp.zeros_like(wout_out)

    for start in range(0, win_ref.shape[1], step):
        part = slice(start, start + step)
        value, slope = gelu_pair(dot(slots, win_ref[:, part], 1, 0))
        pre_grad = dot(cotan, wout_ref[:, part], 1, 0) * slope
        win_out[:, part] += dot(own_slots, pre_grad.astype(BF16), 1, 0)
        wout_out[:, part] += dot(own_cotan, value.astype(BF16), 1, 0)


def on_device(tokens, router, w_in, w_out, out_grad):
    owners, shares = lax.axis_size("expert"), lax.axis_size("dp")
    experts_order = exchange_order(owners)
    share_order = [*range(1, shares, 2), *range(0, shares, 2)]
    images, per_image, width = tokens.shape
    experts = router.shape[1]
    hidden = w_in.shape[2]
    columns = images * per_image
    row_count = width // shares
    tokens2 = tokens.reshape(columns, width)
    grad2 = out_grad.reshape(columns, width)
    router_rows = router.T
    w_in2, w_out2 = w_in.reshape(width, hidden), w_out.reshape(width, hidden)
    params = pltpu.CompilerParams(vmem_limit_bytes=VMEM_BYTES)
    whole = pltpu.CompilerParams(vmem_limit_bytes=WHOLE_BYTES)

    def struct(shape, dtype):
        return jax.ShapeDtypeStruct(shape, dtype)

    in_place = pl.BlockSpec(memory_space=pl.ANY)
    sent = pl.pallas_call(
        functools.partial(slots_kernel, images),
        in_specs=[in_place] * 3,
        out_shape=struct((experts, 2 * images, width), BF16),
        scratch_shapes=[
            pltpu.VMEM((columns, width), BF16),
            pltpu.VMEM((experts, width), BF16),
            pltpu.VMEM((columns, width), BF16),
            pltpu.SemaphoreType.DMA((3,)),
        ],
        compiler_params=whole,
        name="slots",
    )(tokens2, router_rows, grad2)
    w_in2, w_out2 = pl.pallas_call(
        stage_kernel,
        in_specs=[in_place] * 2,
        out_specs=[in_place] * 2,
        out_shape=[struct((width, hidden), BF16)] * 2,
        scratch_shapes=[pltpu.SemaphoreType.DMA((2,))],
        compiler_params=pltpu.CompilerParams(vmem_limit_bytes=1024 * 1024),
        cost_estimate=pl.CostEstimate(
            flops=0, bytes_accessed=8 * width * hidden, transcendentals=0
        ),
        name="stage",
    )(w_in2, w_out2)
    recv = exchange(sent, "expert", experts_order)
    back = pl.pallas_call(
        functools.partial(expert_kernel, step=512),
        out_shape=struct(recv.shape, BF16),
        compiler_params=params,
        name="expert",
    )(recv, w_in2, w_out2)
    recv, back = lax.optimization_barrier((recv, back))
    slots_back = exchange(back, "expert", experts_order)
    few = shares * owners * images <= 512
    if few:
        spread = [recv] + [
            lax.ppermute(recv, "dp", [(i, i ^ k) for i in range(shares)])
            for k in range(1, shares)
        ]
    else:
        spread = [lax.all_gather(recv, "dp", axis=0, tiled=False)]

    in_vmem = pl.BlockSpec(memory_space=pltpu.VMEM)
    router_send, logit_grad = pl.pallas_call(
        functools.partial(logits_kernel, images, share_order),
        in_specs=[in_place] + [in_vmem] * 3,
        out_shape=(
            struct((owners * shares, experts, row_count), BF16),
            struct((experts, columns), BF16),
        ),
        scratch_shapes=[pltpu.VMEM(back.shape, BF16), pltpu.SemaphoreType.DMA],
        compiler_params=params,
        name="logits",
    )(slots_back, tokens2, router_rows, grad2)
    share, router_send = lax.optimization_barrier((lax.axis_index("dp").reshape(1), router_send))
    router_parts = exchange(
        router_send,
        ("expert", "dp"),
        [owner * shares + i for owner in experts_order for i in share_order],
    )
    tokens_grad = pl.pallas_call(
        functools.partial(tokens_kernel, images),
        out_shape=struct((columns, width), BF16),
        compiler_params=params,
        name="tokens",
    )(slots_back, tokens2, router_rows, logit_grad)
    in_smem = pl.BlockSpec(memory_space=pltpu.SMEM)
    out_shape = [struct((row_count, hidden), F32)] * 2
    if few:
        chunks, step = hidden // 512, 512
        w_in_grad, w_out_grad = pl.pallas_call(
            functools.partial(weights_kernel, shares),
            in_specs=[in_smem] + [in_place] * shares + [in_vmem] * 2,
            out_specs=[in_place] * 2,
            out_shape=out_shape,
            scratch_shapes=[
                pltpu.VMEM((shares,) + recv.shape, BF16),
                pltpu.VMEM((chunks, row_count, step), F32),
                pltpu.VMEM((chunks, row_count, step), F32),
                pltpu.SemaphoreType.DMA((shares,)),
                pltpu.SemaphoreType.DMA((2, chunks)),
            ],
            compiler_params=params,
            name="weights",
        )(share, *spread, w_in2, w_out2)
    else:
        w_in_grad, w_out_grad = pl.pallas_call(
            functools.partial(long_weights_kernel, step=512),
            grid=(shares,),
            in_specs=[
                in_smem,
                pl.BlockSpec((1,) + recv.shape, lambda i: (i, 0, 0, 0)),
                pl.BlockSpec((width, hidden), lambda i: (0, 0)),
                pl.BlockSpec((width, hidden), lambda i: (0, 0)),
            ],
            out_specs=[pl.BlockSpec((row_count, hidden), lambda i: (0, 0))] * 2,
            out_shape=out_shape,
            compiler_params=params,
            name="weights",
        )(share, *spread, w_in2, w_out2)
    router_grad = jnp.sum(router_parts.astype(F32), axis=0).T
    return (
        tokens_grad.reshape(tokens.shape),
        w_in_grad.reshape(1, row_count, hidden),
        w_out_grad.reshape(1, row_count, hidden),
        router_grad,
    )


def solution(mesh):
    placed = (
        P(("expert", "dp"), None, None),
        P(),
        P("expert", None, None),
        P("expert", None, None),
        P(("expert", "dp"), None, None),
    )
    return jax.shard_map(
        on_device,
        mesh=mesh,
        in_specs=placed,
        out_specs=(
            P(("expert", "dp"), None, None),
            P("expert", "dp", None),
            P("expert", "dp", None),
            P("dp", None),
        ),
        check_vma=False,
    )
```

```python
import functools
import math

import jax
import jax.numpy as jnp
from jax import lax
from jax.experimental import pallas as pl
from jax.experimental.pallas import tpu as pltpu
from jax.sharding import PartitionSpec as P

F32 = jnp.float32
BF16 = jnp.bfloat16
VMEM_BYTES = 24 * 1024 * 1024
WHOLE_BYTES = 56 * 1024 * 1024


def gelu_pair(value):
    coef = math.sqrt(2.0 / math.pi)
    cubic = 0.044715 * coef
    square = value * value
    half = 0.5 * jnp.tanh(value * (coef + cubic * square)) + 0.5
    steep = value * (2.0 * coef + 6.0 * cubic * square) * (1.0 - half)
    return value * half, half + half * steep


def dot(left, right, left_dim, right_dim):
    return lax.dot_general(
        left, right, (((left_dim,), (right_dim,)), ((), ())), preferred_element_type=F32
    )


def own_image(experts, images, columns):
    shape = (experts, images, columns)
    image = lax.broadcasted_iota(jnp.int32, shape, 1)
    token = lax.broadcasted_iota(jnp.int32, shape, 2)
    low = image * (columns // images)
    inside = (token >= low) & (token < low + columns // images)
    return inside.reshape(experts * images, columns)


def spread_rows(compact, images):
    experts, columns = compact.shape
    wide = jnp.broadcast_to(compact[:, None, :], (experts, images, columns))
    return wide.reshape(experts * images, columns)


def fold_rows(block, images):
    rows, columns = block.shape
    return jnp.sum(block.reshape(rows // images, images, columns), axis=1)


def pair_rows(first, second, groups):
    images = first.shape[0] // groups
    first = first.reshape(groups, images, first.shape[1])
    second = second.reshape(groups, images, second.shape[1])
    return jnp.concatenate((first, second), axis=1).astype(BF16)


def split_rows(pairs):
    groups, both, width = pairs.shape
    wide = pairs.astype(F32)
    first = wide[:, : both // 2].reshape(groups * both // 2, width)
    second = wide[:, both // 2 :].reshape(groups * both // 2, width)
    return first.astype(BF16), second.astype(BF16)


def centre_out(count):
    return sorted(range(count), key=lambda i: (abs(2 * i - count + 1), i))


def in_expert_order(ref):
    order = centre_out(ref.shape[0])
    return jnp.stack([ref[order.index(i)] for i in range(len(order))], axis=0)


def exchange(chunks, axis, order):
    return lax.all_to_all(
        chunks, axis, split_axis=0, concat_axis=0, tiled=True, axis_index_groups=[order]
    )


def softmaxes(router, tokens, images):
    logits = dot(router, tokens, 1, 1)
    experts, columns = logits.shape
    mask = own_image(experts, images, columns)
    combine = jnp.exp(logits - jnp.max(logits, axis=0, keepdims=True))
    combine = combine / jnp.sum(combine, axis=0, keepdims=True)
    block = jnp.where(mask, spread_rows(logits, images), -jnp.inf)
    block = jnp.exp(block - jnp.max(block, axis=1, keepdims=True))
    block = block / jnp.sum(block, axis=1, keepdims=True)
    return block, combine, mask


def slots_kernel(images, tokens_hbm, router_hbm, grad_hbm, sent_ref, *scratch):
    tokens_ref, router_ref, grad_ref, sems = scratch
    first = [
        pltpu.make_async_copy(tokens_hbm, tokens_ref, sems.at[0]),
        pltpu.make_async_copy(router_hbm, router_ref, sems.at[1]),
    ]
    second = [pltpu.make_async_copy(grad_hbm, grad_ref, sems.at[2])]
    for load in first + second:
        load.start()
    for load in first:
        load.wait()
    tokens = tokens_ref[...]
    block, combine, mask = softmaxes(router_ref[...], tokens, images)
    combine_block = jnp.where(mask, spread_rows(combine, images), 0.0)
    slot_in = dot(block.astype(BF16), tokens, 1, 0)
    for load in second:
        load.wait()
    slot_grad = dot(combine_block.astype(BF16), grad_ref[...], 1, 0)
    pairs = pair_rows(slot_in, slot_grad, combine.shape[0])
    for k, i in enumerate(centre_out(pairs.shape[0])):
        sent_ref[k] = pairs[i]


def stage_kernel(win_hbm, wout_hbm, win_ref, wout_ref, sems):
    loads = (
        pltpu.make_async_copy(win_hbm, win_ref, sems.at[0]),
        pltpu.make_async_copy(wout_hbm, wout_ref, sems.at[1]),
    )
    for load in loads:
        load.start()
    for load in loads:
        load.wait()


def expert_kernel(recv_ref, win_ref, wout_ref, back_ref, *, step):
    slots, cotan = split_rows(recv_ref[...])
    out = jnp.zeros(slots.shape, F32)
    back = jnp.zeros(slots.shape, F32)
    for start in range(0, win_ref.shape[1], step):
        w_in = win_ref[:, start : start + step]
        w_out = wout_ref[:, start : start + step]
        value, slope = gelu_pair(dot(slots, w_in, 1, 0))
        pre_grad = dot(cotan, w_out, 1, 0) * slope
        out = out + dot(value.astype(BF16), w_out, 1, 1)
        back = back + dot(pre_grad.astype(BF16), w_in, 1, 1)
    back_ref[...] = pair_rows(out, back, recv_ref.shape[0])


def logits_kernel(
    images, share_order, back_ref, tokens_ref, router_ref, grad_ref, send_ref, logit_ref
):
    tokens = tokens_ref[...]
    dispatch, combine, mask = softmaxes(router_ref[...], tokens, images)
    slot_out, slot_in_grad = split_rows(in_expert_order(back_ref))
    disp = jnp.where(mask, dot(slot_in_grad, tokens, 1, 1), 0.0)
    comb = fold_rows(jnp.where(mask, dot(slot_out, grad_ref[...], 1, 1), 0.0), images)
    mean = jnp.sum(dispatch * disp, axis=1, keepdims=True)
    from_dispatch = fold_rows(dispatch * (disp - mean), images)
    from_combine = combine * (comb - jnp.sum(combine * comb, axis=0, keepdims=True))
    logit_grad = (from_combine + from_dispatch).astype(BF16)
    logit_ref[...] = logit_grad
    part = dot(logit_grad, tokens, 1, 0)
    devices, _, width = send_ref.shape
    shares = len(share_order)
    for place, share in enumerate(share_order):
        piece = part[:, share * width : (share + 1) * width].astype(BF16)
        for device in range(place, devices, shares):
            send_ref[device] = piece


def tokens_kernel(images, back_ref, tokens_ref, router_ref, logit_ref, out_ref):
    router = router_ref[...]
    dispatch, _, _ = softmaxes(router, tokens_ref[...], images)
    _, slot_in_grad = split_rows(in_expert_order(back_ref))
    out = dot(dispatch.astype(BF16), slot_in_grad, 0, 0)
    out = out + dot(logit_ref[...], router, 0, 0)
    out_ref[...] = out.astype(BF16)


def own_rows(share, rows, row_count):
    shape = (row_count, rows.shape[1])
    row = lax.broadcasted_iota(jnp.int32, shape, 0) + share * row_count
    pick = jnp.where(lax.broadcasted_iota(jnp.int32, shape, 1) == row, 1.0, 0.0)
    return dot(pick.astype(BF16), rows, 1, 1).astype(BF16)


def weights_kernel(count, share_ref, *refs):
    spread, (win_ref, wout_ref, win_hbm, wout_hbm) = refs[:count], refs[count : count + 4]
    rows_ref, win_out, wout_out, load_sems, store_sems = refs[count + 4 :]
    chunks, row_count, step = win_out.shape
    loads = [
        pltpu.make_async_copy(ref, rows_ref.at[k], load_sems.at[k])
        for k, ref in enumerate(spread)
    ]
    for load in loads:
        load.start()
    for load in loads:
        load.wait()
    slots, cotan = split_rows(rows_ref[...].reshape((-1,) + rows_ref.shape[2:]))
    own_slots = own_rows(share_ref[0], slots, row_count)
    own_cotan = own_rows(share_ref[0], cotan, row_count)
    stores = []
    for chunk in range(chunks):
        part = slice(chunk * step, (chunk + 1) * step)
        value, slope = gelu_pair(dot(slots, win_ref[:, part], 1, 0))
        pre_grad = dot(cotan, wout_ref[:, part], 1, 0) * slope
        win_out[chunk] = dot(own_slots, pre_grad.astype(BF16), 1, 0)
        wout_out[chunk] = dot(own_cotan, value.astype(BF16), 1, 0)
        where = (slice(None), pl.ds(chunk * step, step))
        for which, (source, target) in enumerate(((win_out, win_hbm), (wout_out, wout_hbm))):
            store = pltpu.make_async_copy(
                source.at[chunk], target.at[where], store_sems.at[which, chunk]
            )
            store.start()
            stores.append(store)
    for store in stores:
        store.wait()


def long_weights_kernel(share_ref, spread_ref, win_ref, wout_ref, win_out, wout_out, *, step):
    slots, cotan = split_rows(spread_ref[...].reshape((-1,) + spread_ref.shape[2:]))
    own_slots = own_rows(share_ref[0], slots, win_out.shape[0])
    own_cotan = own_rows(share_ref[0], cotan, win_out.shape[0])

    @pl.when(pl.program_id(0) == 0)
    def _():
        win_out[...] = jnp.zeros_like(win_out)
        wout_out[...] = jnp.zeros_like(wout_out)

    for start in range(0, win_ref.shape[1], step):
        part = slice(start, start + step)
        value, slope = gelu_pair(dot(slots, win_ref[:, part], 1, 0))
        pre_grad = dot(cotan, wout_ref[:, part], 1, 0) * slope
        win_out[:, part] += dot(own_slots, pre_grad.astype(BF16), 1, 0)
        wout_out[:, part] += dot(own_cotan, value.astype(BF16), 1, 0)


def on_device(tokens, router, w_in, w_out, out_grad):
    owners, shares = lax.axis_size("expert"), lax.axis_size("dp")
    experts_order = centre_out(owners)
    share_order = [*range(1, shares, 2), *range(0, shares, 2)]
    images, per_image, width = tokens.shape
    experts = router.shape[1]
    hidden = w_in.shape[2]
    columns = images * per_image
    row_count = width // shares
    tokens2 = tokens.reshape(columns, width)
    grad2 = out_grad.reshape(columns, width)
    router_rows = router.T
    w_in2, w_out2 = w_in.reshape(width, hidden), w_out.reshape(width, hidden)
    params = pltpu.CompilerParams(vmem_limit_bytes=VMEM_BYTES)
    whole = pltpu.CompilerParams(vmem_limit_bytes=WHOLE_BYTES)

    def struct(shape, dtype):
        return jax.ShapeDtypeStruct(shape, dtype)

    in_place = pl.BlockSpec(memory_space=pl.ANY)
    sent = pl.pallas_call(
        functools.partial(slots_kernel, images),
        in_specs=[in_place] * 3,
        out_shape=struct((experts, 2 * images, width), BF16),
        scratch_shapes=[
            pltpu.VMEM((columns, width), BF16),
            pltpu.VMEM((experts, width), BF16),
            pltpu.VMEM((columns, width), BF16),
            pltpu.SemaphoreType.DMA((3,)),
        ],
        compiler_params=whole,
        name="slots",
    )(tokens2, router_rows, grad2)
    w_in2, w_out2 = pl.pallas_call(
        stage_kernel,
        in_specs=[in_place] * 2,
        out_specs=[in_place] * 2,
        out_shape=[struct((width, hidden), BF16)] * 2,
        scratch_shapes=[pltpu.SemaphoreType.DMA((2,))],
        compiler_params=pltpu.CompilerParams(vmem_limit_bytes=1024 * 1024),
        cost_estimate=pl.CostEstimate(
            flops=0, bytes_accessed=8 * width * hidden, transcendentals=0
        ),
        name="stage",
    )(w_in2, w_out2)
    recv = exchange(sent, "expert", experts_order)
    back = pl.pallas_call(
        functools.partial(expert_kernel, step=512),
        out_shape=struct(recv.shape, BF16),
        compiler_params=params,
        name="expert",
    )(recv, w_in2, w_out2)
    recv, back = lax.optimization_barrier((recv, back))
    slots_back = exchange(back, "expert", experts_order)
    few = shares * owners * images <= 512
    if few:
        spread = [recv] + [
            lax.ppermute(recv, "dp", [(i, i ^ k) for i in range(shares)])
            for k in range(1, shares)
        ]
    else:
        spread = [lax.all_gather(recv, "dp", axis=0, tiled=False)]

    in_vmem = pl.BlockSpec(memory_space=pltpu.VMEM)
    router_send, logit_grad = pl.pallas_call(
        functools.partial(logits_kernel, images, share_order),
        in_specs=[in_vmem] * 4,
        out_shape=(
            struct((owners * shares, experts, row_count), BF16),
            struct((experts, columns), BF16),
        ),
        compiler_params=params,
        name="logits",
    )(slots_back, tokens2, router_rows, grad2)
    share, router_send = lax.optimization_barrier((lax.axis_index("dp").reshape(1), router_send))
    router_parts = exchange(
        router_send,
        ("expert", "dp"),
        [owner * shares + i for owner in experts_order for i in share_order],
    )
    tokens_grad = pl.pallas_call(
        functools.partial(tokens_kernel, images),
        out_shape=struct((columns, width), BF16),
        compiler_params=params,
        name="tokens",
    )(slots_back, tokens2, router_rows, logit_grad)
    in_smem = pl.BlockSpec(memory_space=pltpu.SMEM)
    out_shape = [struct((row_count, hidden), F32)] * 2
    if few:
        chunks, step = hidden // 512, 512
        w_in_grad, w_out_grad = pl.pallas_call(
            functools.partial(weights_kernel, shares),
            in_specs=[in_smem] + [in_place] * shares + [in_vmem] * 2,
            out_specs=[in_place] * 2,
            out_shape=out_shape,
            scratch_shapes=[
                pltpu.VMEM((shares,) + recv.shape, BF16),
                pltpu.VMEM((chunks, row_count, step), F32),
                pltpu.VMEM((chunks, row_count, step), F32),
                pltpu.SemaphoreType.DMA((shares,)),
                pltpu.SemaphoreType.DMA((2, chunks)),
            ],
            compiler_params=params,
            name="weights",
        )(share, *spread, w_in2, w_out2)
    else:
        w_in_grad, w_out_grad = pl.pallas_call(
            functools.partial(long_weights_kernel, step=512),
            grid=(shares,),
            in_specs=[
                in_smem,
                pl.BlockSpec((1,) + recv.shape, lambda i: (i, 0, 0, 0)),
                pl.BlockSpec((width, hidden), lambda i: (0, 0)),
                pl.BlockSpec((width, hidden), lambda i: (0, 0)),
            ],
            out_specs=[pl.BlockSpec((row_count, hidden), lambda i: (0, 0))] * 2,
            out_shape=out_shape,
            compiler_params=params,
            name="weights",
        )(share, *spread, w_in2, w_out2)
    router_grad = jnp.sum(router_parts.astype(F32), axis=0).T
    return (
        tokens_grad.reshape(tokens.shape),
        w_in_grad.reshape(1, row_count, hidden),
        w_out_grad.reshape(1, row_count, hidden),
        router_grad,
    )


def solution(mesh):
    placed = (
        P(("expert", "dp"), None, None),
        P(),
        P("expert", None, None),
        P("expert", None, None),
        P(("expert", "dp"), None, None),
    )
    return jax.shard_map(
        on_device,
        mesh=mesh,
        in_specs=placed,
        out_specs=(
            P(("expert", "dp"), None, None),
            P("expert", "dp", None),
            P("expert", "dp", None),
            P("dp", None),
        ),
        check_vma=False,
    )
```

```python
import functools
import math

import jax
import jax.numpy as jnp
from jax import lax
from jax.experimental import pallas as pl
from jax.experimental.pallas import tpu as pltpu
from jax.sharding import PartitionSpec as P

F32 = jnp.float32
BF16 = jnp.bfloat16
VMEM_BYTES = 24 * 1024 * 1024
WHOLE_BYTES = 56 * 1024 * 1024


def gelu_pair(value):
    coef = math.sqrt(2.0 / math.pi)
    cubic = 0.044715 * coef
    square = value * value
    half = 0.5 * jnp.tanh(value * (coef + cubic * square)) + 0.5
    steep = value * (2.0 * coef + 6.0 * cubic * square) * (1.0 - half)
    return value * half, half + half * steep


def dot(left, right, left_dim, right_dim):
    return lax.dot_general(
        left, right, (((left_dim,), (right_dim,)), ((), ())), preferred_element_type=F32
    )


def own_image(experts, images, columns):
    shape = (experts, images, columns)
    image = lax.broadcasted_iota(jnp.int32, shape, 1)
    token = lax.broadcasted_iota(jnp.int32, shape, 2)
    low = image * (columns // images)
    inside = (token >= low) & (token < low + columns // images)
    return inside.reshape(experts * images, columns)


def spread_rows(compact, images):
    experts, columns = compact.shape
    wide = jnp.broadcast_to(compact[:, None, :], (experts, images, columns))
    return wide.reshape(experts * images, columns)


def fold_rows(block, images):
    rows, columns = block.shape
    return jnp.sum(block.reshape(rows // images, images, columns), axis=1)


def pair_rows(first, second, groups):
    images = first.shape[0] // groups
    first = first.reshape(groups, images, first.shape[1])
    second = second.reshape(groups, images, second.shape[1])
    return jnp.concatenate((first, second), axis=1).astype(BF16)


def split_rows(pairs):
    groups, both, width = pairs.shape
    wide = pairs.astype(F32)
    first = wide[:, : both // 2].reshape(groups * both // 2, width)
    second = wide[:, both // 2 :].reshape(groups * both // 2, width)
    return first.astype(BF16), second.astype(BF16)


def centre_out(count):
    return sorted(range(count), key=lambda i: (abs(2 * i - count + 1), i))


def in_expert_order(ref):
    order = centre_out(ref.shape[0])
    return jnp.stack([ref[order.index(i)] for i in range(len(order))], axis=0)


def exchange(chunks, axis, order):
    return lax.all_to_all(
        chunks, axis, split_axis=0, concat_axis=0, tiled=True, axis_index_groups=[order]
    )


def softmaxes(router, tokens, images):
    logits = dot(router, tokens, 1, 1)
    experts, columns = logits.shape
    mask = own_image(experts, images, columns)
    combine = jnp.exp(logits - jnp.max(logits, axis=0, keepdims=True))
    combine = combine / jnp.sum(combine, axis=0, keepdims=True)
    block = jnp.where(mask, spread_rows(logits, images), -jnp.inf)
    block = jnp.exp(block - jnp.max(block, axis=1, keepdims=True))
    block = block / jnp.sum(block, axis=1, keepdims=True)
    return block, combine, mask


def slots_kernel(images, tokens_hbm, router_hbm, grad_hbm, sent_ref, *scratch):
    tokens_ref, router_ref, grad_ref, sems = scratch
    loads = [
        pltpu.make_async_copy(source, target, sems.at[i])
        for i, (source, target) in enumerate(
            ((tokens_hbm, tokens_ref), (router_hbm, router_ref), (grad_hbm, grad_ref))
        )
    ]
    for load in loads:
        load.start()
    for load in loads:
        load.wait()
    tokens = tokens_ref[...]
    block, combine, mask = softmaxes(router_ref[...], tokens, images)
    combine_block = jnp.where(mask, spread_rows(combine, images), 0.0)
    slot_in = dot(block.astype(BF16), tokens, 1, 0)
    slot_grad = dot(combine_block.astype(BF16), grad_ref[...], 1, 0)
    pairs = pair_rows(slot_in, slot_grad, combine.shape[0])
    for k, i in enumerate(centre_out(pairs.shape[0])):
        sent_ref[k] = pairs[i]


def stage_kernel(win_hbm, wout_hbm, win_ref, wout_ref, sems):
    loads = (
        pltpu.make_async_copy(win_hbm, win_ref, sems.at[0]),
        pltpu.make_async_copy(wout_hbm, wout_ref, sems.at[1]),
    )
    for load in loads:
        load.start()
    for load in loads:
        load.wait()


def expert_kernel(recv_ref, win_ref, wout_ref, back_ref, *, step):
    slots, cotan = split_rows(recv_ref[...])
    out = jnp.zeros(slots.shape, F32)
    back = jnp.zeros(slots.shape, F32)
    for start in range(0, win_ref.shape[1], step):
        w_in = win_ref[:, start : start + step]
        w_out = wout_ref[:, start : start + step]
        value, slope = gelu_pair(dot(slots, w_in, 1, 0))
        pre_grad = dot(cotan, w_out, 1, 0) * slope
        out = out + dot(value.astype(BF16), w_out, 1, 1)
        back = back + dot(pre_grad.astype(BF16), w_in, 1, 1)
    back_ref[...] = pair_rows(out, back, recv_ref.shape[0])


def logits_kernel(
    images, share_order, back_ref, tokens_ref, router_ref, grad_ref, send_ref, logit_ref
):
    tokens = tokens_ref[...]
    dispatch, combine, mask = softmaxes(router_ref[...], tokens, images)
    slot_out, slot_in_grad = split_rows(in_expert_order(back_ref))
    disp = jnp.where(mask, dot(slot_in_grad, tokens, 1, 1), 0.0)
    comb = fold_rows(jnp.where(mask, dot(slot_out, grad_ref[...], 1, 1), 0.0), images)
    mean = jnp.sum(dispatch * disp, axis=1, keepdims=True)
    from_dispatch = fold_rows(dispatch * (disp - mean), images)
    from_combine = combine * (comb - jnp.sum(combine * comb, axis=0, keepdims=True))
    logit_grad = (from_combine + from_dispatch).astype(BF16)
    logit_ref[...] = logit_grad
    part = dot(logit_grad, tokens, 1, 0)
    devices, _, width = send_ref.shape
    shares = len(share_order)
    for place, share in enumerate(share_order):
        piece = part[:, share * width : (share + 1) * width].astype(BF16)
        for device in range(place, devices, shares):
            send_ref[device] = piece


def tokens_kernel(images, back_ref, tokens_ref, router_ref, logit_ref, out_ref):
    router = router_ref[...]
    dispatch, _, _ = softmaxes(router, tokens_ref[...], images)
    _, slot_in_grad = split_rows(in_expert_order(back_ref))
    out = dot(dispatch.astype(BF16), slot_in_grad, 0, 0)
    out = out + dot(logit_ref[...], router, 0, 0)
    out_ref[...] = out.astype(BF16)


def own_rows(share, rows, row_count):
    shape = (row_count, rows.shape[1])
    row = lax.broadcasted_iota(jnp.int32, shape, 0) + share * row_count
    pick = jnp.where(lax.broadcasted_iota(jnp.int32, shape, 1) == row, 1.0, 0.0)
    return dot(pick.astype(BF16), rows, 1, 1).astype(BF16)


def weights_kernel(count, share_ref, *refs):
    spread, (win_ref, wout_ref, win_hbm, wout_hbm) = refs[:count], refs[count : count + 4]
    rows_ref, win_out, wout_out, load_sems, store_sems = refs[count + 4 :]
    chunks, row_count, step = win_out.shape
    loads = [
        pltpu.make_async_copy(ref, rows_ref.at[k], load_sems.at[k])
        for k, ref in enumerate(spread)
    ]
    for load in loads:
        load.start()
    for load in loads:
        load.wait()
    slots, cotan = split_rows(rows_ref[...].reshape((-1,) + rows_ref.shape[2:]))
    own_slots = own_rows(share_ref[0], slots, row_count)
    own_cotan = own_rows(share_ref[0], cotan, row_count)
    stores = []
    for chunk in range(chunks):
        part = slice(chunk * step, (chunk + 1) * step)
        value, slope = gelu_pair(dot(slots, win_ref[:, part], 1, 0))
        pre_grad = dot(cotan, wout_ref[:, part], 1, 0) * slope
        win_out[chunk] = dot(own_slots, pre_grad.astype(BF16), 1, 0)
        wout_out[chunk] = dot(own_cotan, value.astype(BF16), 1, 0)
        where = (slice(None), pl.ds(chunk * step, step))
        for which, (source, target) in enumerate(((win_out, win_hbm), (wout_out, wout_hbm))):
            store = pltpu.make_async_copy(
                source.at[chunk], target.at[where], store_sems.at[which, chunk]
            )
            store.start()
            stores.append(store)
    for store in stores:
        store.wait()


def long_weights_kernel(share_ref, spread_ref, win_ref, wout_ref, win_out, wout_out, *, step):
    slots, cotan = split_rows(spread_ref[...].reshape((-1,) + spread_ref.shape[2:]))
    own_slots = own_rows(share_ref[0], slots, win_out.shape[0])
    own_cotan = own_rows(share_ref[0], cotan, win_out.shape[0])

    @pl.when(pl.program_id(0) == 0)
    def _():
        win_out[...] = jnp.zeros_like(win_out)
        wout_out[...] = jnp.zeros_like(wout_out)

    for start in range(0, win_ref.shape[1], step):
        part = slice(start, start + step)
        value, slope = gelu_pair(dot(slots, win_ref[:, part], 1, 0))
        pre_grad = dot(cotan, wout_ref[:, part], 1, 0) * slope
        win_out[:, part] += dot(own_slots, pre_grad.astype(BF16), 1, 0)
        wout_out[:, part] += dot(own_cotan, value.astype(BF16), 1, 0)


def on_device(tokens, router, w_in, w_out, out_grad):
    owners, shares = lax.axis_size("expert"), lax.axis_size("dp")
    experts_order = centre_out(owners)
    share_order = [*range(1, shares, 2), *range(0, shares, 2)]
    images, per_image, width = tokens.shape
    experts = router.shape[1]
    hidden = w_in.shape[2]
    columns = images * per_image
    row_count = width // shares
    tokens2 = tokens.reshape(columns, width)
    grad2 = out_grad.reshape(columns, width)
    router_rows = router.T
    w_in2, w_out2 = w_in.reshape(width, hidden), w_out.reshape(width, hidden)
    params = pltpu.CompilerParams(vmem_limit_bytes=VMEM_BYTES)
    whole = pltpu.CompilerParams(vmem_limit_bytes=WHOLE_BYTES)

    def struct(shape, dtype):
        return jax.ShapeDtypeStruct(shape, dtype)

    in_place = pl.BlockSpec(memory_space=pl.ANY)
    in_vmem = pl.BlockSpec(memory_space=pltpu.VMEM)
    sent = pl.pallas_call(
        functools.partial(slots_kernel, images),
        in_specs=[in_place] * 3,
        out_specs=in_vmem,
        out_shape=struct((experts, 2 * images, width), BF16),
        scratch_shapes=[
            pltpu.VMEM((columns, width), BF16),
            pltpu.VMEM((experts, width), BF16),
            pltpu.VMEM((columns, width), BF16),
            pltpu.SemaphoreType.DMA((3,)),
        ],
        compiler_params=whole,
        name="slots",
    )(tokens2, router_rows, grad2)
    w_in2, w_out2 = pl.pallas_call(
        stage_kernel,
        in_specs=[in_place] * 2,
        out_specs=[in_place] * 2,
        out_shape=[struct((width, hidden), BF16)] * 2,
        scratch_shapes=[pltpu.SemaphoreType.DMA((2,))],
        compiler_params=pltpu.CompilerParams(vmem_limit_bytes=1024 * 1024),
        cost_estimate=pl.CostEstimate(
            flops=0, bytes_accessed=8 * width * hidden, transcendentals=0
        ),
        name="stage",
    )(w_in2, w_out2)
    recv = exchange(sent, "expert", experts_order)
    back = pl.pallas_call(
        functools.partial(expert_kernel, step=512),
        in_specs=[in_vmem] * 3,
        out_specs=in_vmem,
        out_shape=struct(recv.shape, BF16),
        compiler_params=params,
        name="expert",
    )(recv, w_in2, w_out2)
    recv, back = lax.optimization_barrier((recv, back))
    slots_back = exchange(back, "expert", experts_order)
    few = shares * owners * images <= 512
    if few:
        spread = [recv] + [
            lax.ppermute(recv, "dp", [(i, i ^ k) for i in range(shares)])
            for k in range(1, shares)
        ]
    else:
        spread = [lax.all_gather(recv, "dp", axis=0, tiled=False)]

    router_send, logit_grad = pl.pallas_call(
        functools.partial(logits_kernel, images, share_order),
        in_specs=[in_vmem] * 4,
        out_specs=(in_vmem, in_vmem),
        out_shape=(
            struct((owners * shares, experts, row_count), BF16),
            struct((experts, columns), BF16),
        ),
        compiler_params=params,
        name="logits",
    )(slots_back, tokens2, router_rows, grad2)
    share, router_send = lax.optimization_barrier((lax.axis_index("dp").reshape(1), router_send))
    router_parts = exchange(
        router_send,
        ("expert", "dp"),
        [owner * shares + i for owner in experts_order for i in share_order],
    )
    tokens_grad = pl.pallas_call(
        functools.partial(tokens_kernel, images),
        in_specs=[in_vmem] * 4,
        out_specs=in_vmem,
        out_shape=struct((columns, width), BF16),
        compiler_params=params,
        name="tokens",
    )(slots_back, tokens2, router_rows, logit_grad)
    in_smem = pl.BlockSpec(memory_space=pltpu.SMEM)
    out_shape = [struct((row_count, hidden), F32)] * 2
    if few:
        chunks, step = hidden // 512, 512
        w_in_grad, w_out_grad = pl.pallas_call(
            functools.partial(weights_kernel, shares),
            in_specs=[in_smem] + [in_place] * shares + [in_vmem] * 2,
            out_specs=[in_place] * 2,
            out_shape=out_shape,
            scratch_shapes=[
                pltpu.VMEM((shares,) + recv.shape, BF16),
                pltpu.VMEM((chunks, row_count, step), F32),
                pltpu.VMEM((chunks, row_count, step), F32),
                pltpu.SemaphoreType.DMA((shares,)),
                pltpu.SemaphoreType.DMA((2, chunks)),
            ],
            compiler_params=params,
            name="weights",
        )(share, *spread, w_in2, w_out2)
    else:
        w_in_grad, w_out_grad = pl.pallas_call(
            functools.partial(long_weights_kernel, step=512),
            grid=(shares,),
            in_specs=[
                in_smem,
                pl.BlockSpec((1,) + recv.shape, lambda i: (i, 0, 0, 0)),
                pl.BlockSpec((width, hidden), lambda i: (0, 0)),
                pl.BlockSpec((width, hidden), lambda i: (0, 0)),
            ],
            out_specs=[pl.BlockSpec((row_count, hidden), lambda i: (0, 0))] * 2,
            out_shape=out_shape,
            compiler_params=params,
            name="weights",
        )(share, *spread, w_in2, w_out2)
    router_grad = jnp.sum(router_parts.astype(F32), axis=0).T
    return (
        tokens_grad.reshape(tokens.shape),
        w_in_grad.reshape(1, row_count, hidden),
        w_out_grad.reshape(1, row_count, hidden),
        router_grad,
    )


def solution(mesh):
    placed = (
        P(("expert", "dp"), None, None),
        P(),
        P("expert", None, None),
        P("expert", None, None),
        P(("expert", "dp"), None, None),
    )
    return jax.shard_map(
        on_device,
        mesh=mesh,
        in_specs=placed,
        out_specs=(
            P(("expert", "dp"), None, None),
            P("expert", "dp", None),
            P("expert", "dp", None),
            P("dp", None),
        ),
        check_vma=False,
    )
```

```python
import functools
import math

import jax
import jax.numpy as jnp
from jax import lax
from jax.experimental import pallas as pl
from jax.experimental.pallas import tpu as pltpu
from jax.sharding import PartitionSpec as P

F32 = jnp.float32
BF16 = jnp.bfloat16
VMEM_BYTES = 24 * 1024 * 1024
WHOLE_BYTES = 56 * 1024 * 1024


def gelu_pair(value):
    coef = math.sqrt(2.0 / math.pi)
    cubic = 0.044715 * coef
    square = value * value
    half = 0.5 * jnp.tanh(value * (coef + cubic * square)) + 0.5
    steep = value * (2.0 * coef + 6.0 * cubic * square) * (1.0 - half)
    return value * half, half + half * steep


def dot(left, right, left_dim, right_dim):
    return lax.dot_general(
        left, right, (((left_dim,), (right_dim,)), ((), ())), preferred_element_type=F32
    )


def own_image(experts, images, columns):
    shape = (experts, images, columns)
    image = lax.broadcasted_iota(jnp.int32, shape, 1)
    token = lax.broadcasted_iota(jnp.int32, shape, 2)
    low = image * (columns // images)
    inside = (token >= low) & (token < low + columns // images)
    return inside.reshape(experts * images, columns)


def spread_rows(compact, images):
    experts, columns = compact.shape
    wide = jnp.broadcast_to(compact[:, None, :], (experts, images, columns))
    return wide.reshape(experts * images, columns)


def fold_rows(block, images):
    rows, columns = block.shape
    return jnp.sum(block.reshape(rows // images, images, columns), axis=1)


def pair_rows(first, second, groups):
    images = first.shape[0] // groups
    first = first.reshape(groups, images, first.shape[1])
    second = second.reshape(groups, images, second.shape[1])
    return jnp.concatenate((first, second), axis=1).astype(BF16)


def split_rows(pairs):
    groups, both, width = pairs.shape
    wide = pairs.astype(F32)
    first = wide[:, : both // 2].reshape(groups * both // 2, width)
    second = wide[:, both // 2 :].reshape(groups * both // 2, width)
    return first.astype(BF16), second.astype(BF16)


def centre_out(count):
    return sorted(range(count), key=lambda i: (abs(2 * i - count + 1), i))


def in_expert_order(ref):
    order = centre_out(ref.shape[0])
    return jnp.stack([ref[order.index(i)] for i in range(len(order))], axis=0)


def exchange(chunks, axis, order):
    return lax.all_to_all(
        chunks, axis, split_axis=0, concat_axis=0, tiled=True, axis_index_groups=[order]
    )


def softmaxes(router, tokens, images):
    logits = dot(router, tokens, 1, 1)
    experts, columns = logits.shape
    mask = own_image(experts, images, columns)
    combine = jnp.exp(logits - jnp.max(logits, axis=0, keepdims=True))
    combine = combine / jnp.sum(combine, axis=0, keepdims=True)
    block = jnp.where(mask, spread_rows(logits, images), -jnp.inf)
    block = jnp.exp(block - jnp.max(block, axis=1, keepdims=True))
    block = block * (1.0 / jnp.sum(block, axis=1, keepdims=True))
    return block, combine, mask


def slots_kernel(images, tokens_hbm, router_hbm, grad_hbm, sent_ref, *scratch):
    tokens_ref, router_ref, grad_ref, sems = scratch
    first = [
        pltpu.make_async_copy(tokens_hbm, tokens_ref, sems.at[0]),
        pltpu.make_async_copy(router_hbm, router_ref, sems.at[1]),
    ]
    second = [pltpu.make_async_copy(grad_hbm, grad_ref, sems.at[2])]
    for load in first + second:
        load.start()
    for load in first:
        load.wait()
    tokens = tokens_ref[...]
    block, combine, mask = softmaxes(router_ref[...], tokens, images)
    combine_block = jnp.where(mask, spread_rows(combine, images), 0.0)
    slot_in = dot(block.astype(BF16), tokens, 1, 0)
    for load in second:
        load.wait()
    slot_grad = dot(combine_block.astype(BF16), grad_ref[...], 1, 0)
    pairs = pair_rows(slot_in, slot_grad, combine.shape[0])
    for k, i in enumerate(centre_out(pairs.shape[0])):
        sent_ref[k] = pairs[i]


def stage_kernel(win_hbm, wout_hbm, win_ref, wout_ref, sems):
    loads = (
        pltpu.make_async_copy(win_hbm, win_ref, sems.at[0]),
        pltpu.make_async_copy(wout_hbm, wout_ref, sems.at[1]),
    )
    for load in loads:
        load.start()
    for load in loads:
        load.wait()


def expert_kernel(recv_ref, win_ref, wout_ref, back_ref, *, step):
    slots, cotan = split_rows(recv_ref[...])
    out = jnp.zeros(slots.shape, F32)
    back = jnp.zeros(slots.shape, F32)
    for start in range(0, win_ref.shape[1], step):
        w_in = win_ref[:, start : start + step]
        w_out = wout_ref[:, start : start + step]
        value, slope = gelu_pair(dot(slots, w_in, 1, 0))
        pre_grad = dot(cotan, w_out, 1, 0) * slope
        out = out + dot(value.astype(BF16), w_out, 1, 1)
        back = back + dot(pre_grad.astype(BF16), w_in, 1, 1)
    back_ref[...] = pair_rows(out, back, recv_ref.shape[0])


def logits_kernel(
    images, share_order, back_ref, tokens_ref, router_ref, grad_ref, send_ref, logit_ref
):
    tokens = tokens_ref[...]
    dispatch, combine, mask = softmaxes(router_ref[...], tokens, images)
    slot_out, slot_in_grad = split_rows(in_expert_order(back_ref))
    disp = dot(slot_in_grad, tokens, 1, 1)
    comb = fold_rows(jnp.where(mask, dot(slot_out, grad_ref[...], 1, 1), 0.0), images)
    mean = jnp.sum(dispatch * disp, axis=1, keepdims=True)
    from_dispatch = fold_rows(dispatch * (disp - mean), images)
    from_combine = combine * (comb - jnp.sum(combine * comb, axis=0, keepdims=True))
    logit_grad = (from_combine + from_dispatch).astype(BF16)
    logit_ref[...] = logit_grad
    part = dot(logit_grad, tokens, 1, 0)
    devices, _, width = send_ref.shape
    shares = len(share_order)
    for place, share in enumerate(share_order):
        piece = part[:, share * width : (share + 1) * width].astype(BF16)
        for device in range(place, devices, shares):
            send_ref[device] = piece


def tokens_kernel(images, back_ref, tokens_ref, router_ref, logit_ref, out_ref):
    router = router_ref[...]
    dispatch, _, _ = softmaxes(router, tokens_ref[...], images)
    _, slot_in_grad = split_rows(in_expert_order(back_ref))
    out = dot(dispatch.astype(BF16), slot_in_grad, 0, 0)
    out = out + dot(logit_ref[...], router, 0, 0)
    out_ref[...] = out.astype(BF16)


def own_rows(share, rows, row_count):
    shape = (row_count, rows.shape[1])
    row = lax.broadcasted_iota(jnp.int32, shape, 0) + share * row_count
    pick = jnp.where(lax.broadcasted_iota(jnp.int32, shape, 1) == row, 1.0, 0.0)
    return dot(pick.astype(BF16), rows, 1, 1).astype(BF16)


def weights_kernel(count, share_ref, *refs):
    spread, (win_ref, wout_ref, win_hbm, wout_hbm) = refs[:count], refs[count : count + 4]
    rows_ref, win_out, wout_out, load_sems, store_sems = refs[count + 4 :]
    chunks, row_count, step = win_out.shape
    loads = [
        pltpu.make_async_copy(ref, rows_ref.at[k], load_sems.at[k])
        for k, ref in enumerate(spread)
    ]
    for load in loads:
        load.start()
    for load in loads:
        load.wait()
    slots, cotan = split_rows(rows_ref[...].reshape((-1,) + rows_ref.shape[2:]))
    own_slots = own_rows(share_ref[0], slots, row_count)
    own_cotan = own_rows(share_ref[0], cotan, row_count)
    stores = []
    for chunk in range(chunks):
        part = slice(chunk * step, (chunk + 1) * step)
        value, slope = gelu_pair(dot(slots, win_ref[:, part], 1, 0))
        pre_grad = dot(cotan, wout_ref[:, part], 1, 0) * slope
        win_out[chunk] = dot(own_slots, pre_grad.astype(BF16), 1, 0)
        wout_out[chunk] = dot(own_cotan, value.astype(BF16), 1, 0)
        where = (slice(None), pl.ds(chunk * step, step))
        for which, (source, target) in enumerate(((win_out, win_hbm), (wout_out, wout_hbm))):
            store = pltpu.make_async_copy(
                source.at[chunk], target.at[where], store_sems.at[which, chunk]
            )
            store.start()
            stores.append(store)
    for store in stores:
        store.wait()


def long_weights_kernel(share_ref, spread_ref, win_ref, wout_ref, win_out, wout_out, *, step):
    slots, cotan = split_rows(spread_ref[...].reshape((-1,) + spread_ref.shape[2:]))
    own_slots = own_rows(share_ref[0], slots, win_out.shape[0])
    own_cotan = own_rows(share_ref[0], cotan, win_out.shape[0])

    @pl.when(pl.program_id(0) == 0)
    def _():
        win_out[...] = jnp.zeros_like(win_out)
        wout_out[...] = jnp.zeros_like(wout_out)

    for start in range(0, win_ref.shape[1], step):
        part = slice(start, start + step)
        value, slope = gelu_pair(dot(slots, win_ref[:, part], 1, 0))
        pre_grad = dot(cotan, wout_ref[:, part], 1, 0) * slope
        win_out[:, part] += dot(own_slots, pre_grad.astype(BF16), 1, 0)
        wout_out[:, part] += dot(own_cotan, value.astype(BF16), 1, 0)


def on_device(tokens, router, w_in, w_out, out_grad):
    owners, shares = lax.axis_size("expert"), lax.axis_size("dp")
    experts_order = centre_out(owners)
    share_order = [*range(1, shares, 2), *range(0, shares, 2)]
    images, per_image, width = tokens.shape
    experts = router.shape[1]
    hidden = w_in.shape[2]
    columns = images * per_image
    row_count = width // shares
    tokens2 = tokens.reshape(columns, width)
    grad2 = out_grad.reshape(columns, width)
    router_rows = router.T
    w_in2, w_out2 = w_in.reshape(width, hidden), w_out.reshape(width, hidden)
    params = pltpu.CompilerParams(vmem_limit_bytes=VMEM_BYTES)
    whole = pltpu.CompilerParams(vmem_limit_bytes=WHOLE_BYTES)

    def struct(shape, dtype):
        return jax.ShapeDtypeStruct(shape, dtype)

    in_place = pl.BlockSpec(memory_space=pl.ANY)
    sent = pl.pallas_call(
        functools.partial(slots_kernel, images),
        in_specs=[in_place] * 3,
        out_shape=struct((experts, 2 * images, width), BF16),
        scratch_shapes=[
            pltpu.VMEM((columns, width), BF16),
            pltpu.VMEM((experts, width), BF16),
            pltpu.VMEM((columns, width), BF16),
            pltpu.SemaphoreType.DMA((3,)),
        ],
        compiler_params=whole,
        name="slots",
    )(tokens2, router_rows, grad2)
    w_in2, w_out2 = pl.pallas_call(
        stage_kernel,
        in_specs=[in_place] * 2,
        out_specs=[in_place] * 2,
        out_shape=[struct((width, hidden), BF16)] * 2,
        scratch_shapes=[pltpu.SemaphoreType.DMA((2,))],
        compiler_params=pltpu.CompilerParams(vmem_limit_bytes=1024 * 1024),
        cost_estimate=pl.CostEstimate(
            flops=0, bytes_accessed=8 * width * hidden, transcendentals=0
        ),
        name="stage",
    )(w_in2, w_out2)
    recv = exchange(sent, "expert", experts_order)
    back = pl.pallas_call(
        functools.partial(expert_kernel, step=hidden),
        out_shape=struct(recv.shape, BF16),
        compiler_params=params,
        name="expert",
    )(recv, w_in2, w_out2)
    recv, back = lax.optimization_barrier((recv, back))
    slots_back = exchange(back, "expert", experts_order)
    few = shares * owners * images <= 512
    if few:
        spread = [recv] + [
            lax.ppermute(recv, "dp", [(i, i ^ k) for i in range(shares)])
            for k in range(1, shares)
        ]
    else:
        spread = [lax.all_gather(recv, "dp", axis=0, tiled=False)]

    in_vmem = pl.BlockSpec(memory_space=pltpu.VMEM)
    router_send, logit_grad = pl.pallas_call(
        functools.partial(logits_kernel, images, share_order),
        in_specs=[in_vmem] * 4,
        out_shape=(
            struct((owners * shares, experts, row_count), BF16),
            struct((experts, columns), BF16),
        ),
        compiler_params=params,
        name="logits",
    )(slots_back, tokens2, router_rows, grad2)
    share, router_send = lax.optimization_barrier((lax.axis_index("dp").reshape(1), router_send))
    router_parts = exchange(
        router_send,
        ("expert", "dp"),
        [owner * shares + i for owner in experts_order for i in share_order],
    )
    tokens_grad = pl.pallas_call(
        functools.partial(tokens_kernel, images),
        out_shape=struct((columns, width), BF16),
        compiler_params=params,
        name="tokens",
    )(slots_back, tokens2, router_rows, logit_grad)
    in_smem = pl.BlockSpec(memory_space=pltpu.SMEM)
    out_shape = [struct((row_count, hidden), F32)] * 2
    if few:
        chunks, step = hidden // 512, 512
        w_in_grad, w_out_grad = pl.pallas_call(
            functools.partial(weights_kernel, shares),
            in_specs=[in_smem] + [in_place] * shares + [in_vmem] * 2,
            out_specs=[in_place] * 2,
            out_shape=out_shape,
            scratch_shapes=[
                pltpu.VMEM((shares,) + recv.shape, BF16),
                pltpu.VMEM((chunks, row_count, step), F32),
                pltpu.VMEM((chunks, row_count, step), F32),
                pltpu.SemaphoreType.DMA((shares,)),
                pltpu.SemaphoreType.DMA((2, chunks)),
            ],
            compiler_params=params,
            name="weights",
        )(share, *spread, w_in2, w_out2)
    else:
        w_in_grad, w_out_grad = pl.pallas_call(
            functools.partial(long_weights_kernel, step=512),
            grid=(shares,),
            in_specs=[
                in_smem,
                pl.BlockSpec((1,) + recv.shape, lambda i: (i, 0, 0, 0)),
                pl.BlockSpec((width, hidden), lambda i: (0, 0)),
                pl.BlockSpec((width, hidden), lambda i: (0, 0)),
            ],
            out_specs=[pl.BlockSpec((row_count, hidden), lambda i: (0, 0))] * 2,
            out_shape=out_shape,
            compiler_params=params,
            name="weights",
        )(share, *spread, w_in2, w_out2)
    router_grad = jnp.sum(router_parts.astype(F32), axis=0).T
    return (
        tokens_grad.reshape(tokens.shape),
        w_in_grad.reshape(1, row_count, hidden),
        w_out_grad.reshape(1, row_count, hidden),
        router_grad,
    )


def solution(mesh):
    placed = (
        P(("expert", "dp"), None, None),
        P(),
        P("expert", None, None),
        P("expert", None, None),
        P(("expert", "dp"), None, None),
    )
    return jax.shard_map(
        on_device,
        mesh=mesh,
        in_specs=placed,
        out_specs=(
            P(("expert", "dp"), None, None),
            P("expert", "dp", None),
            P("expert", "dp", None),
            P("dp", None),
        ),
        check_vma=False,
    )
```

```python
import functools
import math

import jax
import jax.numpy as jnp
from jax import lax
from jax.experimental import pallas as pl
from jax.experimental.pallas import tpu as pltpu
from jax.sharding import PartitionSpec as P

F32 = jnp.float32
BF16 = jnp.bfloat16
VMEM_BYTES = 24 * 1024 * 1024
WHOLE_BYTES = 56 * 1024 * 1024


def gelu_pair(value):
    coef = math.sqrt(2.0 / math.pi)
    cubic = 0.044715 * coef
    square = value * value
    half = 0.5 * jnp.tanh(value * (coef + cubic * square)) + 0.5
    steep = value * (2.0 * coef + 6.0 * cubic * square) * (1.0 - half)
    return value * half, half + half * steep


def dot(left, right, left_dim, right_dim):
    return lax.dot_general(
        left, right, (((left_dim,), (right_dim,)), ((), ())), preferred_element_type=F32
    )


def own_image(experts, images, columns):
    shape = (experts, images, columns)
    image = lax.broadcasted_iota(jnp.int32, shape, 1)
    token = lax.broadcasted_iota(jnp.int32, shape, 2)
    low = image * (columns // images)
    inside = (token >= low) & (token < low + columns // images)
    return inside.reshape(experts * images, columns)


def spread_rows(compact, images):
    experts, columns = compact.shape
    wide = jnp.broadcast_to(compact[:, None, :], (experts, images, columns))
    return wide.reshape(experts * images, columns)


def fold_rows(block, images):
    rows, columns = block.shape
    return jnp.sum(block.reshape(rows // images, images, columns), axis=1)


def pair_rows(first, second, groups):
    images = first.shape[0] // groups
    first = first.reshape(groups, images, first.shape[1])
    second = second.reshape(groups, images, second.shape[1])
    return jnp.concatenate((first, second), axis=1).astype(BF16)


def split_rows(pairs):
    groups, both, width = pairs.shape
    wide = pairs.astype(F32)
    first = wide[:, : both // 2].reshape(groups * both // 2, width)
    second = wide[:, both // 2 :].reshape(groups * both // 2, width)
    return first.astype(BF16), second.astype(BF16)


def centre_out(count):
    return sorted(range(count), key=lambda i: (abs(2 * i - count + 1), i))


def in_expert_order(ref):
    order = centre_out(ref.shape[0])
    return jnp.stack([ref[order.index(i)] for i in range(len(order))], axis=0)


def exchange(chunks, axis, order):
    return lax.all_to_all(
        chunks, axis, split_axis=0, concat_axis=0, tiled=True, axis_index_groups=[order]
    )


def softmaxes(router, tokens, images):
    logits = dot(router, tokens, 1, 1)
    experts, columns = logits.shape
    mask = own_image(experts, images, columns)
    combine = jnp.exp(logits - jnp.max(logits, axis=0, keepdims=True))
    combine = combine / jnp.sum(combine, axis=0, keepdims=True)
    block = jnp.where(mask, spread_rows(logits, images), -jnp.inf)
    block = jnp.exp(block - jnp.max(block, axis=1, keepdims=True))
    block = block * (1.0 / jnp.sum(block, axis=1, keepdims=True))
    return block, combine, mask


def slots_kernel(images, tokens_ref, router_ref, grad_ref, sent_ref):
    tokens = tokens_ref[...]
    block, combine, mask = softmaxes(router_ref[...], tokens, images)
    combine_block = jnp.where(mask, spread_rows(combine, images), 0.0)
    slot_in = dot(block.astype(BF16), tokens, 1, 0)
    slot_grad = dot(combine_block.astype(BF16), grad_ref[...], 1, 0)
    pairs = pair_rows(slot_in, slot_grad, combine.shape[0])
    for k, i in enumerate(centre_out(pairs.shape[0])):
        sent_ref[k] = pairs[i]


def stage_kernel(win_hbm, wout_hbm, win_ref, wout_ref, sems):
    loads = (
        pltpu.make_async_copy(win_hbm, win_ref, sems.at[0]),
        pltpu.make_async_copy(wout_hbm, wout_ref, sems.at[1]),
    )
    for load in loads:
        load.start()
    for load in loads:
        load.wait()


def expert_kernel(recv_ref, win_ref, wout_ref, back_ref, *, step):
    slots, cotan = split_rows(recv_ref[...])
    out = jnp.zeros(slots.shape, F32)
    back = jnp.zeros(slots.shape, F32)
    for start in range(0, win_ref.shape[1], step):
        w_in = win_ref[:, start : start + step]
        w_out = wout_ref[:, start : start + step]
        value, slope = gelu_pair(dot(slots, w_in, 1, 0))
        pre_grad = dot(cotan, w_out, 1, 0) * slope
        out = out + dot(value.astype(BF16), w_out, 1, 1)
        back = back + dot(pre_grad.astype(BF16), w_in, 1, 1)
    back_ref[...] = pair_rows(out, back, recv_ref.shape[0])


def logits_kernel(
    images, share_order, back_ref, tokens_ref, router_ref, grad_ref, send_ref, logit_ref
):
    tokens = tokens_ref[...]
    dispatch, combine, mask = softmaxes(router_ref[...], tokens, images)
    slot_out, slot_in_grad = split_rows(in_expert_order(back_ref))
    disp = dot(slot_in_grad, tokens, 1, 1)
    comb = fold_rows(jnp.where(mask, dot(slot_out, grad_ref[...], 1, 1), 0.0), images)
    mean = jnp.sum(dispatch * disp, axis=1, keepdims=True)
    from_dispatch = fold_rows(dispatch * (disp - mean), images)
    from_combine = combine * (comb - jnp.sum(combine * comb, axis=0, keepdims=True))
    logit_grad = (from_combine + from_dispatch).astype(BF16)
    logit_ref[...] = logit_grad
    part = dot(logit_grad, tokens, 1, 0)
    devices, _, width = send_ref.shape
    shares = len(share_order)
    for place, share in enumerate(share_order):
        piece = part[:, share * width : (share + 1) * width].astype(BF16)
        for device in range(place, devices, shares):
            send_ref[device] = piece


def tokens_kernel(images, back_ref, tokens_ref, router_ref, logit_ref, out_ref):
    router = router_ref[...]
    dispatch, _, _ = softmaxes(router, tokens_ref[...], images)
    _, slot_in_grad = split_rows(in_expert_order(back_ref))
    out = dot(dispatch.astype(BF16), slot_in_grad, 0, 0)
    out = out + dot(logit_ref[...], router, 0, 0)
    out_ref[...] = out.astype(BF16)


def own_rows(share, rows, row_count):
    shape = (row_count, rows.shape[1])
    row = lax.broadcasted_iota(jnp.int32, shape, 0) + share * row_count
    pick = jnp.where(lax.broadcasted_iota(jnp.int32, shape, 1) == row, 1.0, 0.0)
    return dot(pick.astype(BF16), rows, 1, 1).astype(BF16)


def weights_kernel(count, share_ref, *refs):
    spread, (win_ref, wout_ref, win_hbm, wout_hbm) = refs[:count], refs[count : count + 4]
    rows_ref, win_out, wout_out, load_sems, store_sems = refs[count + 4 :]
    chunks, row_count, step = win_out.shape
    loads = [
        pltpu.make_async_copy(ref, rows_ref.at[k], load_sems.at[k])
        for k, ref in enumerate(spread)
    ]
    for load in loads:
        load.start()
    for load in loads:
        load.wait()
    slots, cotan = split_rows(rows_ref[...].reshape((-1,) + rows_ref.shape[2:]))
    own_slots = own_rows(share_ref[0], slots, row_count)
    own_cotan = own_rows(share_ref[0], cotan, row_count)
    stores = []
    for chunk in range(chunks):
        part = slice(chunk * step, (chunk + 1) * step)
        value, slope = gelu_pair(dot(slots, win_ref[:, part], 1, 0))
        pre_grad = dot(cotan, wout_ref[:, part], 1, 0) * slope
        win_out[chunk] = dot(own_slots, pre_grad.astype(BF16), 1, 0)
        wout_out[chunk] = dot(own_cotan, value.astype(BF16), 1, 0)
        where = (slice(None), pl.ds(chunk * step, step))
        for which, (source, target) in enumerate(((win_out, win_hbm), (wout_out, wout_hbm))):
            store = pltpu.make_async_copy(
                source.at[chunk], target.at[where], store_sems.at[which, chunk]
            )
            store.start()
            stores.append(store)
    for store in stores:
        store.wait()


def long_weights_kernel(share_ref, spread_ref, win_ref, wout_ref, win_out, wout_out, *, step):
    slots, cotan = split_rows(spread_ref[...].reshape((-1,) + spread_ref.shape[2:]))
    own_slots = own_rows(share_ref[0], slots, win_out.shape[0])
    own_cotan = own_rows(share_ref[0], cotan, win_out.shape[0])

    @pl.when(pl.program_id(0) == 0)
    def _():
        win_out[...] = jnp.zeros_like(win_out)
        wout_out[...] = jnp.zeros_like(wout_out)

    for start in range(0, win_ref.shape[1], step):
        part = slice(start, start + step)
        value, slope = gelu_pair(dot(slots, win_ref[:, part], 1, 0))
        pre_grad = dot(cotan, wout_ref[:, part], 1, 0) * slope
        win_out[:, part] += dot(own_slots, pre_grad.astype(BF16), 1, 0)
        wout_out[:, part] += dot(own_cotan, value.astype(BF16), 1, 0)


def on_device(tokens, router, w_in, w_out, out_grad):
    owners, shares = lax.axis_size("expert"), lax.axis_size("dp")
    experts_order = centre_out(owners)
    share_order = [*range(1, shares, 2), *range(0, shares, 2)]
    images, per_image, width = tokens.shape
    experts = router.shape[1]
    hidden = w_in.shape[2]
    columns = images * per_image
    row_count = width // shares
    tokens2 = tokens.reshape(columns, width)
    grad2 = out_grad.reshape(columns, width)
    router_rows = router.T
    w_in2, w_out2 = w_in.reshape(width, hidden), w_out.reshape(width, hidden)
    params = pltpu.CompilerParams(vmem_limit_bytes=VMEM_BYTES)
    whole = pltpu.CompilerParams(vmem_limit_bytes=WHOLE_BYTES)

    def struct(shape, dtype):
        return jax.ShapeDtypeStruct(shape, dtype)

    in_place = pl.BlockSpec(memory_space=pl.ANY)
    in_vmem = pl.BlockSpec(memory_space=pltpu.VMEM)
    sent = pl.pallas_call(
        functools.partial(slots_kernel, images),
        in_specs=[in_vmem] * 3,
        out_shape=struct((experts, 2 * images, width), BF16),
        compiler_params=whole,
        name="slots",
    )(tokens2, router_rows, grad2)
    w_in2, w_out2 = pl.pallas_call(
        stage_kernel,
        in_specs=[in_place] * 2,
        out_specs=[in_place] * 2,
        out_shape=[struct((width, hidden), BF16)] * 2,
        scratch_shapes=[pltpu.SemaphoreType.DMA((2,))],
        compiler_params=pltpu.CompilerParams(vmem_limit_bytes=1024 * 1024),
        cost_estimate=pl.CostEstimate(
            flops=0, bytes_accessed=8 * width * hidden, transcendentals=0
        ),
        name="stage",
    )(w_in2, w_out2)
    recv = exchange(sent, "expert", experts_order)
    back = pl.pallas_call(
        functools.partial(expert_kernel, step=hidden),
        out_shape=struct(recv.shape, BF16),
        compiler_params=params,
        name="expert",
    )(recv, w_in2, w_out2)
    recv, back = lax.optimization_barrier((recv, back))
    slots_back = exchange(back, "expert", experts_order)
    few = shares * owners * images <= 512
    if few:
        spread = [recv] + [
            lax.ppermute(recv, "dp", [(i, i ^ k) for i in range(shares)])
            for k in range(1, shares)
        ]
    else:
        spread = [lax.all_gather(recv, "dp", axis=0, tiled=False)]

    router_send, logit_grad = pl.pallas_call(
        functools.partial(logits_kernel, images, share_order),
        in_specs=[in_vmem] * 4,
        out_shape=(
            struct((owners * shares, experts, row_count), BF16),
            struct((experts, columns), BF16),
        ),
        compiler_params=params,
        name="logits",
    )(slots_back, tokens2, router_rows, grad2)
    share, router_send = lax.optimization_barrier((lax.axis_index("dp").reshape(1), router_send))
    router_parts = exchange(
        router_send,
        ("expert", "dp"),
        [owner * shares + i for owner in experts_order for i in share_order],
    )
    tokens_grad = pl.pallas_call(
        functools.partial(tokens_kernel, images),
        out_shape=struct((columns, width), BF16),
        compiler_params=params,
        name="tokens",
    )(slots_back, tokens2, router_rows, logit_grad)
    in_smem = pl.BlockSpec(memory_space=pltpu.SMEM)
    out_shape = [struct((row_count, hidden), F32)] * 2
    if few:
        chunks, step = hidden // 512, 512
        w_in_grad, w_out_grad = pl.pallas_call(
            functools.partial(weights_kernel, shares),
            in_specs=[in_smem] + [in_place] * shares + [in_vmem] * 2,
            out_specs=[in_place] * 2,
            out_shape=out_shape,
            scratch_shapes=[
                pltpu.VMEM((shares,) + recv.shape, BF16),
                pltpu.VMEM((chunks, row_count, step), F32),
                pltpu.VMEM((chunks, row_count, step), F32),
                pltpu.SemaphoreType.DMA((shares,)),
                pltpu.SemaphoreType.DMA((2, chunks)),
            ],
            compiler_params=params,
            name="weights",
        )(share, *spread, w_in2, w_out2)
    else:
        w_in_grad, w_out_grad = pl.pallas_call(
            functools.partial(long_weights_kernel, step=512),
            grid=(shares,),
            in_specs=[
                in_smem,
                pl.BlockSpec((1,) + recv.shape, lambda i: (i, 0, 0, 0)),
                pl.BlockSpec((width, hidden), lambda i: (0, 0)),
                pl.BlockSpec((width, hidden), lambda i: (0, 0)),
            ],
            out_specs=[pl.BlockSpec((row_count, hidden), lambda i: (0, 0))] * 2,
            out_shape=out_shape,
            compiler_params=params,
            name="weights",
        )(share, *spread, w_in2, w_out2)
    router_grad = jnp.sum(router_parts.astype(F32), axis=0).T
    return (
        tokens_grad.reshape(tokens.shape),
        w_in_grad.reshape(1, row_count, hidden),
        w_out_grad.reshape(1, row_count, hidden),
        router_grad,
    )


def solution(mesh):
    placed = (
        P(("expert", "dp"), None, None),
        P(),
        P("expert", None, None),
        P("expert", None, None),
        P(("expert", "dp"), None, None),
    )
    return jax.shard_map(
        on_device,
        mesh=mesh,
        in_specs=placed,
        out_specs=(
            P(("expert", "dp"), None, None),
            P("expert", "dp", None),
            P("expert", "dp", None),
            P("dp", None),
        ),
        check_vma=False,
    )
```

```python
import functools
import math

import jax
import jax.numpy as jnp
from jax import lax
from jax.experimental import pallas as pl
from jax.experimental.pallas import tpu as pltpu
from jax.sharding import PartitionSpec as P

F32 = jnp.float32
BF16 = jnp.bfloat16
VMEM_BYTES = 24 * 1024 * 1024
WHOLE_BYTES = 56 * 1024 * 1024


def gelu_pair(value):
    coef = math.sqrt(2.0 / math.pi)
    cubic = 0.044715 * coef
    square = value * value
    half = 0.5 * jnp.tanh(value * (coef + cubic * square)) + 0.5
    steep = value * (2.0 * coef + 6.0 * cubic * square) * (1.0 - half)
    return value * half, half + half * steep


def dot(left, right, left_dim, right_dim):
    return lax.dot_general(
        left, right, (((left_dim,), (right_dim,)), ((), ())), preferred_element_type=F32
    )


def own_image(experts, images, columns):
    shape = (experts, images, columns)
    image = lax.broadcasted_iota(jnp.int32, shape, 1)
    token = lax.broadcasted_iota(jnp.int32, shape, 2)
    low = image * (columns // images)
    inside = (token >= low) & (token < low + columns // images)
    return inside.reshape(experts * images, columns)


def spread_rows(compact, images):
    experts, columns = compact.shape
    wide = jnp.broadcast_to(compact[:, None, :], (experts, images, columns))
    return wide.reshape(experts * images, columns)


def fold_rows(block, images):
    rows, columns = block.shape
    return jnp.sum(block.reshape(rows // images, images, columns), axis=1)


def pair_rows(first, second, groups):
    images = first.shape[0] // groups
    first = first.reshape(groups, images, first.shape[1])
    second = second.reshape(groups, images, second.shape[1])
    return jnp.concatenate((first, second), axis=1).astype(BF16)


def split_rows(pairs):
    groups, both, width = pairs.shape
    wide = pairs.astype(F32)
    first = wide[:, : both // 2].reshape(groups * both // 2, width)
    second = wide[:, both // 2 :].reshape(groups * both // 2, width)
    return first.astype(BF16), second.astype(BF16)


def centre_out(count):
    return sorted(range(count), key=lambda i: (abs(2 * i - count + 1), -i))


def in_expert_order(ref):
    order = centre_out(ref.shape[0])
    return jnp.stack([ref[order.index(i)] for i in range(len(order))], axis=0)


def exchange(chunks, axis, order):
    return lax.all_to_all(
        chunks, axis, split_axis=0, concat_axis=0, tiled=True, axis_index_groups=[order]
    )


def softmaxes(router, tokens, images):
    logits = dot(router, tokens, 1, 1)
    experts, columns = logits.shape
    mask = own_image(experts, images, columns)
    combine = jnp.exp(logits - jnp.max(logits, axis=0, keepdims=True))
    combine = combine / jnp.sum(combine, axis=0, keepdims=True)
    block = jnp.where(mask, spread_rows(logits, images), -jnp.inf)
    block = jnp.exp(block - jnp.max(block, axis=1, keepdims=True))
    block = block * (1.0 / jnp.sum(block, axis=1, keepdims=True))
    return block, combine, mask


def slots_kernel(images, tokens_ref, router_ref, grad_ref, sent_ref):
    tokens = tokens_ref[...]
    block, combine, mask = softmaxes(router_ref[...], tokens, images)
    combine_block = jnp.where(mask, spread_rows(combine, images), 0.0)
    slot_in = dot(block.astype(BF16), tokens, 1, 0)
    slot_grad = dot(combine_block.astype(BF16), grad_ref[...], 1, 0)
    pairs = pair_rows(slot_in, slot_grad, combine.shape[0])
    for k, i in enumerate(centre_out(pairs.shape[0])):
        sent_ref[k] = pairs[i]


def stage_kernel(win_hbm, wout_hbm, win_ref, wout_ref, sems):
    loads = (
        pltpu.make_async_copy(win_hbm, win_ref, sems.at[0]),
        pltpu.make_async_copy(wout_hbm, wout_ref, sems.at[1]),
    )
    for load in loads:
        load.start()
    for load in loads:
        load.wait()


def expert_kernel(recv_ref, win_ref, wout_ref, back_ref, *, step):
    slots, cotan = split_rows(recv_ref[...])
    out = jnp.zeros(slots.shape, F32)
    back = jnp.zeros(slots.shape, F32)
    for start in range(0, win_ref.shape[1], step):
        w_in = win_ref[:, start : start + step]
        w_out = wout_ref[:, start : start + step]
        value, slope = gelu_pair(dot(slots, w_in, 1, 0))
        pre_grad = dot(cotan, w_out, 1, 0) * slope
        out = out + dot(value.astype(BF16), w_out, 1, 1)
        back = back + dot(pre_grad.astype(BF16), w_in, 1, 1)
    back_ref[...] = pair_rows(out, back, recv_ref.shape[0])


def logits_kernel(
    images, share_order, back_ref, tokens_ref, router_ref, grad_ref, send_ref, logit_ref
):
    tokens = tokens_ref[...]
    dispatch, combine, mask = softmaxes(router_ref[...], tokens, images)
    slot_out, slot_in_grad = split_rows(in_expert_order(back_ref))
    disp = dot(slot_in_grad, tokens, 1, 1)
    comb = fold_rows(jnp.where(mask, dot(slot_out, grad_ref[...], 1, 1), 0.0), images)
    mean = jnp.sum(dispatch * disp, axis=1, keepdims=True)
    from_dispatch = fold_rows(dispatch * (disp - mean), images)
    from_combine = combine * (comb - jnp.sum(combine * comb, axis=0, keepdims=True))
    logit_grad = (from_combine + from_dispatch).astype(BF16)
    logit_ref[...] = logit_grad
    part = dot(logit_grad, tokens, 1, 0)
    devices, _, width = send_ref.shape
    shares = len(share_order)
    for place, share in enumerate(share_order):
        piece = part[:, share * width : (share + 1) * width].astype(BF16)
        for device in range(place, devices, shares):
            send_ref[device] = piece


def tokens_kernel(images, back_ref, tokens_ref, router_ref, logit_ref, out_ref):
    router = router_ref[...]
    dispatch, _, _ = softmaxes(router, tokens_ref[...], images)
    _, slot_in_grad = split_rows(in_expert_order(back_ref))
    out = dot(dispatch.astype(BF16), slot_in_grad, 0, 0)
    out = out + dot(logit_ref[...], router, 0, 0)
    out_ref[...] = out.astype(BF16)


def own_rows(share, rows, row_count):
    shape = (row_count, rows.shape[1])
    row = lax.broadcasted_iota(jnp.int32, shape, 0) + share * row_count
    pick = jnp.where(lax.broadcasted_iota(jnp.int32, shape, 1) == row, 1.0, 0.0)
    return dot(pick.astype(BF16), rows, 1, 1).astype(BF16)


def weights_kernel(count, share_ref, *refs):
    spread, (win_ref, wout_ref, win_hbm, wout_hbm) = refs[:count], refs[count : count + 4]
    rows_ref, win_out, wout_out, load_sems, store_sems = refs[count + 4 :]
    chunks, row_count, step = win_out.shape
    loads = [
        pltpu.make_async_copy(ref, rows_ref.at[k], load_sems.at[k])
        for k, ref in enumerate(spread)
    ]
    for load in loads:
        load.start()
    for load in loads:
        load.wait()
    slots, cotan = split_rows(rows_ref[...].reshape((-1,) + rows_ref.shape[2:]))
    own_slots = own_rows(share_ref[0], slots, row_count)
    own_cotan = own_rows(share_ref[0], cotan, row_count)
    stores = []
    for chunk in range(chunks):
        part = slice(chunk * step, (chunk + 1) * step)
        value, slope = gelu_pair(dot(slots, win_ref[:, part], 1, 0))
        pre_grad = dot(cotan, wout_ref[:, part], 1, 0) * slope
        win_out[chunk] = dot(own_slots, pre_grad.astype(BF16), 1, 0)
        wout_out[chunk] = dot(own_cotan, value.astype(BF16), 1, 0)
        where = (slice(None), pl.ds(chunk * step, step))
        for which, (source, target) in enumerate(((win_out, win_hbm), (wout_out, wout_hbm))):
            store = pltpu.make_async_copy(
                source.at[chunk], target.at[where], store_sems.at[which, chunk]
            )
            store.start()
            stores.append(store)
    for store in stores:
        store.wait()


def long_weights_kernel(share_ref, spread_ref, win_ref, wout_ref, win_out, wout_out, *, step):
    slots, cotan = split_rows(spread_ref[...].reshape((-1,) + spread_ref.shape[2:]))
    own_slots = own_rows(share_ref[0], slots, win_out.shape[0])
    own_cotan = own_rows(share_ref[0], cotan, win_out.shape[0])

    @pl.when(pl.program_id(0) == 0)
    def _():
        win_out[...] = jnp.zeros_like(win_out)
        wout_out[...] = jnp.zeros_like(wout_out)

    for start in range(0, win_ref.shape[1], step):
        part = slice(start, start + step)
        value, slope = gelu_pair(dot(slots, win_ref[:, part], 1, 0))
        pre_grad = dot(cotan, wout_ref[:, part], 1, 0) * slope
        win_out[:, part] += dot(own_slots, pre_grad.astype(BF16), 1, 0)
        wout_out[:, part] += dot(own_cotan, value.astype(BF16), 1, 0)


def on_device(tokens, router, w_in, w_out, out_grad):
    owners, shares = lax.axis_size("expert"), lax.axis_size("dp")
    experts_order = centre_out(owners)
    share_order = [*range(1, shares, 2), *range(0, shares, 2)]
    images, per_image, width = tokens.shape
    experts = router.shape[1]
    hidden = w_in.shape[2]
    columns = images * per_image
    row_count = width // shares
    tokens2 = tokens.reshape(columns, width)
    grad2 = out_grad.reshape(columns, width)
    router_rows = router.T
    w_in2, w_out2 = w_in.reshape(width, hidden), w_out.reshape(width, hidden)
    params = pltpu.CompilerParams(vmem_limit_bytes=VMEM_BYTES)
    whole = pltpu.CompilerParams(vmem_limit_bytes=WHOLE_BYTES)

    def struct(shape, dtype):
        return jax.ShapeDtypeStruct(shape, dtype)

    in_place = pl.BlockSpec(memory_space=pl.ANY)
    in_vmem = pl.BlockSpec(memory_space=pltpu.VMEM)
    sent = pl.pallas_call(
        functools.partial(slots_kernel, images),
        in_specs=[in_vmem] * 3,
        out_shape=struct((experts, 2 * images, width), BF16),
        compiler_params=whole,
        name="slots",
    )(tokens2, router_rows, grad2)
    w_in2, w_out2 = pl.pallas_call(
        stage_kernel,
        in_specs=[in_place] * 2,
        out_specs=[in_place] * 2,
        out_shape=[struct((width, hidden), BF16)] * 2,
        scratch_shapes=[pltpu.SemaphoreType.DMA((2,))],
        compiler_params=pltpu.CompilerParams(vmem_limit_bytes=1024 * 1024),
        cost_estimate=pl.CostEstimate(
            flops=0, bytes_accessed=8 * width * hidden, transcendentals=0
        ),
        name="stage",
    )(w_in2, w_out2)
    recv = exchange(sent, "expert", experts_order)
    back = pl.pallas_call(
        functools.partial(expert_kernel, step=hidden),
        out_shape=struct(recv.shape, BF16),
        compiler_params=params,
        name="expert",
    )(recv, w_in2, w_out2)
    recv, back = lax.optimization_barrier((recv, back))
    slots_back = exchange(back, "expert", experts_order)
    few = shares * owners * images <= 512
    if few:
        spread = [recv] + [
            lax.ppermute(recv, "dp", [(i, i ^ k) for i in range(shares)])
            for k in range(1, shares)
        ]
    else:
        spread = [lax.all_gather(recv, "dp", axis=0, tiled=False)]

    router_send, logit_grad = pl.pallas_call(
        functools.partial(logits_kernel, images, share_order),
        in_specs=[in_vmem] * 4,
        out_shape=(
            struct((owners * shares, experts, row_count), BF16),
            struct((experts, columns), BF16),
        ),
        compiler_params=params,
        name="logits",
    )(slots_back, tokens2, router_rows, grad2)
    share, router_send = lax.optimization_barrier((lax.axis_index("dp").reshape(1), router_send))
    router_parts = exchange(
        router_send,
        ("expert", "dp"),
        [owner * shares + i for owner in experts_order for i in share_order],
    )
    tokens_grad = pl.pallas_call(
        functools.partial(tokens_kernel, images),
        out_shape=struct((columns, width), BF16),
        compiler_params=params,
        name="tokens",
    )(slots_back, tokens2, router_rows, logit_grad)
    in_smem = pl.BlockSpec(memory_space=pltpu.SMEM)
    out_shape = [struct((row_count, hidden), F32)] * 2
    if few:
        chunks, step = hidden // 512, 512
        w_in_grad, w_out_grad = pl.pallas_call(
            functools.partial(weights_kernel, shares),
            in_specs=[in_smem] + [in_place] * shares + [in_vmem] * 2,
            out_specs=[in_place] * 2,
            out_shape=out_shape,
            scratch_shapes=[
                pltpu.VMEM((shares,) + recv.shape, BF16),
                pltpu.VMEM((chunks, row_count, step), F32),
                pltpu.VMEM((chunks, row_count, step), F32),
                pltpu.SemaphoreType.DMA((shares,)),
                pltpu.SemaphoreType.DMA((2, chunks)),
            ],
            compiler_params=params,
            name="weights",
        )(share, *spread, w_in2, w_out2)
    else:
        w_in_grad, w_out_grad = pl.pallas_call(
            functools.partial(long_weights_kernel, step=512),
            grid=(shares,),
            in_specs=[
                in_smem,
                pl.BlockSpec((1,) + recv.shape, lambda i: (i, 0, 0, 0)),
                pl.BlockSpec((width, hidden), lambda i: (0, 0)),
                pl.BlockSpec((width, hidden), lambda i: (0, 0)),
            ],
            out_specs=[pl.BlockSpec((row_count, hidden), lambda i: (0, 0))] * 2,
            out_shape=out_shape,
            compiler_params=params,
            name="weights",
        )(share, *spread, w_in2, w_out2)
    router_grad = jnp.sum(router_parts.astype(F32), axis=0).T
    return (
        tokens_grad.reshape(tokens.shape),
        w_in_grad.reshape(1, row_count, hidden),
        w_out_grad.reshape(1, row_count, hidden),
        router_grad,
    )


def solution(mesh):
    placed = (
        P(("expert", "dp"), None, None),
        P(),
        P("expert", None, None),
        P("expert", None, None),
        P(("expert", "dp"), None, None),
    )
    return jax.shard_map(
        on_device,
        mesh=mesh,
        in_specs=placed,
        out_specs=(
            P(("expert", "dp"), None, None),
            P("expert", "dp", None),
            P("expert", "dp", None),
            P("dp", None),
        ),
        check_vma=False,
    )
```

```python
import functools
import math

import jax
import jax.numpy as jnp
from jax import lax
from jax.experimental import pallas as pl
from jax.experimental.pallas import tpu as pltpu
from jax.sharding import PartitionSpec as P

F32 = jnp.float32
BF16 = jnp.bfloat16
VMEM_BYTES = 24 * 1024 * 1024
WHOLE_BYTES = 56 * 1024 * 1024


def gelu_pair(value):
    coef = math.sqrt(2.0 / math.pi)
    cubic = 0.044715 * coef
    square = value * value
    half = 0.5 * jnp.tanh(value * (coef + cubic * square)) + 0.5
    steep = value * (2.0 * coef + 6.0 * cubic * square) * (1.0 - half)
    return value * half, half + half * steep


def dot(left, right, left_dim, right_dim):
    return lax.dot_general(
        left, right, (((left_dim,), (right_dim,)), ((), ())), preferred_element_type=F32
    )


def own_image(experts, images, columns):
    shape = (experts, images, columns)
    image = lax.broadcasted_iota(jnp.int32, shape, 1)
    token = lax.broadcasted_iota(jnp.int32, shape, 2)
    low = image * (columns // images)
    inside = (token >= low) & (token < low + columns // images)
    return inside.reshape(experts * images, columns)


def spread_rows(compact, images):
    experts, columns = compact.shape
    wide = jnp.broadcast_to(compact[:, None, :], (experts, images, columns))
    return wide.reshape(experts * images, columns)


def fold_rows(block, images):
    rows, columns = block.shape
    return jnp.sum(block.reshape(rows // images, images, columns), axis=1)


def pair_rows(first, second, groups):
    images = first.shape[0] // groups
    first = first.reshape(groups, images, first.shape[1])
    second = second.reshape(groups, images, second.shape[1])
    return jnp.concatenate((first, second), axis=1).astype(BF16)


def split_rows(pairs):
    groups, both, width = pairs.shape
    wide = pairs.astype(F32)
    first = wide[:, : both // 2].reshape(groups * both // 2, width)
    second = wide[:, both // 2 :].reshape(groups * both // 2, width)
    return first.astype(BF16), second.astype(BF16)


def centre_out(count):
    return sorted(range(count), key=lambda i: (abs(2 * i - count + 1), i))


def in_expert_order(ref):
    order = centre_out(ref.shape[0])
    return jnp.stack([ref[order.index(i)] for i in range(len(order))], axis=0)


def exchange(chunks, axis, order):
    return lax.all_to_all(
        chunks, axis, split_axis=0, concat_axis=0, tiled=True, axis_index_groups=[order]
    )


def softmaxes(router, tokens, images):
    logits = dot(router, tokens, 1, 1)
    experts, columns = logits.shape
    mask = own_image(experts, images, columns)
    combine = jnp.exp(logits - jnp.max(logits, axis=0, keepdims=True))
    combine = combine / jnp.sum(combine, axis=0, keepdims=True)
    block = jnp.where(mask, spread_rows(logits, images), -jnp.inf)
    block = jnp.exp(block - jnp.max(block, axis=1, keepdims=True))
    block = block * (1.0 / jnp.sum(block, axis=1, keepdims=True))
    return block, combine, mask


def slots_kernel(images, tokens_ref, router_ref, grad_ref, sent_ref):
    tokens = tokens_ref[...]
    block, combine, mask = softmaxes(router_ref[...], tokens, images)
    combine_block = jnp.where(mask, spread_rows(combine, images), 0.0)
    slot_in = dot(block.astype(BF16), tokens, 1, 0)
    slot_grad = dot(combine_block.astype(BF16), grad_ref[...], 1, 0)
    pairs = pair_rows(slot_in, slot_grad, combine.shape[0])
    for k, i in enumerate(centre_out(pairs.shape[0])):
        sent_ref[k] = pairs[i]


def stage_kernel(win_hbm, wout_hbm, win_ref, wout_ref, sems):
    loads = (
        pltpu.make_async_copy(win_hbm, win_ref, sems.at[0]),
        pltpu.make_async_copy(wout_hbm, wout_ref, sems.at[1]),
    )
    for load in loads:
        load.start()
    for load in loads:
        load.wait()


def expert_kernel(recv_ref, win_ref, wout_ref, back_ref, *, step):
    slots, cotan = split_rows(recv_ref[...])
    out = jnp.zeros(slots.shape, F32)
    back = jnp.zeros(slots.shape, F32)
    for start in range(0, win_ref.shape[1], step):
        w_in = win_ref[:, start : start + step]
        w_out = wout_ref[:, start : start + step]
        value, slope = gelu_pair(dot(slots, w_in, 1, 0))
        pre_grad = dot(cotan, w_out, 1, 0) * slope
        out = out + dot(value.astype(BF16), w_out, 1, 1)
        back = back + dot(pre_grad.astype(BF16), w_in, 1, 1)
    back_ref[...] = pair_rows(out, back, recv_ref.shape[0])


def soft_kernel(images, tokens_ref, router_ref, block_ref, combine_ref):
    block_ref[...], combine_ref[...], _ = softmaxes(router_ref[...], tokens_ref[...], images)


def logits_kernel(
    images, share_order, back_ref, tokens_ref, block_ref, combine_ref, grad_ref, send_ref, logit_ref
):
    tokens = tokens_ref[...]
    dispatch, combine = block_ref[...], combine_ref[...]
    mask = own_image(combine.shape[0], images, tokens.shape[0])
    slot_out, slot_in_grad = split_rows(in_expert_order(back_ref))
    disp = dot(slot_in_grad, tokens, 1, 1)
    comb = fold_rows(jnp.where(mask, dot(slot_out, grad_ref[...], 1, 1), 0.0), images)
    mean = jnp.sum(dispatch * disp, axis=1, keepdims=True)
    from_dispatch = fold_rows(dispatch * (disp - mean), images)
    from_combine = combine * (comb - jnp.sum(combine * comb, axis=0, keepdims=True))
    logit_grad = (from_combine + from_dispatch).astype(BF16)
    logit_ref[...] = logit_grad
    part = dot(logit_grad, tokens, 1, 0)
    devices, _, width = send_ref.shape
    shares = len(share_order)
    for place, share in enumerate(share_order):
        piece = part[:, share * width : (share + 1) * width].astype(BF16)
        for device in range(place, devices, shares):
            send_ref[device] = piece


def tokens_kernel(back_ref, block_ref, router_ref, logit_ref, out_ref):
    router = router_ref[...]
    dispatch = block_ref[...]
    _, slot_in_grad = split_rows(in_expert_order(back_ref))
    out = dot(dispatch.astype(BF16), slot_in_grad, 0, 0)
    out = out + dot(logit_ref[...], router, 0, 0)
    out_ref[...] = out.astype(BF16)


def own_rows(share, rows, row_count):
    shape = (row_count, rows.shape[1])
    row = lax.broadcasted_iota(jnp.int32, shape, 0) + share * row_count
    pick = jnp.where(lax.broadcasted_iota(jnp.int32, shape, 1) == row, 1.0, 0.0)
    return dot(pick.astype(BF16), rows, 1, 1).astype(BF16)


def weights_kernel(count, share_ref, *refs):
    spread, (win_ref, wout_ref, win_hbm, wout_hbm) = refs[:count], refs[count : count + 4]
    rows_ref, win_out, wout_out, load_sems, store_sems = refs[count + 4 :]
    chunks, row_count, step = win_out.shape
    loads = [
        pltpu.make_async_copy(ref, rows_ref.at[k], load_sems.at[k])
        for k, ref in enumerate(spread)
    ]
    for load in loads:
        load.start()
    for load in loads:
        load.wait()
    slots, cotan = split_rows(rows_ref[...].reshape((-1,) + rows_ref.shape[2:]))
    own_slots = own_rows(share_ref[0], slots, row_count)
    own_cotan = own_rows(share_ref[0], cotan, row_count)
    stores = []
    for chunk in range(chunks):
        part = slice(chunk * step, (chunk + 1) * step)
        value, slope = gelu_pair(dot(slots, win_ref[:, part], 1, 0))
        pre_grad = dot(cotan, wout_ref[:, part], 1, 0) * slope
        win_out[chunk] = dot(own_slots, pre_grad.astype(BF16), 1, 0)
        wout_out[chunk] = dot(own_cotan, value.astype(BF16), 1, 0)
        where = (slice(None), pl.ds(chunk * step, step))
        for which, (source, target) in enumerate(((win_out, win_hbm), (wout_out, wout_hbm))):
            store = pltpu.make_async_copy(
                source.at[chunk], target.at[where], store_sems.at[which, chunk]
            )
            store.start()
            stores.append(store)
    for store in stores:
        store.wait()


def long_weights_kernel(share_ref, spread_ref, win_ref, wout_ref, win_out, wout_out, *, step):
    slots, cotan = split_rows(spread_ref[...].reshape((-1,) + spread_ref.shape[2:]))
    own_slots = own_rows(share_ref[0], slots, win_out.shape[0])
    own_cotan = own_rows(share_ref[0], cotan, win_out.shape[0])

    @pl.when(pl.program_id(0) == 0)
    def _():
        win_out[...] = jnp.zeros_like(win_out)
        wout_out[...] = jnp.zeros_like(wout_out)

    for start in range(0, win_ref.shape[1], step):
        part = slice(start, start + step)
        value, slope = gelu_pair(dot(slots, win_ref[:, part], 1, 0))
        pre_grad = dot(cotan, wout_ref[:, part], 1, 0) * slope
        win_out[:, part] += dot(own_slots, pre_grad.astype(BF16), 1, 0)
        wout_out[:, part] += dot(own_cotan, value.astype(BF16), 1, 0)


def on_device(tokens, router, w_in, w_out, out_grad):
    owners, shares = lax.axis_size("expert"), lax.axis_size("dp")
    experts_order = centre_out(owners)
    share_order = [*range(1, shares, 2), *range(0, shares, 2)]
    images, per_image, width = tokens.shape
    experts = router.shape[1]
    hidden = w_in.shape[2]
    columns = images * per_image
    row_count = width // shares
    tokens2 = tokens.reshape(columns, width)
    grad2 = out_grad.reshape(columns, width)
    router_rows = router.T
    w_in2, w_out2 = w_in.reshape(width, hidden), w_out.reshape(width, hidden)
    params = pltpu.CompilerParams(vmem_limit_bytes=VMEM_BYTES)
    whole = pltpu.CompilerParams(vmem_limit_bytes=WHOLE_BYTES)

    def struct(shape, dtype):
        return jax.ShapeDtypeStruct(shape, dtype)

    in_place = pl.BlockSpec(memory_space=pl.ANY)
    in_vmem = pl.BlockSpec(memory_space=pltpu.VMEM)
    sent = pl.pallas_call(
        functools.partial(slots_kernel, images),
        in_specs=[in_vmem] * 3,
        out_shape=struct((experts, 2 * images, width), BF16),
        compiler_params=whole,
        name="slots",
    )(tokens2, router_rows, grad2)
    w_in2, w_out2 = pl.pallas_call(
        stage_kernel,
        in_specs=[in_place] * 2,
        out_specs=[in_place] * 2,
        out_shape=[struct((width, hidden), BF16)] * 2,
        scratch_shapes=[pltpu.SemaphoreType.DMA((2,))],
        compiler_params=pltpu.CompilerParams(vmem_limit_bytes=1024 * 1024),
        cost_estimate=pl.CostEstimate(
            flops=0, bytes_accessed=8 * width * hidden, transcendentals=0
        ),
        name="stage",
    )(w_in2, w_out2)
    recv = exchange(sent, "expert", experts_order)
    back = pl.pallas_call(
        functools.partial(expert_kernel, step=hidden),
        out_shape=struct(recv.shape, BF16),
        compiler_params=params,
        name="expert",
    )(recv, w_in2, w_out2)
    recv, back = lax.optimization_barrier((recv, back))
    slots_back = exchange(back, "expert", experts_order)
    soft_rows, _ = lax.optimization_barrier((router_rows, back))
    block, combine = pl.pallas_call(
        functools.partial(soft_kernel, images),
        in_specs=[in_vmem] * 2,
        out_shape=(struct((experts * images, columns), F32), struct((experts, columns), F32)),
        compiler_params=params,
        name="soft",
    )(tokens2, soft_rows)
    few = shares * owners * images <= 512
    if few:
        spread = [recv] + [
            lax.ppermute(recv, "dp", [(i, i ^ k) for i in range(shares)])
            for k in range(1, shares)
        ]
    else:
        spread = [lax.all_gather(recv, "dp", axis=0, tiled=False)]

    router_send, logit_grad = pl.pallas_call(
        functools.partial(logits_kernel, images, share_order),
        in_specs=[in_vmem] * 5,
        out_shape=(
            struct((owners * shares, experts, row_count), BF16),
            struct((experts, columns), BF16),
        ),
        compiler_params=params,
        name="logits",
    )(slots_back, tokens2, block, combine, grad2)
    share, router_send = lax.optimization_barrier((lax.axis_index("dp").reshape(1), router_send))
    router_parts = exchange(
        router_send,
        ("expert", "dp"),
        [owner * shares + i for owner in experts_order for i in share_order],
    )
    tokens_grad = pl.pallas_call(
        tokens_kernel,
        out_shape=struct((columns, width), BF16),
        compiler_params=params,
        name="tokens",
    )(slots_back, block, router_rows, logit_grad)
    in_smem = pl.BlockSpec(memory_space=pltpu.SMEM)
    out_shape = [struct((row_count, hidden), F32)] * 2
    if few:
        chunks, step = hidden // 512, 512
        w_in_grad, w_out_grad = pl.pallas_call(
            functools.partial(weights_kernel, shares),
            in_specs=[in_smem] + [in_place] * shares + [in_vmem] * 2,
            out_specs=[in_place] * 2,
            out_shape=out_shape,
            scratch_shapes=[
                pltpu.VMEM((shares,) + recv.shape, BF16),
                pltpu.VMEM((chunks, row_count, step), F32),
                pltpu.VMEM((chunks, row_count, step), F32),
                pltpu.SemaphoreType.DMA((shares,)),
                pltpu.SemaphoreType.DMA((2, chunks)),
            ],
            compiler_params=params,
            name="weights",
        )(share, *spread, w_in2, w_out2)
    else:
        w_in_grad, w_out_grad = pl.pallas_call(
            functools.partial(long_weights_kernel, step=512),
            grid=(shares,),
            in_specs=[
                in_smem,
                pl.BlockSpec((1,) + recv.shape, lambda i: (i, 0, 0, 0)),
                pl.BlockSpec((width, hidden), lambda i: (0, 0)),
                pl.BlockSpec((width, hidden), lambda i: (0, 0)),
            ],
            out_specs=[pl.BlockSpec((row_count, hidden), lambda i: (0, 0))] * 2,
            out_shape=out_shape,
            compiler_params=params,
            name="weights",
        )(share, *spread, w_in2, w_out2)
    router_grad = jnp.sum(router_parts.astype(F32), axis=0).T
    return (
        tokens_grad.reshape(tokens.shape),
        w_in_grad.reshape(1, row_count, hidden),
        w_out_grad.reshape(1, row_count, hidden),
        router_grad,
    )


def solution(mesh):
    placed = (
        P(("expert", "dp"), None, None),
        P(),
        P("expert", None, None),
        P("expert", None, None),
        P(("expert", "dp"), None, None),
    )
    return jax.shard_map(
        on_device,
        mesh=mesh,
        in_specs=placed,
        out_specs=(
            P(("expert", "dp"), None, None),
            P("expert", "dp", None),
            P("expert", "dp", None),
            P("dp", None),
        ),
        check_vma=False,
    )
```
